128 devices in a mesh: tp: 4 (over z_lo, core), seq: 32 (over x, z_hi, y).
Axes of the slice: x: 4, y: 4, z: 4 (z_hi: 2, z_lo: 2; z = z_hi * 2 + z_lo), core: 2. Of those that a mesh axis runs over, the one named last changes fastest.
Arguments:
- tokens: bfloat16 [8192, 2048], P('seq'), may hold values from -6 to 6
- norm1_gain: bfloat16 [2048], P('seq'), may hold values from 0.25 to 1.75
- norm1_bias: bfloat16 [2048], P('seq'), may hold values from -3 to 3
- w_query: bfloat16 [2048, 2048], P('seq', 'tp'), may hold values from -0.125 to 0.125
- w_key: bfloat16 [2048, 2048], P('seq', 'tp'), may hold values from -0.125 to 0.125
- w_value: bfloat16 [2048, 4096], P('seq', 'tp'), may hold values from -0.125 to 0.125
- w_gate: bfloat16 [2048, 4096], P('seq', 'tp'), may hold values from -0.125 to 0.125
- w_out: bfloat16 [4096, 2048], P('tp', 'seq'), may hold values from -0.1875 to 0.1875
- norm2_gain: bfloat16 [2048], P('seq'), may hold values from 0.25 to 1.75
- norm2_bias: bfloat16 [2048], P('seq'), may hold values from -3 to 3
- w_up: bfloat16 [2048, 4096], P('seq', 'tp'), may hold values from -0.125 to 0.125
- w_down: bfloat16 [4096, 2048], P('tp', 'seq'), may hold values from -0.09375 to 0.09375
- decay_rate: float32 [8], P('tp'), may hold values from 1.2207031e-05 to 0.03
- out_grad: bfloat16 [8192, 2048], P('seq'), may hold values from -6 to 6
Outputs:
- block_out: bfloat16 [8192, 2048], P('seq')
- tokens_grad: float32 [8192, 2048], P('seq')
- norm1_gain_grad: float32 [2048], P('seq')
- norm1_bias_grad: float32 [2048], P('seq')
- w_query_grad: float32 [2048, 2048], P('seq', 'tp')
- w_key_grad: float32 [2048, 2048], P('seq', 'tp')
- w_value_grad: float32 [2048, 4096], P('seq', 'tp')
- w_gate_grad: float32 [2048, 4096], P('seq', 'tp')
- w_out_grad: float32 [4096, 2048], P('tp', 'seq')
- norm2_gain_grad: float32 [2048], P('seq')
- norm2_bias_grad: float32 [2048], P('seq')
- w_up_grad: float32 [2048, 4096], P('seq', 'tp')
- w_down_grad: float32 [4096, 2048], P('tp', 'seq')
The draws below stay inside these ranges and needn't reach their ends.
All inputs are finite; a program needn't handle non-finite values.
Results may differ from the reference program's by a relative error of at most 0.025.
Values may be sent and summed in bfloat16 or wider, within the bound.
No kernel may reach another device: no remote copies, remote signals or barrier semaphores. Data moves between devices by JAX's collectives and lax.ppermute only.
A program may use at most 192 MiB of HBM per device.

```python
import math
import jax
import jax.numpy as jnp
from jax import lax

D = 2048
HEADS = 8
DK = 256
DV = 512
FF = 4096
TOK_DEV = 256
TOKENS = 8192
QK = 2048
VD = 4096


def level_of(stream_key, dims, cuts, least, top_value):
    def one(axis_at, shards_of):
        steps = jax.random.uniform(jax.random.fold_in(jax.random.fold_in(stream_key, 6), axis_at), (shards_of,), jnp.float32, least / len(cuts), top_value / len(cuts))
        return jnp.repeat(jnp.exp(steps), dims[axis_at] // shards_of).reshape((-1,) + (1,) * (len(dims) - axis_at - 1))

    level = one(*cuts[0])
    for cut in cuts[1:]:
        level = level * one(*cut)
    return level


def gaussian(key, dims, width, most, cuts=(), held_as=jnp.bfloat16):
    level = level_of(key, dims, cuts, -0.22, 0.18) if cuts else 1.0
    values = jax.random.normal(key, dims, jnp.float32) * width * level
    return jnp.minimum(jnp.maximum(values, -most), most).astype(held_as)


def setup_inputs(seed: int = 0) -> dict:
    streams_of = jax.random.split(jax.random.key(seed), 15)
    return {
        "tokens": gaussian(streams_of[0], (TOKENS, D), 1.0, 6.0, ((0, 32),)),
        "norm1_gain": jnp.clip(1.0 + 0.15 * jax.random.normal(streams_of[1], (D,), jnp.float32), 0.25, 1.75).astype(jnp.bfloat16),
        "norm1_bias": gaussian(streams_of[2], (D,), 0.5, 3.0, ((0, 32),)),
        "w_query": gaussian(streams_of[3], (D, QK), D ** -0.5, 0.125, ((0, 32), (1, 4))),
        "w_key": gaussian(streams_of[4], (D, QK), D ** -0.5, 0.125, ((0, 32), (1, 4))),
        "w_value": gaussian(streams_of[5], (D, VD), D ** -0.5, 0.125, ((0, 32), (1, 4))),
        "w_gate": gaussian(streams_of[6], (D, VD), D ** -0.5, 0.125, ((0, 32), (1, 4))),
        "w_out": gaussian(streams_of[7], (VD, D), (VD // 4) ** -0.5, 0.1875, ((0, 4), (1, 32))),
        "norm2_gain": jnp.clip(1.0 + 0.15 * jax.random.normal(streams_of[8], (D,), jnp.float32), 0.25, 1.75).astype(jnp.bfloat16),
        "norm2_bias": gaussian(streams_of[9], (D,), 0.5, 3.0, ((0, 32),)),
        "w_up": gaussian(streams_of[10], (D, FF), D ** -0.5, 0.125, ((0, 32), (1, 4))),
        "w_down": gaussian(streams_of[11], (FF, D), FF ** -0.5, 0.09375, ((0, 4), (1, 32))),
        "decay_rate": jnp.clip(jnp.exp(math.log(0.03) - 7.8069405 * jax.random.uniform(streams_of[12], (HEADS,), jnp.float32) ** level_of(streams_of[12], (HEADS,), ((0, 4),), -0.2, 0.2)), 1.220703143189894e-05, 0.03),
        "out_grad": gaussian(streams_of[13], (TOKENS, D), 1.0, 6.0, ((0, 32),)),
    }


@jax.custom_vjp
def low(v):
    return lax.optimization_barrier(v.astype(jnp.bfloat16)).astype(jnp.float32)

@jax.custom_vjp
def low_back(v):
    return v

def low_keep(v):
    return (low(v), None)

def low_pass(kept, grad):
    return (grad,)

def back_keep(v):
    return (v, None)

def back_low(kept, grad):
    return (low(grad),)
low.defvjp(low_keep, low_pass)
low_back.defvjp(back_keep, back_low)

def layer_norm(values, gain, bias):
    center = values - lax.optimization_barrier(jnp.mean(values, axis=-1, keepdims=True))
    spread = lax.optimization_barrier(jnp.mean(center * center, axis=-1, keepdims=True))
    return center * lax.rsqrt(spread + 1e-05) * gain + bias

def group_norm(values):
    center = values - lax.optimization_barrier(jnp.mean(values, axis=-1, keepdims=True))
    spread = lax.optimization_barrier(jnp.mean(center * center, axis=-1, keepdims=True))
    return center * lax.rsqrt(spread + 1e-05)

def rotate(values, cosine, sine):
    half = values.shape[-1] // 2
    first = values[..., :half]
    second = values[..., half:]
    return jnp.concatenate([first * cosine - second * sine, second * cosine + first * sine], axis=-1)

def matmul(left, right):
    return jnp.dot(left, right, preferred_element_type=jnp.float32, precision=lax.Precision.HIGHEST)

def product(form, left, right):
    return jnp.einsum(form, left, right, precision=lax.Precision.HIGHEST)

def retention(query, key, value, rates):
    blocks = query.shape[0] // TOK_DEV
    index = jnp.arange(TOK_DEV).astype(jnp.float32)
    offset = index[:, None] - index[None, :]
    dmask = jnp.where(offset[None] >= 0.0, jnp.exp(-rates[:, None, None] * jnp.maximum(offset, 0.0)[None]), 0.0)
    qdec = jnp.exp(-rates[None, :] * (index[:, None] + 1.0))
    kdec = jnp.exp(-rates[None, :] * (TOK_DEV - 1.0 - index[:, None]))
    carry_decay = jnp.exp(-rates * TOK_DEV)

    def step(state, piece):
        qb, kb, vb = piece
        scores = low_back(product('ihd,jhd->hij', qb, kb))
        probs = low(scores * dmask)
        inner = product('hij,jhv->ihv', probs, vb)
        cross = qdec[:, :, None] * product('ihd,hdv->ihv', qb, state)
        fresh = product('jhd,jhv->hdv', kdec[:, :, None] * kb, vb)
        return (carry_decay[:, None, None] * state + fresh, inner + cross)
    start = jnp.zeros((HEADS, DK, DV), jnp.float32)
    pieces = (query.reshape(blocks, TOK_DEV, HEADS, DK), key.reshape(blocks, TOK_DEV, HEADS, DK), value.reshape(blocks, TOK_DEV, HEADS, DV))
    final, outs = lax.scan(jax.checkpoint(step), start, pieces)
    return outs.reshape(blocks * TOK_DEV, HEADS, DV)

def forward(stream, gain1, bias1, w_query, w_key, w_value, w_gate, w_out, gain2, bias2, w_up, w_down, rates):
    count = stream.shape[0]
    normed1 = low(layer_norm(stream, gain1, bias1))
    query_raw = low_back(matmul(normed1, w_query)).reshape(count, HEADS, DK)
    key_raw = low_back(matmul(normed1, w_key)).reshape(count, HEADS, DK)
    value = low(low_back(matmul(normed1, w_value))).reshape(count, HEADS, DV)
    gate_raw = low_back(matmul(normed1, w_gate))
    half = DK // 2
    position = jnp.arange(count).astype(jnp.float32)
    freq = 10000.0 ** (-jnp.arange(half).astype(jnp.float32) / half)
    angle = position[:, None] * freq[None, :]
    cosine = jnp.cos(angle)[:, None, :]
    sine = jnp.sin(angle)[:, None, :]
    query = low(rotate(query_raw, cosine, sine))
    key = low(rotate(key_raw, cosine, sine))
    retained = low_back(retention(query, key, value, rates))
    grouped = group_norm(retained).reshape(count, HEADS * DV)
    mixed = low(jax.nn.silu(gate_raw) * grouped)
    resid = stream + low_back(matmul(mixed, w_out))
    normed2 = low(layer_norm(resid, gain2, bias2))
    up_raw = low_back(matmul(normed2, w_up))
    hidden = low(jax.nn.gelu(up_raw, approximate=True))
    return resid + low_back(matmul(hidden, w_down))

def reference(tokens, norm1_gain, norm1_bias, w_query, w_key, w_value, w_gate, w_out, norm2_gain, norm2_bias, w_up, w_down, decay_rate, out_grad):
    primals = tuple((item.astype(jnp.float32) for item in (tokens, norm1_gain, norm1_bias, w_query, w_key, w_value, w_gate, w_out, norm2_gain, norm2_bias, w_up, w_down)))

    def wrapped(*items):
        return forward(*items, decay_rate)
    result, pullback = jax.vjp(wrapped, *primals)
    grads = pullback(out_grad.astype(jnp.float32))
    return (result.astype(jnp.bfloat16), grads[0], grads[1], grads[2], grads[3], grads[4], grads[5], grads[6], grads[7], grads[8], grads[9], grads[10], grads[11])
```

```python
import itertools

import jax
import jax.numpy as jnp
from jax import lax
from jax.sharding import Mesh, PartitionSpec as P

DK = 256
DV = 512
AXES = ("zl", "c", "x", "zh", "y")
SIZES = {"zl": 2, "c": 2, "x": 4, "zh": 2, "y": 4}
SPANS = ("x", "c", "y")
BF = jnp.bfloat16
F32 = jnp.float32


def pairs(axes, move):
    def flat(place):
        at = 0
        for axis in axes:
            at = at * SIZES[axis] + place[axis]
        return at

    found = []
    for values in itertools.product(*[range(SIZES[axis]) for axis in axes]):
        place = dict(zip(axes, values))
        target = move(dict(place))
        if target is not None:
            found.append((flat(place), flat(target)))
    return found


def swap_roles(values):
    return lax.ppermute(
        values, ("c", "zh"), pairs(("c", "zh"), lambda p: {"c": p["zh"], "zh": p["c"]})
    )


def z_shift(values, shift):
    def move(place):
        z = (place["zh"] * 2 + place["zl"] + shift) % 4
        return {"zl": z % 2, "zh": z // 2}

    return lax.ppermute(values, ("zl", "zh"), pairs(("zl", "zh"), move))


def z_shift_home(values, shift):
    def move(place):
        z = (place["zh"] * 2 + place["zl"] + shift) % 4
        if z // 2 != place["c"]:
            return None
        return {"zl": z % 2, "zh": z // 2, "c": place["c"]}

    return lax.ppermute(values, ("zl", "c", "zh"), pairs(("zl", "c", "zh"), move))


def core_from_home(values):
    def move(place):
        if place["zh"] != place["c"]:
            return None
        return {"c": 1 - place["c"], "zh": place["zh"]}

    return lax.ppermute(values, ("c", "zh"), pairs(("c", "zh"), move))


def core_swap(values):
    return lax.ppermute(values, "c", [(0, 1), (1, 0)])


def z_reduce(values):
    part = values.astype(BF)
    rows = part.shape[0] // 4
    total = values[:rows]
    for shift in (1, 3, 2):
        total = total + z_shift(part[shift * rows : (shift + 1) * rows], shift).astype(F32)
    return total


def z_gather(values):
    near, far, across = z_shift(values, 3), z_shift(values, 1), z_shift(values, 2)
    return jnp.concatenate([values, near, across, far], axis=0)


def z_gather_home(values, place, home):
    rows = values.shape[0]
    near, far, across = z_shift_home(values, 3), z_shift_home(values, 1), z_shift_home(values, 2)
    full = jnp.concatenate([values, near, across, far] * 2, axis=0)
    full = lax.dynamic_slice_in_dim(full, (4 - place) % 4 * rows, 4 * rows, 0)
    return jnp.where(home, full, core_from_home(full))


def nn(left, right):
    return jnp.dot(left, right, preferred_element_type=F32)


def nt(left, right):
    return lax.dot_general(left, right, (((1,), (1,)), ((), ())), preferred_element_type=F32)


def tn(left, right):
    return lax.dot_general(left, right, (((0,), (0,)), ((), ())), preferred_element_type=F32)


def norm_parts(values):
    center = values - jnp.mean(values, axis=-1, keepdims=True)
    spread = jnp.mean(center * center, axis=-1, keepdims=True)
    scale = lax.rsqrt(spread + 1e-05)
    return center * scale, scale


def norm_back(grad, hat, scale):
    mean_grad = jnp.mean(grad, axis=-1, keepdims=True)
    mean_both = jnp.mean(grad * hat, axis=-1, keepdims=True)
    return (grad - mean_grad - hat * mean_both) * scale


def span_scan(fresh, rate, reverse):
    parts = fresh.astype(BF).reshape(32, 16, DV)
    parts = lax.all_to_all(parts, SPANS, 0, 0, tiled=True)
    at = jnp.arange(32).astype(F32)
    steps = at[:, None] - 1.0 - at[None, :]
    decay = jnp.where(steps >= 0.0, jnp.exp(-256.0 * rate * jnp.maximum(steps, 0.0)), 0.0)
    if reverse:
        decay = decay.T
    carried = lax.dot_general(
        decay,
        parts.astype(F32),
        (((1,), (0,)), ((), ())),
        precision=lax.Precision.HIGHEST,
    ).astype(BF)
    return lax.all_to_all(carried, SPANS, 0, 0, tiled=True).reshape(2, DK, DV)


def scatter_direct(grad, core):
    cols = grad.shape[1]
    grad = grad.astype(BF).reshape(4, 2, 256, cols)
    mine = lax.dynamic_index_in_dim(grad, core, 1, False)
    other = lax.dynamic_index_in_dim(grad, 1 - core, 1, False)
    total = (mine.astype(F32) + core_swap(other).astype(F32)).astype(BF)
    total = lax.all_to_all(total.reshape(16, 64, cols), ("x", "y"), 0, 0, tiled=True)
    return jnp.sum(total.astype(F32), axis=0)


def scatter_wide(grad):
    return lax.psum_scatter(grad.astype(BF), SPANS, scatter_dimension=0, tiled=True)


def body(
    tokens,
    norm1_gain,
    norm1_bias,
    w_query,
    w_key,
    w_value,
    w_gate,
    w_out,
    norm2_gain,
    norm2_bias,
    w_up,
    w_down,
    decay_rate,
    out_grad,
):
    x, y, c = lax.axis_index("x"), lax.axis_index("y"), lax.axis_index("c")
    zl, zh = lax.axis_index("zl"), lax.axis_index("zh")
    z = zh * 2 + zl
    home = zh == c
    span = x * 8 + c * 4 + y

    gains = jnp.stack([norm1_gain, norm1_bias, norm2_gain, norm2_bias], axis=1)
    gains = jnp.pad(gains, ((0, 0), (0, 124)))
    first = swap_roles(jnp.concatenate([w_key, w_value, gains], axis=1))
    second = swap_roles(jnp.concatenate([w_query, w_gate, w_out.T, w_up, w_down.T], axis=1))
    rate = swap_roles(decay_rate)
    tokens = swap_roles(tokens)
    out_grad = swap_roles(out_grad)

    cols = first.shape[1]
    early = lax.all_to_all(
        jnp.broadcast_to(first[None], (16, 64, cols)), ("x", "y"), 0, 0, tiled=True
    )
    early_other = core_swap(early)
    low = jnp.where(c == 0, early, early_other).reshape(4, 1, 256, cols)
    high = jnp.where(c == 0, early_other, early).reshape(4, 1, 256, cols)
    early = jnp.concatenate([low, high], axis=1).reshape(2048, cols)
    late = lax.all_gather(second, SPANS, axis=0, tiled=True)
    full_key, full_value, gains = early[:, :512], early[:, 512:1536], early[:, 1536:].T.astype(F32)
    gain1, bias1, gain2, bias2 = gains[0], gains[1], gains[2], gains[3]
    full_query, full_gate = late[:, :512], late[:, 512:1536]
    full_out, full_up, full_down = late[:, 1536:2560], late[:, 2560:3584], late[:, 3584:]

    tokens = lax.dynamic_slice_in_dim(jnp.concatenate([tokens, tokens]), z * 64, 256, 0)
    out_grad = lax.dynamic_slice_in_dim(jnp.concatenate([out_grad, out_grad]), z * 64, 256, 0)
    index = ((jnp.arange(256) + z * 64) % 256).astype(F32)
    half = DK // 2
    position = (span * 256).astype(F32) + index
    freq = 10000.0 ** (-jnp.arange(half).astype(F32) / half)
    angle = position[:, None] * freq[None, :]
    cosine, sine = jnp.cos(angle), jnp.sin(angle)

    def turn(values):
        a, b = values[:, :half], values[:, half:]
        return jnp.concatenate([a * cosine - b * sine, b * cosine + a * sine], axis=1)

    def turn_back(values):
        a, b = values[:, :half], values[:, half:]
        return jnp.concatenate([a * cosine + b * sine, b * cosine - a * sine], axis=1)

    stream = tokens.astype(F32)
    hat1, scale1 = norm_parts(stream)
    normed1 = (hat1 * gain1 + bias1).astype(BF)

    offset = index[:, None] - index[None, :]
    masks, qdecs, kdecs = [], [], []
    for h in range(2):
        masks.append(
            jnp.where(offset >= 0.0, jnp.exp(-rate[h] * jnp.maximum(offset, 0.0)), 0.0)
        )
        qdecs.append(jnp.exp(-rate[h] * (index + 1.0))[:, None])
        kdecs.append(jnp.exp(-rate[h] * (255.0 - index))[:, None])

    key_raw = nn(normed1, full_key)
    value = nn(normed1, full_value).astype(BF)
    keys, values, fresh = [], [], []
    for h in range(2):
        keys.append(turn(key_raw[:, h * DK : (h + 1) * DK]).astype(BF))
        values.append(value[:, h * DV : (h + 1) * DV])
        fresh.append(tn((kdecs[h] * keys[h].astype(F32)).astype(BF), values[h]))
    scan_rate = jnp.where(x < 2, rate[0], rate[1])
    state = span_scan(jnp.stack(fresh), scan_rate, False)

    query_raw = nn(normed1, full_query)
    gate_raw = nn(normed1, full_gate)
    queries, probs, hats, scales = [], [], [], []
    for h in range(2):
        queries.append(turn(query_raw[:, h * DK : (h + 1) * DK]).astype(BF))
        probs.append((nt(queries[h], keys[h]) * masks[h]).astype(BF))
        retained = nn(probs[h], values[h]) + qdecs[h] * nn(queries[h], state[h])
        hat, scale = norm_parts(retained)
        hats.append(hat)
        scales.append(scale)
    grouped = jnp.concatenate(hats, axis=1)
    gate_sig = jax.nn.sigmoid(gate_raw)
    gate_act = gate_raw * gate_sig
    mixed = (gate_act * grouped).astype(BF)

    resid = stream[:64] + z_reduce(nt(mixed, full_out))
    hat2, scale2 = norm_parts(resid)
    normed2 = z_gather((hat2 * gain2 + bias2).astype(BF))
    up_raw = nn(normed2, full_up)

    def smooth(values):
        return jax.nn.gelu(values, approximate=True)

    hidden_wide, smooth_back = jax.vjp(smooth, up_raw)
    hidden = hidden_wide.astype(BF)
    d_hidden = nn(out_grad, full_down)
    d_up = smooth_back(d_hidden)[0].astype(BF)
    d_normed2 = z_reduce(nt(d_up, full_up))

    ffn = z_reduce(nt(hidden, full_down))
    block_out = z_gather_home((resid + ffn).astype(BF), z, home)

    own_grad = out_grad[:64].astype(F32)
    d_resid = own_grad + norm_back(d_normed2 * gain2, hat2, scale2)
    grad_gain2 = jnp.sum(d_normed2 * hat2, axis=0)
    grad_bias2 = jnp.sum(d_normed2, axis=0)
    d_attn = z_gather(d_resid.astype(BF))

    grad_ffn = scatter_wide(jnp.concatenate([tn(normed2, d_up), tn(out_grad, hidden)], axis=1))

    d_mixed = nn(d_attn, full_out)
    d_gate = (d_mixed * grouped * gate_sig * (1.0 + gate_raw * (1.0 - gate_sig))).astype(BF)
    d_grouped = d_mixed * gate_act
    d_rets, outgoing = [], []
    for h in range(2):
        d_ret = norm_back(d_grouped[:, h * DV : (h + 1) * DV], hats[h], scales[h]).astype(BF)
        d_rets.append(d_ret)
        outgoing.append(tn((qdecs[h] * queries[h].astype(F32)).astype(BF), d_ret))
    later = span_scan(jnp.stack(outgoing), scan_rate, True)

    grad_gate = scatter_wide(jnp.concatenate([tn(normed1, d_gate), tn(d_attn, mixed)], axis=1))

    d_query_raw, d_key_raw, d_value = [], [], []
    for h in range(2):
        d_scores = (nt(d_rets[h], values[h]) * masks[h]).astype(BF)
        d_query = nn(d_scores, keys[h]) + qdecs[h] * nt(d_rets[h], state[h])
        d_key = tn(d_scores, queries[h]) + kdecs[h] * nt(values[h], later[h])
        d_value.append((tn(probs[h], d_rets[h]) + kdecs[h] * nn(keys[h], later[h])).astype(BF))
        d_query_raw.append(turn_back(d_query).astype(BF))
        d_key_raw.append(turn_back(d_key).astype(BF))
    d_query_raw = jnp.concatenate(d_query_raw, axis=1)
    d_key_raw = jnp.concatenate(d_key_raw, axis=1)
    d_value = jnp.concatenate(d_value, axis=1)

    d_normed1 = z_reduce(
        nt(d_query_raw, full_query)
        + nt(d_key_raw, full_key)
        + nt(d_value, full_value)
        + nt(d_gate, full_gate)
    )
    grad_qkv = scatter_direct(
        tn(normed1, jnp.concatenate([d_query_raw, d_key_raw, d_value], axis=1)), c
    )
    tokens_grad = d_resid + norm_back(d_normed1 * gain1, hat1[:64], scale1[:64])
    tokens_grad = z_gather_home(tokens_grad.astype(BF), z, home).astype(F32)
    grad_gain1 = jnp.sum(d_normed1 * hat1[:64], axis=0)
    grad_bias1 = jnp.sum(d_normed1, axis=0)

    vectors = jnp.stack([grad_gain1, grad_bias1, grad_gain2, grad_bias2])
    vectors = vectors.reshape(4, 32, 64).transpose(1, 0, 2).reshape(1, 32, 256)
    vectors = jnp.broadcast_to(vectors, (4, 32, 256)).reshape(128, 256)
    vectors = lax.all_to_all(vectors, AXES, 0, 0, tiled=True)
    vectors = jnp.sum(vectors, axis=0)

    grad_qkv = swap_roles(grad_qkv.astype(BF)).astype(F32)
    grad_gate = swap_roles(grad_gate).astype(F32)
    grad_ffn = swap_roles(grad_ffn).astype(F32)
    return (
        block_out,
        tokens_grad,
        vectors[:64],
        vectors[64:128],
        grad_qkv[:, :512],
        grad_qkv[:, 512:1024],
        grad_qkv[:, 1024:],
        grad_gate[:, :1024],
        grad_gate[:, 1024:].T,
        vectors[128:192],
        vectors[192:],
        grad_ffn[:, :1024],
        grad_ffn[:, 1024:].T,
    )


def solution(mesh):
    fine = Mesh(mesh.devices.reshape(2, 2, 4, 2, 4), AXES)
    seq, tp = ("x", "zh", "y"), ("zl", "c")
    rows, wide, tall, vector = P(seq, None), P(seq, tp), P(tp, seq), P(seq)
    in_specs = (
        rows,
        vector,
        vector,
        wide,
        wide,
        wide,
        wide,
        tall,
        vector,
        vector,
        wide,
        tall,
        P(tp),
        rows,
    )
    out_specs = (
        rows,
        rows,
        vector,
        vector,
        wide,
        wide,
        wide,
        wide,
        tall,
        vector,
        vector,
        wide,
        tall,
    )
    return jax.shard_map(body, mesh=fine, in_specs=in_specs, out_specs=out_specs, check_vma=False)
```

```python
import functools
import itertools

import jax
import jax.numpy as jnp
from jax import lax
from jax.experimental import pallas as pl
from jax.experimental.pallas import tpu as pltpu
from jax.sharding import Mesh, PartitionSpec as P

DK = 256
DV = 512
AXES = ("zl", "c", "x", "zh", "y")
SIZES = {"zl": 2, "c": 2, "x": 4, "zh": 2, "y": 4}
SPANS = ("x", "c", "y")
BF = jnp.bfloat16
F32 = jnp.float32


def pairs(axes, move):
    def flat(place):
        at = 0
        for axis in axes:
            at = at * SIZES[axis] + place[axis]
        return at

    found = []
    for values in itertools.product(*[range(SIZES[axis]) for axis in axes]):
        place = dict(zip(axes, values))
        target = move(dict(place))
        if target is not None:
            found.append((flat(place), flat(target)))
    return found


def swap_roles(values):
    return lax.ppermute(
        values, ("c", "zh"), pairs(("c", "zh"), lambda p: {"c": p["zh"], "zh": p["c"]})
    )


def z_shift(values, shift):
    def move(place):
        z = (place["zh"] * 2 + place["zl"] + shift) % 4
        return {"zl": z % 2, "zh": z // 2}

    return lax.ppermute(values, ("zl", "zh"), pairs(("zl", "zh"), move))


def z_shift_home(values, shift):
    def move(place):
        z = (place["zh"] * 2 + place["zl"] + shift) % 4
        if z // 2 != place["c"]:
            return None
        return {"zl": z % 2, "zh": z // 2, "c": place["c"]}

    return lax.ppermute(values, ("zl", "c", "zh"), pairs(("zl", "c", "zh"), move))


def core_from_home(values):
    def move(place):
        if place["zh"] != place["c"]:
            return None
        return {"c": 1 - place["c"], "zh": place["zh"]}

    return lax.ppermute(values, ("c", "zh"), pairs(("c", "zh"), move))


def core_swap(values):
    return lax.ppermute(values, "c", [(0, 1), (1, 0)])


def z_reduce(part, mine):
    rows = part.shape[0] // 4
    total = mine
    for shift in (1, 3, 2):
        total = total + z_shift(part[shift * rows : (shift + 1) * rows], shift).astype(F32)
    return total


def z_gather(values):
    near, far, across = z_shift(values, 3), z_shift(values, 1), z_shift(values, 2)
    return jnp.concatenate([values, near, across, far], axis=0)


def z_gather_home(values, place, home, dtype):
    near, far, across = z_shift_home(values, 3), z_shift_home(values, 1), z_shift_home(values, 2)
    full = in_place(place, values, near, across, far)
    return chosen(home, full, core_from_home(full), dtype)


def nn(left, right):
    return jnp.dot(left, right, preferred_element_type=F32)


def nt(left, right):
    return lax.dot_general(left, right, (((1,), (1,)), ((), ())), preferred_element_type=F32)


def tn(left, right):
    return lax.dot_general(left, right, (((0,), (0,)), ((), ())), preferred_element_type=F32)


def norm_parts(values):
    center = values - jnp.mean(values, axis=-1, keepdims=True)
    spread = jnp.mean(center * center, axis=-1, keepdims=True)
    scale = lax.rsqrt(spread + 1e-05)
    return center * scale, scale


def norm_back(grad, hat, scale):
    mean_grad = jnp.mean(grad, axis=-1, keepdims=True)
    mean_both = jnp.mean(grad * hat, axis=-1, keepdims=True)
    return (grad - mean_grad - hat * mean_both) * scale


def scan_parts(fresh):
    return lax.all_to_all(fresh.reshape(32, 16, DV), SPANS, 0, 0, tiled=True)


def scan_back(carried):
    return lax.all_to_all(carried, SPANS, 0, 0, tiled=True).reshape(2 * DK, DV)


def halves_sum(own, other):
    total = (own.astype(F32) + core_swap(other).astype(F32)).astype(BF)
    return total.reshape(16, 64, own.shape[1])


def scatter_sum(total):
    total = lax.all_to_all(total, ("x", "y"), 0, 0, tiled=True)
    return jnp.sum(total.astype(F32), axis=0).astype(BF)


def run(kernel, grid, ins, outs, operands, flops, scratch=()):
    moved = sum(a.size * a.dtype.itemsize for a in operands)
    moved += sum(o[0].size * o[0].dtype.itemsize for o in outs)
    return pl.pallas_call(
        kernel,
        grid=grid,
        in_specs=ins,
        out_specs=[o[1] for o in outs],
        out_shape=[o[0] for o in outs],
        scratch_shapes=list(scratch),
        compiler_params=pltpu.CompilerParams(vmem_limit_bytes=48 * 1024 * 1024),
        cost_estimate=pl.CostEstimate(flops=int(flops), bytes_accessed=int(moved), transcendentals=0),
    )(*operands)


def shape(dims, dtype):
    return jax.ShapeDtypeStruct(dims, dtype)


def columns(rows, cols, first=0):
    return pl.BlockSpec((rows, cols), lambda h: (0, first + h))


def whole(dims):
    return pl.BlockSpec(dims, lambda h: (0,) * len(dims))


SCALARS = pl.BlockSpec(memory_space=pltpu.SMEM)


def places(dims, axis, z):
    at = lax.broadcasted_iota(jnp.int32, dims, axis) + z * 64
    return jnp.where(at >= 256, at - 256, at).astype(F32)


def decays(rate, z):
    at = places((256, 1), 0, z)
    return jnp.exp(-rate * (at + 1.0)), jnp.exp(-rate * (255.0 - at))


def span_mask(rate, z):
    offset = places((256, 256), 0, z) - places((256, 256), 1, z)
    return jnp.where(offset >= 0.0, jnp.exp(-rate * jnp.maximum(offset, 0.0)), 0.0)


def turn_into(ref, values, cosine, sine, start=0):
    half = DK // 2
    a, b = values[:, :half], values[:, half:]
    ref[:, start : start + half] = (a * cosine - b * sine).astype(ref.dtype)
    ref[:, start + half : start + DK] = (b * cosine + a * sine).astype(ref.dtype)


def in_place_kernel(place, *refs):
    out = refs[-1]
    for k in range(4):
        at = place[0] + k
        at = pl.multiple_of(jnp.where(at >= 4, at - 4, at) * 64, 64)
        out[pl.ds(at, 64), :] = refs[k][...]


def in_place(place, *pieces):
    return run(
        in_place_kernel,
        (1,),
        [SCALARS] + [whole((64, 2048))] * 4,
        [(shape((256, 2048), BF), whole((256, 2048)))],
        [place, *pieces],
        1,
    )[0]


def chosen_kernel(home, mine, other, out):
    @pl.when(home[0] == 1)
    def here():
        out[...] = mine[...].astype(out.dtype)

    @pl.when(home[0] == 0)
    def there():
        out[...] = other[...].astype(out.dtype)


def chosen(home, mine, other, dtype):
    block = pl.BlockSpec((128, 2048), lambda i: (i, 0))
    return run(
        chosen_kernel,
        (2,),
        [SCALARS, block, block],
        [(shape((256, 2048), dtype), block)],
        [home, mine, other],
        1,
    )[0]


def scan_kernel(reverse, rate, parts, out):
    decay = jnp.exp(jnp.full((16, DV), -256.0 * rate[0], F32))
    state = jnp.zeros((16, DV), F32)
    for k in range(31, -1, -1) if reverse else range(32):
        out[k] = state.astype(BF)
        state = decay * state + parts[k].astype(F32)


def scan_spans(rate, parts, reverse):
    dims = (32, 16, DV)
    return run(
        functools.partial(scan_kernel, reverse),
        (1,),
        [SCALARS, whole(dims)],
        [(shape(dims, BF), whole(dims))],
        [rate, parts],
        2 * 32 * 16 * DV,
    )[0]


def pack_kernel(*refs):
    out, start = refs[-1], 0
    for ref in refs[:-1]:
        out[:, start : start + ref.shape[1]] = ref[...]
        start += ref.shape[1]


def pack(*parts):
    cols = sum(p.shape[1] for p in parts)
    return run(
        pack_kernel,
        (1,),
        [whole(p.shape) for p in parts],
        [(shape((64, cols), BF), whole((64, cols)))],
        list(parts),
        1,
    )[0]


def pack_first_kernel(w_key, w_value, gains, out):
    out[:, :512] = w_key[...]
    out[:, 512:1536] = w_value[...]
    wide = gains[...].astype(F32)
    same = lax.broadcasted_iota(jnp.int32, (64, 64), 0) == lax.broadcasted_iota(
        jnp.int32, (64, 64), 1
    )
    lane = lax.broadcasted_iota(jnp.int32, (64, 128), 1)
    total = jnp.zeros((64, 128), F32)
    for k in range(4):
        column = jnp.sum(jnp.where(same, wide[k : k + 1, :], 0.0), axis=1, keepdims=True)
        total = jnp.where(lane == k, column, total)
    out[:, 1536:] = total.astype(BF)


def pack_first(w_key, w_value, gains):
    return run(
        pack_first_kernel,
        (1,),
        [whole((64, 512)), whole((64, 1024)), whole((4, 64))],
        [(shape((64, 1664), BF), whole((64, 1664)))],
        [w_key, w_value, gains],
        1,
    )[0]


def norm_kernel(place, tokens, gains_own, gains_other, normed, own, other, hat, scale, gains):
    values = tokens[...].astype(F32)
    made, spread = norm_parts(values)
    scale[...] = spread
    hat[...] = made
    mine = gains_own[...].astype(F32).T
    yours = gains_other[...].astype(F32).T
    for i in range(4):
        for ref, rows, side in ((own, mine, place[1]), (other, yours, 1 - place[1])):
            at = pl.multiple_of((2 * i + side) * 256, 256)
            rows = rows[:8, i * 256 : i * 256 + 256]
            gains[:, pl.ds(at, 256)] = rows
            out = (hat[:, pl.ds(at, 256)] * rows[0:1] + rows[1:2]).astype(BF)
            normed[:, pl.ds(at, 256)] = out
            ref[:, i * 256 : i * 256 + 256] = out


def norm_first(place, tokens, early, early_other):
    gains = pl.BlockSpec((1024, 128), lambda h: (0, 12))
    return run(
        norm_kernel,
        (1,),
        [SCALARS, whole((256, 2048)), gains, gains],
        [
            (shape((256, 2048), BF), whole((256, 2048))),
            (shape((256, 1024), BF), whole((256, 1024))),
            (shape((256, 1024), BF), whole((256, 1024))),
            (shape((256, 2048), F32), whole((256, 2048))),
            (shape((256, 1), F32), whole((256, 1))),
            (shape((8, 2048), F32), whole((8, 2048))),
        ],
        [place, tokens, early, early_other],
        10 * 256 * 2048,
    )


def kv_kernel(
    rate, place, own, other, key_own, key_other, value_own, value_other, cosine, sine, key, value, fresh
):
    qdec, kdec = decays(rate[pl.program_id(0)], place[0])
    raw = nn(own[...], key_own[...]) + nn(other[...], key_other[...])
    turn_into(key, raw, cosine[...], sine[...])
    made = (nn(own[...], value_own[...]) + nn(other[...], value_other[...])).astype(BF)
    value[...] = made
    fresh[...] = tn((kdec * key[...].astype(F32)).astype(BF), made).astype(BF)


def key_value(rate, place, own, other, early, early_other, cosine, sine):
    return run(
        kv_kernel,
        (2,),
        [
            SCALARS,
            SCALARS,
            whole((256, 1024)),
            whole((256, 1024)),
            columns(1024, 256),
            columns(1024, 256),
            columns(1024, 512, 1),
            columns(1024, 512, 1),
            whole((256, 128)),
            whole((256, 128)),
        ],
        [
            (shape((256, 512), BF), columns(256, 256)),
            (shape((256, 1024), BF), columns(256, 512)),
            (shape((512, 512), BF), pl.BlockSpec((256, 512), lambda h: (h, 0))),
        ],
        [rate, place, own, other, early, early_other, early, early_other, cosine, sine],
        2 * 256 * 2048 * 1536,
    )


def query_kernel(
    rate, place, normed, w_query, w_gate, key, value, cosine, sine, query, gate, probs, inner
):
    raw = nn(normed[...], w_query[...])
    turn_into(query, raw, cosine[...], sine[...])
    gate[...] = nn(normed[...], w_gate[...])
    mask = span_mask(rate[pl.program_id(0)], place[0])
    made = (nt(query[...], key[...]) * mask).astype(BF)
    probs[0] = made
    inner[...] = nn(made, value[...])


def query_gate(rate, place, normed1, late, key, value, cosine, sine):
    return run(
        query_kernel,
        (2,),
        [
            SCALARS,
            SCALARS,
            whole((256, 2048)),
            columns(2048, 256, 16),
            columns(2048, 512),
            columns(256, 256),
            columns(256, 512),
            whole((256, 128)),
            whole((256, 128)),
        ],
        [
            (shape((256, 512), BF), columns(256, 256)),
            (shape((256, 1024), F32), columns(256, 512)),
            (shape((2, 256, 256), BF), pl.BlockSpec((1, 256, 256), lambda h: (h, 0, 0))),
            (shape((256, 1024), F32), columns(256, 512)),
        ],
        [rate, place, normed1, late, late, key, value, cosine, sine],
        2 * 256 * 2048 * 1536,
    )


def retain_kernel(
    rate, place, query, state, inner, gate, w_out, hat, scale, mixed, part, own, total
):
    h = pl.program_id(0)
    qdec, kdec = decays(rate[h], place[0])
    retained = inner[...] + qdec * nn(query[...], state[...])
    made, spread = norm_parts(retained)
    hat[...] = made
    scale[0] = spread
    wide = gate[...]
    made = (wide * jax.nn.sigmoid(wide) * made).astype(BF)
    mixed[...] = made
    partial = nt(made, w_out[...])

    @pl.when(h == 0)
    def first():
        total[...] = partial

    @pl.when(h == 1)
    def last():
        full = total[...] + partial
        part[...] = full.astype(BF)
        own[...] = full[:64]


def retain(rate, place, query, state, inner, gate, late):
    return run(
        retain_kernel,
        (2,),
        [
            SCALARS,
            SCALARS,
            columns(256, 256),
            pl.BlockSpec((256, 512), lambda h: (h, 0)),
            columns(256, 512),
            columns(256, 512),
            columns(2048, 512, 2),
        ],
        [
            (shape((256, 1024), F32), columns(256, 512)),
            (shape((2, 256, 1), F32), pl.BlockSpec((1, 256, 1), lambda h: (h, 0, 0))),
            (shape((256, 1024), BF), columns(256, 512)),
            (shape((256, 2048), BF), whole((256, 2048))),
            (shape((64, 2048), F32), whole((64, 2048))),
        ],
        [rate, place, query, state, inner, gate, late],
        2 * 256 * 2048 * 1024,
        [pltpu.VMEM((256, 2048), F32)],
    )


def up_kernel(normed, w_up, d_hidden, hidden, d_up, part, own, total):
    j = pl.program_id(0)
    raw = nn(normed[...], w_up[...])
    root = 0.7978845608028654
    square = raw * raw
    tanh = jnp.tanh(root * raw * (1.0 + 0.044715 * square))
    half = 0.5 * (1.0 + tanh)
    hidden[...] = (raw * half).astype(BF)
    slope = half + 0.5 * raw * (1.0 - tanh * tanh) * root * (1.0 + 0.134145 * square)
    made = (slope * d_hidden[...]).astype(BF)
    d_up[...] = made
    partial = nt(made, w_up[...])

    @pl.when(j == 0)
    def first():
        total[...] = partial

    @pl.when(j == 1)
    def last():
        full = total[...] + partial
        part[...] = full.astype(BF)
        own[...] = full[:64]


def up_back(normed2, late, d_hidden):
    return run(
        up_kernel,
        (2,),
        [whole((256, 2048)), columns(2048, 512, 4), columns(256, 512)],
        [
            (shape((256, 1024), BF), columns(256, 512)),
            (shape((256, 1024), BF), columns(256, 512)),
            (shape((256, 2048), BF), whole((256, 2048))),
            (shape((64, 2048), F32), whole((64, 2048))),
        ],
        [normed2, late, d_hidden],
        4 * 256 * 2048 * 1024,
        [pltpu.VMEM((256, 2048), F32)],
    )


def mixed_kernel(rate, place, d_attn, w_out, gate, hat, scale, query, d_gate, d_ret, outgoing):
    qdec, kdec = decays(rate[pl.program_id(0)], place[0])
    d_mixed = nn(d_attn[...], w_out[...])
    wide, normed = gate[...], hat[...]
    sig = jax.nn.sigmoid(wide)
    d_gate[...] = (d_mixed * normed * sig * (1.0 + wide * (1.0 - sig))).astype(BF)
    made = norm_back(d_mixed * wide * sig, normed, scale[0]).astype(BF)
    d_ret[...] = made
    outgoing[...] = tn((qdec * query[...].astype(F32)).astype(BF), made).astype(BF)


def mixed_back(rate, place, d_attn, late, gate, hat, scale, query):
    return run(
        mixed_kernel,
        (2,),
        [
            SCALARS,
            SCALARS,
            whole((256, 2048)),
            columns(2048, 512, 2),
            columns(256, 512),
            columns(256, 512),
            pl.BlockSpec((1, 256, 1), lambda h: (h, 0, 0)),
            columns(256, 256),
        ],
        [
            (shape((256, 1024), BF), columns(256, 512)),
            (shape((256, 1024), BF), columns(256, 512)),
            (shape((512, 512), BF), pl.BlockSpec((256, 512), lambda h: (h, 0))),
        ],
        [rate, place, d_attn, late, gate, hat, scale, query],
        2 * 256 * 2048 * 1024,
    )


def query_back_kernel(
    rate, place, d_ret, value, key, query, probs, state, cosine, sine, d_query, key_part, value_part
):
    h = pl.program_id(0)
    qdec, kdec = decays(rate[h], place[0])
    mask = span_mask(rate[h], place[0])
    d_scores = (nt(d_ret[...], value[...]) * mask).astype(BF)
    turned = nn(d_scores, key[...]) + qdec * nt(d_ret[...], state[...])
    turn_into(d_query, turned, cosine[...], -sine[...])
    key_part[...] = tn(d_scores, query[...])
    value_part[...] = tn(probs[0], d_ret[...])


def query_back(rate, place, d_ret, value, key, query, probs, state, cosine, sine):
    return run(
        query_back_kernel,
        (2,),
        [
            SCALARS,
            SCALARS,
            columns(256, 512),
            columns(256, 512),
            columns(256, 256),
            columns(256, 256),
            pl.BlockSpec((1, 256, 256), lambda h: (h, 0, 0)),
            pl.BlockSpec((256, 512), lambda h: (h, 0)),
            whole((256, 128)),
            whole((256, 128)),
        ],
        [
            (shape((256, 512), BF), columns(256, 256)),
            (shape((256, 512), F32), columns(256, 256)),
            (shape((256, 1024), F32), columns(256, 512)),
        ],
        [rate, place, d_ret, value, key, query, probs, state, cosine, sine],
        2 * 256 * 256 * 2 * 2000,
    )


def key_value_back_kernel(
    rate, place, key_part, value_part, key, value, later, cosine, sine, d_both
):
    for h in range(2):
        qdec, kdec = decays(rate[h], place[0])
        keys, values = slice(h * DK, h * DK + DK), slice(h * DV, h * DV + DV)
        carried = later[keys, :]
        d_key = key_part[:, keys] + kdec * nt(value[:, values], carried)
        turn_into(d_both, d_key, cosine[...], -sine[...], h * DK)
        d_value = value_part[:, values] + kdec * nn(key[:, keys], carried)
        d_both[:, 512 + h * DV : 512 + h * DV + DV] = d_value.astype(BF)


def key_value_back(rate, place, key_part, value_part, key, value, later, cosine, sine):
    return run(
        key_value_back_kernel,
        (1,),
        [
            SCALARS,
            SCALARS,
            whole((256, 512)),
            whole((256, 1024)),
            whole((256, 512)),
            whole((256, 1024)),
            whole((512, 512)),
            whole((256, 128)),
            whole((256, 128)),
        ],
        [(shape((256, 1536), BF), whole((256, 1536)))],
        [rate, place, key_part, value_part, key, value, later, cosine, sine],
        2 * 256 * 256 * 512 * 4,
    )[0]


def normed_first_kernel(d_query, d_gate, w_query, w_gate, part):
    part[...] = nt(d_query[...], w_query[...]) + nt(d_gate[...], w_gate[...])


def normed_back_first(d_query, d_gate, late):
    return run(
        normed_first_kernel,
        (4,),
        [
            whole((256, 512)),
            whole((256, 1024)),
            pl.BlockSpec((512, 512), lambda i: (i, 8)),
            pl.BlockSpec((512, 1024), lambda i: (i, 0)),
        ],
        [(shape((256, 2048), F32), columns(256, 512))],
        [d_query, d_gate, late, late],
        2 * 256 * 2048 * 1536,
    )[0]


def normed_back_kernel(place, first, d_both, w_own, w_other, hat, part, own, vectors):
    left = nt(d_both[...], w_own[:, :1536])
    right = nt(d_both[...], w_other[:, :1536])
    low = place[1] == 0
    total = first[...] + jnp.concatenate(
        [jnp.where(low, left, right), jnp.where(low, right, left)], axis=1
    )
    part[...] = total.astype(BF)
    own[...] = total[:64]
    vectors[0:1] = jnp.sum(total * hat[...], axis=0, keepdims=True)
    vectors[1:2] = jnp.sum(total, axis=0, keepdims=True)


def normed_back(place, first, d_both, early, early_other, hat):
    weights = pl.BlockSpec((256, 1664), lambda i: (i, 0))
    return run(
        normed_back_kernel,
        (4,),
        [
            SCALARS,
            columns(256, 512),
            whole((256, 1536)),
            weights,
            weights,
            columns(256, 512),
        ],
        [
            (shape((256, 2048), BF), columns(256, 512)),
            (shape((64, 2048), F32), columns(64, 512)),
            (shape((2, 2048), F32), columns(2, 512)),
        ],
        [place, first, d_both, early, early_other, hat],
        2 * 256 * 2048 * 1536,
    )


def triple_kernel(*refs):
    w, out = pl.program_id(0), refs[-1]
    for k in range(3):

        @pl.when(w == k)
        def one(k=k):
            out[...] = tn(refs[2 * k][...], refs[2 * k + 1][...]).astype(BF)


def grad_triple(*operands):
    def left(w):
        return pl.BlockSpec(
            (256, 512), lambda v, i: (0, jnp.where(v == w, i, jnp.where(v > w, 3, 0)))
        )

    right = pl.BlockSpec((256, 1024), lambda v, i: (0, 0))
    return run(
        triple_kernel,
        (3, 4),
        [left(0), right, left(1), right, left(2), right],
        [(shape((2048, 3072), BF), pl.BlockSpec((512, 1024), lambda v, i: (i, v)))],
        list(operands),
        2 * 256 * 2048 * 3072,
    )[0]


def split_kernel(place, left, *refs):
    rights, own, other = refs[:-2], refs[-2], refs[-1]
    for ref, side in ((own, place[1]), (other, 1 - place[1])):
        at = pl.multiple_of(side * 256, 256)
        rows = left[:, pl.ds(at, 256)]
        start = 0
        for right in rights:
            ref[:, start : start + right.shape[1]] = tn(rows, right[...]).astype(BF)
            start += right.shape[1]


def grad_split(place, left, rights):
    cols = sum(r.shape[1] for r in rights)
    half = (shape((1024, cols), BF), pl.BlockSpec((256, cols), lambda i: (i, 0)))
    return run(
        split_kernel,
        (4,),
        [SCALARS, columns(256, 512)] + [whole(r.shape) for r in rights],
        [half, half],
        [place, left, *rights],
        2 * 256 * 2048 * cols,
    )


def widen_kernel(values, *outs):
    start = 0
    for out in outs:
        out[...] = values[:, start : start + out.shape[1]].astype(F32)
        start += out.shape[1]


def widen(values, widths):
    return run(
        widen_kernel,
        (1,),
        [whole(values.shape)],
        [(shape((64, n), F32), whole((64, n))) for n in widths],
        [values],
        1,
    )


def body(
    tokens,
    norm1_gain,
    norm1_bias,
    w_query,
    w_key,
    w_value,
    w_gate,
    w_out,
    norm2_gain,
    norm2_bias,
    w_up,
    w_down,
    decay_rate,
    out_grad,
):
    x, y, c = lax.axis_index("x"), lax.axis_index("y"), lax.axis_index("c")
    zl, zh = lax.axis_index("zl"), lax.axis_index("zh")
    z = zh * 2 + zl
    home = (zh == c).astype(jnp.int32).reshape(1)
    span = x * 8 + c * 4 + y
    place = jnp.stack([z, c]).astype(jnp.int32)

    first = pack_first(
        w_key, w_value, jnp.stack([norm1_gain, norm1_bias, norm2_gain, norm2_bias])
    )
    first, w_gate = lax.optimization_barrier((first, w_gate))
    first = swap_roles(first)
    second = swap_roles(pack(w_gate, w_out.T, w_up, w_down.T, w_query))
    rate = swap_roles(decay_rate)
    tokens = swap_roles(tokens)
    out_grad = swap_roles(out_grad)

    cols = first.shape[1]
    early = lax.all_to_all(
        jnp.broadcast_to(first[None], (16, 64, cols)), ("x", "y"), 0, 0, tiled=True
    ).reshape(1024, cols)
    late = lax.all_gather(second, SPANS, axis=0, tiled=True)

    tokens = lax.dynamic_slice_in_dim(jnp.concatenate([tokens, tokens]), z * 64, 256, 0)
    out_grad = lax.dynamic_slice_in_dim(jnp.concatenate([out_grad, out_grad]), z * 64, 256, 0)
    index = ((jnp.arange(256) + z * 64) % 256).astype(F32)
    half = DK // 2
    position = (span * 256).astype(F32) + index
    freq = 10000.0 ** (-jnp.arange(half).astype(F32) / half)
    angle = position[:, None] * freq[None, :]
    cosine, sine = jnp.cos(angle), jnp.sin(angle)
    early, tokens, out_grad, cosine, sine, rate = lax.optimization_barrier(
        (early, tokens, out_grad, cosine, sine, rate)
    )

    early_other = core_swap(early)
    normed1, own, other, hat1, scale1, gains = norm_first(place, tokens, early, early_other)
    gain1, gain2, bias2 = gains[0], gains[2], gains[3]
    key, value, fresh = key_value(rate, place, own, other, early, early_other, cosine, sine)
    scan_rate = jnp.where(x < 2, rate[0], rate[1]).reshape(1)
    carried = scan_spans(scan_rate, scan_parts(fresh), False)
    late, carried = lax.optimization_barrier((late, carried))
    state = scan_back(carried)
    query, gate, probs, inner = query_gate(
        rate, place, normed1, late, key, value, cosine, sine
    )
    hat, scale, mixed, part, mine = retain(rate, place, query, state, inner, gate, late)

    full_down = late[:, 3072:4096]
    d_hidden = nn(out_grad, full_down)
    resid = tokens[:64].astype(F32) + z_reduce(part, mine)
    hat2, scale2 = norm_parts(resid)
    normed2 = z_gather((hat2 * gain2 + bias2).astype(BF))
    hidden, d_up, part, mine = up_back(normed2, late, d_hidden)
    d_normed2 = z_reduce(part, mine)

    ffn = nt(hidden, full_down)
    ffn = z_reduce(ffn.astype(BF), ffn[:64])
    block_out = z_gather_home((resid + ffn).astype(BF), place, home, BF)

    own_grad = out_grad[:64].astype(F32)
    d_resid = own_grad + norm_back(d_normed2 * gain2, hat2, scale2)
    grad_gain2 = jnp.sum(d_normed2 * hat2, axis=0)
    grad_bias2 = jnp.sum(d_normed2, axis=0)
    d_attn = z_gather(d_resid.astype(BF))

    d_gate, d_ret, outgoing = mixed_back(rate, place, d_attn, late, gate, hat, scale, query)
    carried = scan_spans(scan_rate, scan_parts(outgoing), True)
    grad_wide = swap_roles(
        lax.psum_scatter(
            grad_triple(normed2, d_up, out_grad, hidden, d_attn, mixed),
            SPANS,
            scatter_dimension=0,
            tiled=True,
        )
    )
    later = scan_back(carried)

    d_query, key_part, value_part = query_back(
        rate, place, d_ret, value, key, query, probs, state, cosine, sine
    )
    d_first = normed_back_first(d_query, d_gate, late)
    grad_gate = halves_sum(*grad_split(place, normed1, [d_gate, d_query]))
    grad_gate, later = lax.optimization_barrier((grad_gate, later))
    grad_gate = scatter_sum(grad_gate)
    d_both = key_value_back(
        rate, place, key_part, value_part, key, value, later, cosine, sine
    )
    grad_both = halves_sum(*grad_split(place, normed1, [d_both]))
    grad_both, grad_gate = lax.optimization_barrier((grad_both, grad_gate))
    grad_both = scatter_sum(grad_both)

    part, mine, vectors1 = normed_back(place, d_first, d_both, early, early_other, hat1)
    d_normed1 = z_reduce(part, mine)
    tokens_grad = d_resid + norm_back(d_normed1 * gain1, hat1[:64], scale1[:64])
    tokens_grad = z_gather_home(tokens_grad.astype(BF), place, home, F32)

    vectors = jnp.concatenate([vectors1, jnp.stack([grad_gain2, grad_bias2])])
    vectors = vectors.reshape(4, 32, 64).transpose(1, 0, 2).reshape(1, 32, 256)
    vectors = jnp.broadcast_to(vectors, (4, 32, 256)).reshape(128, 256)
    vectors, grad_both = lax.optimization_barrier((vectors, grad_both))
    vectors = lax.all_to_all(vectors, AXES, 0, 0, tiled=True)
    vectors = jnp.sum(vectors, axis=0)

    grad_key, grad_value = widen(swap_roles(grad_both), [512, 1024])
    grad_gate, grad_query = widen(swap_roles(grad_gate), [1024, 512])
    grad_up, grad_down, grad_out = widen(grad_wide, [1024, 1024, 1024])
    return (
        block_out,
        tokens_grad,
        vectors[:64],
        vectors[64:128],
        grad_query,
        grad_key,
        grad_value,
        grad_gate,
        grad_out.T,
        vectors[128:192],
        vectors[192:],
        grad_up,
        grad_down.T,
    )


def solution(mesh):
    fine = Mesh(mesh.devices.reshape(2, 2, 4, 2, 4), AXES)
    seq, tp = ("x", "zh", "y"), ("zl", "c")
    rows, wide, tall, vector = P(seq, None), P(seq, tp), P(tp, seq), P(seq)
    in_specs = (
        rows,
        vector,
        vector,
        wide,
        wide,
        wide,
        wide,
        tall,
        vector,
        vector,
        wide,
        tall,
        P(tp),
        rows,
    )
    out_specs = (
        rows,
        rows,
        vector,
        vector,
        wide,
        wide,
        wide,
        wide,
        tall,
        vector,
        vector,
        wide,
        tall,
    )
    return jax.shard_map(body, mesh=fine, in_specs=in_specs, out_specs=out_specs, check_vma=False)
```

```python
import functools
import itertools

import jax
import jax.numpy as jnp
from jax import lax
from jax.experimental import pallas as pl
from jax.experimental.pallas import tpu as pltpu
from jax.sharding import Mesh, PartitionSpec as P

DK = 256
DV = 512
AXES = ("zl", "c", "x", "zh", "y")
SIZES = {"zl": 2, "c": 2, "x": 4, "zh": 2, "y": 4}
SPANS = ("x", "c", "y")
CHIPS = ("c", "x", "y")
ALONG_X = [[x * 4 + y for x in range(4)] for y in range(4)]
ALONG_Y = [[x * 4 + y for y in range(4)] for x in range(4)]


def other_core(groups):
    return [[16 + i for i in group] for group in groups]


FIRST_WAY = ALONG_X + other_core(ALONG_Y)
SECOND_WAY = ALONG_Y + other_core(ALONG_X)
BF = jnp.bfloat16
F32 = jnp.float32


def pairs(axes, move):
    def flat(place):
        at = 0
        for axis in axes:
            at = at * SIZES[axis] + place[axis]
        return at

    found = []
    for values in itertools.product(*[range(SIZES[axis]) for axis in axes]):
        place = dict(zip(axes, values))
        target = move(dict(place))
        if target is not None:
            found.append((flat(place), flat(target)))
    return found


def swap_roles(values):
    return lax.ppermute(
        values, ("c", "zh"), pairs(("c", "zh"), lambda p: {"c": p["zh"], "zh": p["c"]})
    )


def z_shift(values, shift):
    def move(place):
        z = (place["zh"] * 2 + place["zl"] + shift) % 4
        return {"zl": z % 2, "zh": z // 2}

    return lax.ppermute(values, ("zl", "zh"), pairs(("zl", "zh"), move))


def z_shift_home(values, shift):
    def move(place):
        z = (place["zh"] * 2 + place["zl"] + shift) % 4
        if z // 2 != place["c"]:
            return None
        return {"zl": z % 2, "zh": z // 2, "c": place["c"]}

    return lax.ppermute(values, ("zl", "c", "zh"), pairs(("zl", "c", "zh"), move))


def core_from_home(values):
    def move(place):
        if place["zh"] != place["c"]:
            return None
        return {"c": 1 - place["c"], "zh": place["zh"]}

    return lax.ppermute(values, ("c", "zh"), pairs(("c", "zh"), move))


def core_swap(values):
    return lax.ppermute(values, "c", [(0, 1), (1, 0)])


def z_collect(parts):
    return [z_shift(parts[shift - 1], shift) for shift in (1, 3, 2)]


def z_gather(values):
    return [values, z_shift(values, 3), z_shift(values, 2), z_shift(values, 1)]


def z_gather_home(values, place, home, dtype):
    near, far, across = z_shift_home(values, 3), z_shift_home(values, 1), z_shift_home(values, 2)
    full = in_place(place, values, near, across, far)
    return chosen(home, full, core_from_home(full), dtype)


def to_owner(values, flip_z, flip_core):
    def move(place):
        return {"zl": place["zl"] ^ flip_z, "zh": place["c"], "c": place["zh"] ^ flip_core}

    return lax.ppermute(values, ("zl", "c", "zh"), pairs(("zl", "c", "zh"), move))


def nn(left, right):
    return jnp.dot(left, right, preferred_element_type=F32)


def nt(left, right):
    return lax.dot_general(left, right, (((1,), (1,)), ((), ())), preferred_element_type=F32)


def tn(left, right):
    return lax.dot_general(left, right, (((0,), (0,)), ((), ())), preferred_element_type=F32)


def norm_parts(values):
    center = values - jnp.mean(values, axis=-1, keepdims=True)
    spread = jnp.mean(center * center, axis=-1, keepdims=True)
    scale = lax.rsqrt(spread + 1e-05)
    return center * scale, scale


def norm_back(grad, hat, scale):
    mean_grad = jnp.mean(grad, axis=-1, keepdims=True)
    mean_both = jnp.mean(grad * hat, axis=-1, keepdims=True)
    return (grad - mean_grad - hat * mean_both) * scale


def scan_parts(fresh):
    return lax.all_to_all(fresh.reshape(32, 16, DV), SPANS, 0, 0, tiled=True)


def scan_back(carried):
    return lax.all_to_all(carried, SPANS, 0, 0, tiled=True).reshape(2 * DK, DV)


def exchange(values, groups):
    return lax.all_to_all(values, CHIPS, 0, 0, axis_index_groups=groups, tiled=True)


def run(kernel, grid, ins, outs, operands, scratch=(), limit=48, flops=1, moved=1):
    return pl.pallas_call(
        kernel,
        grid=grid,
        in_specs=ins,
        out_specs=[o[1] for o in outs],
        out_shape=[pltpu.HBM(o[0].shape, o[0].dtype) if len(o) > 2 else o[0] for o in outs],
        scratch_shapes=list(scratch),
        compiler_params=pltpu.CompilerParams(vmem_limit_bytes=limit * 1024 * 1024),
        cost_estimate=pl.CostEstimate(flops=flops, bytes_accessed=moved, transcendentals=0),
    )(*operands)


def shape(dims, dtype):
    return jax.ShapeDtypeStruct(dims, dtype)


def columns(rows, cols, first=0):
    return pl.BlockSpec((rows, cols), lambda h: (0, first + h))


def whole(dims):
    return pl.BlockSpec(dims, lambda h: (0,) * len(dims))


SCALARS = pl.BlockSpec(memory_space=pltpu.SMEM)


def places(dims, axis, z):
    at = lax.broadcasted_iota(jnp.int32, dims, axis) + z * 64
    return jnp.where(at >= 256, at - 256, at).astype(F32)


def decays(rate, z):
    at = places((256, 1), 0, z)
    return jnp.exp(-rate * (at + 1.0)), jnp.exp(-rate * (255.0 - at))


def span_mask(rate, z):
    offset = places((256, 256), 0, z) - places((256, 256), 1, z)
    return jnp.where(offset >= 0.0, jnp.exp(-rate * jnp.maximum(offset, 0.0)), 0.0)


def turn_into(ref, values, cosine, sine, start=0):
    half = DK // 2
    a, b = values[:, :half], values[:, half:]
    ref[:, start : start + half] = (a * cosine - b * sine).astype(ref.dtype)
    ref[:, start + half : start + DK] = (b * cosine + a * sine).astype(ref.dtype)


def in_place_kernel(place, *refs):
    out = refs[-1]
    for k in range(4):
        at = place[0] + k
        at = pl.multiple_of(jnp.where(at >= 4, at - 4, at) * 64, 64)
        out[pl.ds(at, 64), :] = refs[k][...]


def in_place(place, *pieces):
    return run(
        in_place_kernel,
        (1,),
        [SCALARS] + [whole((64, 2048))] * 4,
        [(shape((256, 2048), BF), whole((256, 2048)))],
        [place, *pieces],
    )[0]


def chosen_kernel(home, mine, other, out):
    @pl.when(home[0] == 1)
    def here():
        out[...] = mine[...].astype(out.dtype)

    @pl.when(home[0] == 0)
    def there():
        out[...] = other[...].astype(out.dtype)


def chosen(home, mine, other, dtype):
    block = pl.BlockSpec((128, 2048), lambda i: (i, 0))
    return run(
        chosen_kernel,
        (2,),
        [SCALARS, block, block],
        [(shape((256, 2048), dtype), block)],
        [home, mine, other],
    )[0]


def scan_kernel(reverse, rate, parts, out):
    decay = jnp.exp(jnp.full((16, DV), -256.0 * rate[0], F32))
    state = jnp.zeros((16, DV), F32)
    for k in range(31, -1, -1) if reverse else range(32):
        out[k] = state.astype(BF)
        state = decay * state + parts[k].astype(F32)


def scan_spans(rate, parts, reverse):
    dims = (32, 16, DV)
    return run(
        functools.partial(scan_kernel, reverse),
        (1,),
        [SCALARS, whole(dims)],
        [(shape(dims, BF), whole(dims))],
        [rate, parts],
    )[0]


def pack_kernel(gains, *refs):
    out, start = refs[-1], 0
    for ref in refs[:-1]:
        out[:, start : start + ref.shape[1]] = ref[...]
        start += ref.shape[1]
        if start == 1536:
            start += 128
    wide = gains[...].astype(F32)
    same = lax.broadcasted_iota(jnp.int32, (64, 64), 0) == lax.broadcasted_iota(
        jnp.int32, (64, 64), 1
    )
    lane = lax.broadcasted_iota(jnp.int32, (64, 128), 1)
    total = jnp.zeros((64, 128), F32)
    for k in range(4):
        column = jnp.sum(jnp.where(same, wide[k : k + 1, :], 0.0), axis=1, keepdims=True)
        total = jnp.where(lane == k, column, total)
    out[:, 1536:1664] = total.astype(BF)


def pack(gains, *parts):
    cols = 128 + sum(p.shape[1] for p in parts)
    return run(
        pack_kernel,
        (1,),
        [whole((4, 64))] + [whole(p.shape) for p in parts],
        [(shape((64, cols), BF), whole((64, cols)))],
        [gains, *parts],
        limit=61,
    )[0]


def norm_kernel(place, tokens, gains_own, gains_other, normed, own, other, hat, scale, gains):
    values = tokens[...].astype(F32)
    made, spread = norm_parts(values)
    scale[...] = spread
    hat[...] = made
    mine = gains_own[...].astype(F32).T
    yours = gains_other[...].astype(F32).T
    for i in range(4):
        for ref, rows, side in ((own, mine, place[1]), (other, yours, 1 - place[1])):
            at = pl.multiple_of((2 * i + side) * 256, 256)
            rows = rows[:8, i * 256 : i * 256 + 256]
            gains[:, pl.ds(at, 256)] = rows
            out = (hat[:, pl.ds(at, 256)] * rows[0:1] + rows[1:2]).astype(BF)
            normed[:, pl.ds(at, 256)] = out
            ref[:, i * 256 : i * 256 + 256] = out


def norm_first(place, tokens, early, early_other):
    gains = pl.BlockSpec((1024, 128), lambda h: (0, 12))
    return run(
        norm_kernel,
        (1,),
        [SCALARS, whole((256, 2048)), gains, gains],
        [
            (shape((256, 2048), BF), whole((256, 2048))),
            (shape((256, 1024), BF), whole((256, 1024))),
            (shape((256, 1024), BF), whole((256, 1024))),
            (shape((256, 2048), F32), whole((256, 2048)), "hbm"),
            (shape((256, 1), F32), whole((256, 1))),
            (shape((8, 2048), F32), whole((8, 2048))),
        ],
        [place, tokens, early, early_other],
        limit=61,
    )


def roll_kernel(place, values, out):
    for k in range(4):
        at = place[0] + k
        at = pl.multiple_of(jnp.where(at >= 4, at - 4, at) * 64, 64)
        out[k * 64 : k * 64 + 64, :] = values[pl.ds(at, 64), :]


def roll_rows(place, values):
    return run(
        roll_kernel,
        (1,),
        [SCALARS, whole((256, 2048))],
        [(shape((256, 2048), BF), whole((256, 2048)))],
        [place, values],
    )[0]


def add_kernel(*refs):
    out, start = refs[-1], 0
    for own, other in zip(refs[:-1:2], refs[1:-1:2]):
        cols = own.shape[1]
        total = own[...].astype(F32) + other[...].astype(F32)
        out[:, start : start + cols] = total.astype(BF)
        start += cols


def add_halves(*pairs_of):
    operands = [a for own, other in pairs_of for a in (own, core_swap(other))]
    cols = sum(own.shape[1] for own, other in pairs_of)

    def block(n):
        return pl.BlockSpec((256, n), lambda i: (i, 0))

    return run(
        add_kernel,
        (4,),
        [block(a.shape[1]) for a in operands],
        [(shape((1024, cols), BF), block(cols))],
        operands,
    )[0]


def collected(mine, others):
    total = mine[...]
    for other in others:
        total = total + other[...].astype(F32)
    return total


ROWS = pl.BlockSpec((64, 2048), lambda h: (0, 0))


def resid_kernel(tokens, mine, one, two, three, gains, resid, hat, scale, normed):
    total = tokens[...].astype(F32) + collected(mine, (one, two, three))
    resid[...] = total
    made, spread = norm_parts(total)
    hat[...] = made
    scale[...] = spread
    normed[...] = (made * gains[2:3] + gains[3:4]).astype(BF)


def resid_norm(tokens, mine, others, gains):
    return run(
        resid_kernel,
        (1,),
        [ROWS] * 5 + [whole((8, 2048))],
        [
            (shape((64, 2048), F32), ROWS),
            (shape((64, 2048), F32), ROWS),
            (shape((64, 1), F32), whole((64, 1))),
            (shape((64, 2048), BF), ROWS),
        ],
        [tokens, mine, *others, gains],
    )


def resid_back_kernel(
    out_grad, mine, one, two, three, gains, hat, scale, d_resid, d_attn, vectors
):
    total = collected(mine, (one, two, three))
    made = out_grad[...].astype(F32) + norm_back(total * gains[2:3], hat[...], scale[...])
    d_resid[...] = made
    d_attn[...] = made.astype(BF)
    vectors[0:1] = jnp.sum(total * hat[...], axis=0, keepdims=True)
    vectors[1:2] = jnp.sum(total, axis=0, keepdims=True)


def resid_back(out_grad, mine, others, gains, hat, scale):
    return run(
        resid_back_kernel,
        (1,),
        [ROWS] * 5 + [whole((8, 2048)), ROWS, whole((64, 1))],
        [
            (shape((64, 2048), F32), ROWS),
            (shape((64, 2048), BF), ROWS),
            (shape((2, 2048), F32), whole((2, 2048))),
        ],
        [out_grad, mine, *others, gains, hat, scale],
    )


def out_kernel(resid, mine, one, two, three, out):
    out[...] = (resid[...] + collected(mine, (one, two, three))).astype(BF)


def block_rows(resid, mine, others):
    return run(
        out_kernel,
        (1,),
        [ROWS] * 5,
        [(shape((64, 2048), BF), ROWS)],
        [resid, mine, *others],
    )[0]


def tokens_kernel(d_resid, mine, one, two, three, gains, hat, scale, out):
    total = collected(mine, (one, two, three))
    made = d_resid[...] + norm_back(total * gains[0:1], hat[...], scale[...])
    out[...] = made.astype(BF)


def tokens_back(d_resid, mine, others, gains, hat, scale):
    return run(
        tokens_kernel,
        (1,),
        [ROWS] * 5 + [whole((8, 2048)), ROWS, whole((64, 1))],
        [(shape((64, 2048), BF), ROWS)],
        [d_resid, mine, *others, gains, hat, scale],
    )[0]


def kv_kernel(
    rate, place, own, other, key_own, key_other, value_own, value_other, cosine, sine, key, value, fresh
):
    qdec, kdec = decays(rate[pl.program_id(0)], place[0])
    raw = nn(own[...], key_own[...]) + nn(other[...], key_other[...])
    turn_into(key, raw, cosine[...], sine[...])
    made = (nn(own[...], value_own[...]) + nn(other[...], value_other[...])).astype(BF)
    value[...] = made
    fresh[...] = tn((kdec * key[...].astype(F32)).astype(BF), made).astype(BF)


def key_value(rate, place, own, other, early, early_other, cosine, sine):
    return run(
        kv_kernel,
        (2,),
        [
            SCALARS,
            SCALARS,
            whole((256, 1024)),
            whole((256, 1024)),
            columns(1024, 256),
            columns(1024, 256),
            columns(1024, 512, 1),
            columns(1024, 512, 1),
            whole((256, 128)),
            whole((256, 128)),
        ],
        [
            (shape((256, 512), BF), columns(256, 256)),
            (shape((256, 1024), BF), columns(256, 512)),
            (shape((512, 512), BF), pl.BlockSpec((256, 512), lambda h: (h, 0))),
        ],
        [rate, place, own, other, early, early_other, early, early_other, cosine, sine],
        limit=61,
    )


def query_kernel(
    rate, place, normed, w_query, w_gate, key, value, cosine, sine, query, gate, probs, inner
):
    raw = nn(normed[...], w_query[...])
    turn_into(query, raw, cosine[...], sine[...])
    gate[...] = nn(normed[...], w_gate[...])
    mask = span_mask(rate[pl.program_id(0)], place[0])
    made = (nt(query[...], key[...]) * mask).astype(BF)
    probs[0] = made
    inner[...] = nn(made, value[...])


def query_gate(rate, place, normed1, late, key, value, cosine, sine):
    return run(
        query_kernel,
        (2,),
        [
            SCALARS,
            SCALARS,
            whole((256, 2048)),
            columns(2048, 256, 16),
            columns(2048, 512),
            columns(256, 256),
            columns(256, 512),
            whole((256, 128)),
            whole((256, 128)),
        ],
        [
            (shape((256, 512), BF), columns(256, 256)),
            (shape((256, 1024), F32), columns(256, 512), "hbm"),
            (shape((2, 256, 256), BF), pl.BlockSpec((1, 256, 256), lambda h: (h, 0, 0))),
            (shape((256, 1024), F32), columns(256, 512)),
        ],
        [rate, place, normed1, late, late, key, value, cosine, sine],
        limit=61,
    )


def cut_rows(full, parts):
    parts[0][...] = full[:64]
    for k in range(1, 4):
        parts[k][...] = full[k * 64 : k * 64 + 64].astype(BF)


def row_parts(cols, index):
    spec = pl.BlockSpec((64, cols), index)
    return [(shape((64, 2048), F32 if k == 0 else BF), spec) for k in range(4)]


def retain_kernel(
    rate, place, query, state, inner, gate, w_out, hat, scale, mixed, mine, one, two, three, total
):
    h = pl.program_id(0)
    qdec, kdec = decays(rate[h], place[0])
    retained = inner[...] + qdec * nn(query[...], state[...])
    made, spread = norm_parts(retained)
    hat[...] = made
    scale[0] = spread
    wide = gate[...]
    made = (wide * jax.nn.sigmoid(wide) * made).astype(BF)
    mixed[...] = made
    partial = nt(made, w_out[...])

    @pl.when(h == 0)
    def first():
        total[...] = partial

    @pl.when(h == 1)
    def last():
        cut_rows(total[...] + partial, (mine, one, two, three))


def retain(rate, place, query, state, inner, gate, late):
    return run(
        retain_kernel,
        (2,),
        [
            SCALARS,
            SCALARS,
            columns(256, 256),
            pl.BlockSpec((256, 512), lambda h: (h, 0)),
            columns(256, 512),
            columns(256, 512),
            columns(2048, 512, 2),
        ],
        [
            (shape((256, 1024), F32), columns(256, 512), "hbm"),
            (shape((2, 256, 1), F32), pl.BlockSpec((1, 256, 1), lambda h: (h, 0, 0)), "hbm"),
            (shape((256, 1024), BF), columns(256, 512)),
            *row_parts(2048, lambda h: (0, 0)),
        ],
        [rate, place, query, state, inner, gate, late],
        [pltpu.VMEM((256, 2048), F32)],
        limit=61,
    )


def gathered(pieces, full):
    @pl.when(pl.program_id(0) == 0)
    def join():
        for k, piece in enumerate(pieces):
            full[k * 64 : k * 64 + 64, :] = piece[...]


def up_kernel(
    one, two, three, four, w_up, d_hidden, normed, hidden, d_up, mine, p1, p2, p3, total
):
    j = pl.program_id(0)
    gathered((one, two, three, four), normed)
    raw = nn(normed[...], w_up[...])
    root = 0.7978845608028654
    square = raw * raw
    tanh = jnp.tanh(root * raw * (1.0 + 0.044715 * square))
    half = 0.5 * (1.0 + tanh)
    hidden[...] = (raw * half).astype(BF)
    slope = half + 0.5 * raw * (1.0 - tanh * tanh) * root * (1.0 + 0.134145 * square)
    made = (slope * d_hidden[...]).astype(BF)
    d_up[...] = made
    partial = nt(made, w_up[...])

    @pl.when(j == 0)
    def first():
        total[...] = partial

    @pl.when(j == 1)
    def last():
        cut_rows(total[...] + partial, (mine, p1, p2, p3))


def up_back(pieces, late, d_hidden):
    return run(
        up_kernel,
        (2,),
        [ROWS] * 4 + [columns(2048, 512, 4), columns(256, 512)],
        [
            (shape((256, 2048), BF), whole((256, 2048))),
            (shape((256, 1024), BF), columns(256, 512)),
            (shape((256, 1024), BF), columns(256, 512)),
            *row_parts(2048, lambda h: (0, 0)),
        ],
        [*pieces, late, d_hidden],
        [pltpu.VMEM((256, 2048), F32)],
    )


def mixed_kernel(
    rate, place, one, two, three, four, w_out, gate, hat, scale, query, d_attn, d_gate, d_ret, outgoing
):
    gathered((one, two, three, four), d_attn)
    qdec, kdec = decays(rate[pl.program_id(0)], place[0])
    d_mixed = nn(d_attn[...], w_out[...])
    wide, normed = gate[...], hat[...]
    sig = jax.nn.sigmoid(wide)
    d_gate[...] = (d_mixed * normed * sig * (1.0 + wide * (1.0 - sig))).astype(BF)
    made = norm_back(d_mixed * wide * sig, normed, scale[0]).astype(BF)
    d_ret[...] = made
    outgoing[...] = tn((qdec * query[...].astype(F32)).astype(BF), made).astype(BF)


def mixed_back(rate, place, pieces, late, gate, hat, scale, query):
    return run(
        mixed_kernel,
        (2,),
        [
            SCALARS,
            SCALARS,
            *[ROWS] * 4,
            columns(2048, 512, 2),
            columns(256, 512),
            columns(256, 512),
            pl.BlockSpec((1, 256, 1), lambda h: (h, 0, 0)),
            columns(256, 256),
        ],
        [
            (shape((256, 2048), BF), whole((256, 2048))),
            (shape((256, 1024), BF), columns(256, 512)),
            (shape((256, 1024), BF), columns(256, 512)),
            (shape((512, 512), BF), pl.BlockSpec((256, 512), lambda h: (h, 0))),
        ],
        [rate, place, *pieces, late, gate, hat, scale, query],
        limit=61,
    )


def query_back_kernel(
    rate, place, d_ret, value, key, query, probs, state, cosine, sine, d_query, key_part, value_part
):
    h = pl.program_id(0)
    qdec, kdec = decays(rate[h], place[0])
    mask = span_mask(rate[h], place[0])
    d_scores = (nt(d_ret[...], value[...]) * mask).astype(BF)
    turned = nn(d_scores, key[...]) + qdec * nt(d_ret[...], state[...])
    turn_into(d_query, turned, cosine[...], -sine[...])
    key_part[...] = tn(d_scores, query[...])
    value_part[...] = tn(probs[0], d_ret[...])


def query_back(rate, place, d_ret, value, key, query, probs, state, cosine, sine):
    return run(
        query_back_kernel,
        (2,),
        [
            SCALARS,
            SCALARS,
            columns(256, 512),
            columns(256, 512),
            columns(256, 256),
            columns(256, 256),
            pl.BlockSpec((1, 256, 256), lambda h: (h, 0, 0)),
            pl.BlockSpec((256, 512), lambda h: (h, 0)),
            whole((256, 128)),
            whole((256, 128)),
        ],
        [
            (shape((256, 512), BF), columns(256, 256)),
            (shape((256, 512), F32), columns(256, 256)),
            (shape((256, 1024), F32), columns(256, 512)),
        ],
        [rate, place, d_ret, value, key, query, probs, state, cosine, sine],
    )


def key_value_back_kernel(
    rate, place, key_part, value_part, key, value, later, cosine, sine, d_both
):
    for h in range(2):
        qdec, kdec = decays(rate[h], place[0])
        keys, values = slice(h * DK, h * DK + DK), slice(h * DV, h * DV + DV)
        carried = later[keys, :]
        d_key = key_part[:, keys] + kdec * nt(value[:, values], carried)
        turn_into(d_both, d_key, cosine[...], -sine[...], h * DK)
        d_value = value_part[:, values] + kdec * nn(key[:, keys], carried)
        d_both[:, 512 + h * DV : 512 + h * DV + DV] = d_value.astype(BF)


def key_value_back(rate, place, key_part, value_part, key, value, later, cosine, sine):
    return run(
        key_value_back_kernel,
        (1,),
        [
            SCALARS,
            SCALARS,
            whole((256, 512)),
            whole((256, 1024)),
            whole((256, 512)),
            whole((256, 1024)),
            whole((512, 512)),
            whole((256, 128)),
            whole((256, 128)),
        ],
        [(shape((256, 1536), BF), whole((256, 1536)))],
        [rate, place, key_part, value_part, key, value, later, cosine, sine],
        limit=61,
    )[0]


def normed_first_kernel(d_query, d_gate, w_query, w_gate, part):
    part[...] = nt(d_query[...], w_query[...]) + nt(d_gate[...], w_gate[...])


def normed_back_first(d_query, d_gate, late):
    return run(
        normed_first_kernel,
        (4,),
        [
            whole((256, 512)),
            whole((256, 1024)),
            pl.BlockSpec((512, 512), lambda i: (i, 8)),
            pl.BlockSpec((512, 1024), lambda i: (i, 0)),
        ],
        [(shape((256, 2048), F32), columns(256, 512))],
        [d_query, d_gate, late, late],
    )[0]


def normed_back_kernel(place, first, d_both, w_own, w_other, hat, mine, one, two, three, vectors):
    left = nt(d_both[...], w_own[:, :1536])
    right = nt(d_both[...], w_other[:, :1536])
    low = place[1] == 0
    total = first[...] + jnp.concatenate(
        [jnp.where(low, left, right), jnp.where(low, right, left)], axis=1
    )
    cut_rows(total, (mine, one, two, three))
    vectors[0:1] = jnp.sum(total * hat[...], axis=0, keepdims=True)
    vectors[1:2] = jnp.sum(total, axis=0, keepdims=True)


def normed_back(place, first, d_both, early, early_other, hat):
    weights = pl.BlockSpec((256, 1664), lambda i: (i, 0))
    return run(
        normed_back_kernel,
        (4,),
        [
            SCALARS,
            columns(256, 512),
            whole((256, 1536)),
            weights,
            weights,
            columns(256, 512),
        ],
        [
            *row_parts(512, lambda i: (0, i)),
            (shape((2, 2048), F32), columns(2, 512)),
        ],
        [place, first, d_both, early, early_other, hat],
    )


def pair_kernel(left_one, right_one, left_two, right_two, out):
    w = pl.program_id(0)

    @pl.when(w == 0)
    def first():
        out[...] = tn(left_one[...], right_one[...]).astype(BF)

    @pl.when(w == 1)
    def second():
        out[...] = tn(left_two[...], right_two[...]).astype(BF)


def grad_pair(left_one, right_one, left_two, right_two):
    def left(w):
        return pl.BlockSpec((256, 512), lambda v, i: (0, jnp.where(v == w, i, 3 * (1 - w))))

    right = pl.BlockSpec((256, 1024), lambda v, i: (0, 0))
    return run(
        pair_kernel,
        (2, 4),
        [left(0), right, left(1), right],
        [(shape((2048, 2048), BF), pl.BlockSpec((512, 1024), lambda v, i: (i, v)))],
        [left_one, right_one, left_two, right_two],
        flops=4 * 256 * 2048 * 1024,
        moved=16 * 2048 * 1024,
    )[0]


def down_kernel(out_grad, w_down, d_hidden):
    d_hidden[...] = nn(out_grad[...], w_down[...])


def down_back(out_grad, late):
    return run(
        down_kernel,
        (2,),
        [whole((256, 2048)), columns(2048, 512, 6)],
        [(shape((256, 1024), F32), columns(256, 512))],
        [out_grad, late],
    )[0]


def ffn_kernel(hidden, w_down, mine, one, two, three):
    cut_rows(nt(hidden[...], w_down[...]), (mine, one, two, three))


def ffn_parts(hidden, late):
    return run(
        ffn_kernel,
        (4,),
        [whole((256, 1024)), pl.BlockSpec((512, 1024), lambda i: (i, 3))],
        row_parts(512, lambda i: (0, i)),
        [hidden, late],
    )


def store_rows(ref, made, side, start):
    i = pl.program_id(0)
    for j in range(4):
        to = jnp.where(side == 0, i * 256 + j * 64, j * 256 + i * 64)
        ref[pl.ds(pl.multiple_of(to, 64), 64), start : start + made.shape[1]] = made[
            j * 64 : j * 64 + 64
        ]


def split_kernel(place, left, *refs):
    rights, own, other = refs[:-2], refs[-2], refs[-1]
    for ref, side in ((own, place[1]), (other, 1 - place[1])):
        rows = left[:, pl.ds(pl.multiple_of(side * 256, 256), 256)]
        start = 0
        for right in rights:
            store_rows(ref, tn(rows, right[...]).astype(BF), side, start)
            start += right.shape[1]


def grad_split(place, left, rights):
    cols = sum(r.shape[1] for r in rights)
    half = (shape((1024, cols), BF), whole((1024, cols)))
    return run(
        split_kernel,
        (4,),
        [SCALARS, columns(256, 512)] + [whole(r.shape) for r in rights],
        [half, half],
        [place, left, *rights],
    )


def vector_kernel(place, vectors, own, other):
    for ref, side in ((own, place[1]), (other, 1 - place[1])):
        rows = vectors[:, pl.ds(pl.multiple_of(side * 256, 256), 256)]
        rows = jnp.concatenate([rows, jnp.zeros((120, 256), F32)], axis=0)
        store_rows(ref, rows.T.astype(BF), side, 0)


def vector_split(place, vectors):
    half = (shape((1024, 128), BF), whole((1024, 128)))
    return run(
        vector_kernel,
        (4,),
        [SCALARS, columns(8, 512)],
        [half, half],
        [place, vectors],
    )


def join_kernel(one, two, out):
    start = 0
    for ref in (one, two):
        total = ref[0].astype(F32)
        for k in range(1, 4):
            total = total + ref[k].astype(F32)
        out[:, start : start + total.shape[1]] = total.astype(BF)
        start += total.shape[1]


def join_sums(one, two):
    def block(values):
        return pl.BlockSpec((4, 64, values.shape[2]), lambda i: (0, i, 0))

    cols = one.shape[2] + two.shape[2]
    return run(
        join_kernel,
        (4,),
        [block(one), block(two)],
        [(shape((256, cols), BF), pl.BlockSpec((64, cols), lambda i: (i, 0)))],
        [one, two],
    )[0]


def last_kernel(parts, main, rest):
    total = parts[0].astype(F32)
    for k in range(1, 4):
        total = total + parts[k].astype(F32)
    cols = main.shape[1]
    main[...] = total[:, :cols].astype(BF)
    rest[...] = total[:, cols:]


def last_sum(parts):
    cols = parts.shape[2] - 128
    return run(
        last_kernel,
        (1,),
        [whole(parts.shape)],
        [(shape((64, cols), BF), whole((64, cols))), (shape((64, 128), F32), whole((64, 128)))],
        [parts],
    )


def flip_kernel(*refs):
    total = refs[0][...]
    for ref in refs[1:-1]:
        total = total + ref[...]
    refs[-1][...] = total.T[:8]


def flip_sum(*values):
    return run(
        flip_kernel,
        (1,),
        [whole((64, 128))] * len(values),
        [(shape((8, 64), F32), whole((8, 64)))],
        list(values),
    )[0]


def widen_kernel(values, *outs):
    start = 0
    for out in outs:
        out[...] = values[:, start : start + out.shape[1]].astype(F32)
        start += out.shape[1]


def widen(values, widths):
    return run(
        widen_kernel,
        (1,),
        [whole(values.shape)],
        [(shape((64, n), F32), whole((64, n))) for n in widths],
        [values],
    )


def body(
    tokens,
    norm1_gain,
    norm1_bias,
    w_query,
    w_key,
    w_value,
    w_gate,
    w_out,
    norm2_gain,
    norm2_bias,
    w_up,
    w_down,
    decay_rate,
    out_grad,
):
    x, y, c = lax.axis_index("x"), lax.axis_index("y"), lax.axis_index("c")
    zl, zh = lax.axis_index("zl"), lax.axis_index("zh")
    z = zh * 2 + zl
    home = (zh == c).astype(jnp.int32).reshape(1)
    span = x * 8 + c * 4 + y
    place = jnp.stack([z, c, x, y]).astype(jnp.int32)

    gains = jnp.stack([norm1_gain, norm1_bias, norm2_gain, norm2_bias])
    shards = swap_roles(
        pack(gains, w_key, w_value, w_gate, w_out.T, w_up, w_down.T, w_query)
    )
    first, second = shards[:, :1664], shards[:, 1664:]
    rate = swap_roles(decay_rate)
    tokens, kept = lax.optimization_barrier((tokens, shards))
    tokens = swap_roles(tokens)

    cols = first.shape[1]
    early = lax.all_to_all(
        jnp.broadcast_to(first[None], (16, 64, cols)), ("x", "y"), 0, 0, tiled=True
    ).reshape(1024, cols)
    late = lax.all_gather(second, SPANS, axis=0, tiled=True)

    tokens = roll_rows(place, tokens)
    index = ((jnp.arange(256) + z * 64) % 256).astype(F32)
    half = DK // 2
    position = (span * 256).astype(F32) + index
    freq = 10000.0 ** (-jnp.arange(half).astype(F32) / half)
    angle = position[:, None] * freq[None, :]
    cosine, sine = jnp.cos(angle), jnp.sin(angle)
    early, tokens, cosine, sine, rate = lax.optimization_barrier(
        (early, tokens, cosine, sine, rate)
    )

    early_other = core_swap(early)
    normed1, own, other, hat1, scale1, gains = norm_first(place, tokens, early, early_other)
    key, value, fresh = key_value(rate, place, own, other, early, early_other, cosine, sine)
    out_grad, fresh = lax.optimization_barrier((out_grad, fresh))
    out_grad = roll_rows(place, swap_roles(out_grad))
    scan_rate = jnp.where(x < 2, rate[0], rate[1]).reshape(1)
    carried = scan_spans(scan_rate, scan_parts(fresh), False)
    late, carried, out_grad = lax.optimization_barrier((late, carried, out_grad))
    state = scan_back(carried)
    query, gate, probs, inner = query_gate(
        rate, place, normed1, late, key, value, cosine, sine
    )
    hat, scale, mixed, mine, *parts = retain(rate, place, query, state, inner, gate, late)
    parts = z_collect(parts)
    out_grad, mine = lax.optimization_barrier((out_grad, mine))
    d_hidden = down_back(out_grad, late)
    resid, hat2, scale2, normed2 = resid_norm(tokens[:64], mine, parts, gains)
    normed2, hidden, d_up, mine, *parts = up_back(z_gather(normed2), late, d_hidden)
    parts = z_collect(parts)
    grad_wide = grad_pair(normed2, d_up, out_grad, hidden)
    mine, grad_wide = lax.optimization_barrier((mine, grad_wide))
    d_resid, d_attn, vectors2 = resid_back(out_grad[:64], mine, parts, gains, hat2, scale2)
    grad_wide = swap_roles(
        lax.psum_scatter(grad_wide, SPANS, scatter_dimension=0, tiled=True)
    )
    d_attn, d_gate, d_ret, outgoing = mixed_back(
        rate, place, z_gather(d_attn), late, gate, hat, scale, query
    )
    parts = scan_parts(outgoing)

    d_query, key_part, value_part = query_back(
        rate, place, d_ret, value, key, query, probs, state, cosine, sine
    )
    gate_halves = grad_split(place, normed1, [d_gate, d_query])
    out_halves = grad_split(place, d_attn, [mixed])
    parts, gate_halves, out_halves = lax.optimization_barrier(
        (parts, gate_halves, out_halves)
    )
    later = scan_back(scan_spans(scan_rate, parts, True))
    hidden, d_query, parts = lax.optimization_barrier((hidden, d_query, parts))
    d_first = normed_back_first(d_query, d_gate, late)
    ffn, *ffn_others = ffn_parts(hidden, late)
    early_part = add_halves(gate_halves, out_halves)
    early_part, later, ffn, d_first = lax.optimization_barrier(
        (early_part, later, ffn, d_first)
    )
    early_part = exchange(early_part, FIRST_WAY)

    d_both = key_value_back(
        rate, place, key_part, value_part, key, value, later, cosine, sine
    )
    late_halves = grad_split(place, normed1, [d_both])
    d_both, late_halves = lax.optimization_barrier((d_both, late_halves))
    mine, *parts, vectors = normed_back(place, d_first, d_both, early, early_other, hat1)
    vectors = jnp.concatenate([vectors, vectors2, jnp.zeros((4, 2048), F32)])
    parts = z_collect(parts)
    late_part = add_halves(late_halves, vector_split(place, vectors))
    late_part, early_part = lax.optimization_barrier((late_part, early_part))
    late_part = exchange(late_part, FIRST_WAY)

    tokens_grad = tokens_back(d_resid, mine, parts, gains, hat1[:64], scale1[:64])
    block_out = block_rows(resid, ffn, z_collect(ffn_others))
    tokens_grad, late_part, block_out = lax.optimization_barrier(
        (tokens_grad, late_part, block_out)
    )
    tokens_grad = z_gather_home(tokens_grad, place, home, F32)
    block_out = z_gather_home(block_out, place, home, BF)

    total = exchange(
        join_sums(early_part.reshape(4, 256, -1), late_part.reshape(4, 256, -1)), SECOND_WAY
    )
    total, vectors = last_sum(total.reshape(4, 64, -1))
    total = swap_roles(total)
    vectors = flip_sum(*[to_owner(vectors, a, b) for a in (0, 1) for b in (0, 1)])
    grad_gate, grad_query, grad_out, grad_key, grad_value = widen(
        total, [1024, 512, 1024, 512, 1024]
    )
    grad_up, grad_down = widen(grad_wide, [1024, 1024])
    return (
        block_out,
        tokens_grad,
        vectors[0],
        vectors[1],
        grad_query,
        grad_key,
        grad_value,
        grad_gate,
        grad_out.T,
        vectors[2],
        vectors[3],
        grad_up,
        grad_down.T,
    )


def solution(mesh):
    fine = Mesh(mesh.devices.reshape(2, 2, 4, 2, 4), AXES)
    seq, tp = ("x", "zh", "y"), ("zl", "c")
    rows, wide, tall, vector = P(seq, None), P(seq, tp), P(tp, seq), P(seq)
    in_specs = (
        rows,
        vector,
        vector,
        wide,
        wide,
        wide,
        wide,
        tall,
        vector,
        vector,
        wide,
        tall,
        P(tp),
        rows,
    )
    out_specs = (
        rows,
        rows,
        vector,
        vector,
        wide,
        wide,
        wide,
        wide,
        tall,
        vector,
        vector,
        wide,
        tall,
    )
    return jax.shard_map(body, mesh=fine, in_specs=in_specs, out_specs=out_specs, check_vma=False)
```

```python
import functools
import itertools

import jax
import jax.numpy as jnp
from jax import lax
from jax.experimental import pallas as pl
from jax.experimental.pallas import tpu as pltpu
from jax.sharding import Mesh, PartitionSpec as P

DK = 256
DV = 512
AXES = ("zl", "c", "x", "zh", "y")
SIZES = {"zl": 2, "c": 2, "x": 4, "zh": 2, "y": 4}
SPANS = ("x", "c", "y")
CHIPS = ("c", "x", "y")
ALONG_X = [[x * 4 + y for x in range(4)] for y in range(4)]
ALONG_Y = [[x * 4 + y for y in range(4)] for x in range(4)]


def other_core(groups):
    return [[16 + i for i in group] for group in groups]


FIRST_WAY = ALONG_X + other_core(ALONG_Y)
SECOND_WAY = ALONG_Y + other_core(ALONG_X)
BF = jnp.bfloat16
F32 = jnp.float32


def pairs(axes, move):
    def flat(place):
        at = 0
        for axis in axes:
            at = at * SIZES[axis] + place[axis]
        return at

    found = []
    for values in itertools.product(*[range(SIZES[axis]) for axis in axes]):
        place = dict(zip(axes, values))
        target = move(dict(place))
        if target is not None:
            found.append((flat(place), flat(target)))
    return found


def swap_roles(values):
    return lax.ppermute(
        values, ("c", "zh"), pairs(("c", "zh"), lambda p: {"c": p["zh"], "zh": p["c"]})
    )


def z_shift(values, shift):
    def move(place):
        z = (place["zh"] * 2 + place["zl"] + shift) % 4
        return {"zl": z % 2, "zh": z // 2}

    return lax.ppermute(values, ("zl", "zh"), pairs(("zl", "zh"), move))


def z_shift_home(values, shift):
    def move(place):
        z = (place["zh"] * 2 + place["zl"] + shift) % 4
        if z // 2 != place["c"]:
            return None
        return {"zl": z % 2, "zh": z // 2, "c": place["c"]}

    return lax.ppermute(values, ("zl", "c", "zh"), pairs(("zl", "c", "zh"), move))


def core_from_home(values):
    def move(place):
        if place["zh"] != place["c"]:
            return None
        return {"c": 1 - place["c"], "zh": place["zh"]}

    return lax.ppermute(values, ("c", "zh"), pairs(("c", "zh"), move))


def core_swap(values):
    return lax.ppermute(values, "c", [(0, 1), (1, 0)])


def z_collect(parts):
    return [z_shift(parts[shift - 1], shift) for shift in (1, 3, 2)]


def z_gather(values):
    return [values, z_shift(values, 3), z_shift(values, 2), z_shift(values, 1)]


def z_gather_home(values, place, home):
    near, far, across = z_shift_home(values, 3), z_shift_home(values, 1), z_shift_home(values, 2)
    full = in_place(place, values, near, across, far)
    return chosen(home, full, core_from_home(full))


def nn(left, right):
    return jnp.dot(left, right, preferred_element_type=F32)


def nt(left, right):
    return lax.dot_general(left, right, (((1,), (1,)), ((), ())), preferred_element_type=F32)


def tn(left, right):
    return lax.dot_general(left, right, (((0,), (0,)), ((), ())), preferred_element_type=F32)


def norm_parts(values):
    center = values - jnp.mean(values, axis=-1, keepdims=True)
    spread = jnp.mean(center * center, axis=-1, keepdims=True)
    scale = lax.rsqrt(spread + 1e-05)
    return center * scale, scale


def norm_back(grad, hat, scale):
    mean_grad = jnp.mean(grad, axis=-1, keepdims=True)
    mean_both = jnp.mean(grad * hat, axis=-1, keepdims=True)
    return (grad - mean_grad - hat * mean_both) * scale


def scan_parts(fresh):
    return lax.all_to_all(fresh.reshape(32, 16, DV), SPANS, 0, 0, tiled=True)


def scan_back(carried):
    return lax.all_to_all(carried, SPANS, 0, 0, tiled=True).reshape(2 * DK, DV)


def exchange(values, groups):
    return lax.all_to_all(values, CHIPS, 0, 0, axis_index_groups=groups, tiled=True)


def run(kernel, grid, ins, outs, operands, scratch=(), limit=48, flops=1, moved=1):
    return pl.pallas_call(
        kernel,
        grid=grid,
        in_specs=ins,
        out_specs=[o[1] for o in outs],
        out_shape=[pltpu.HBM(o[0].shape, o[0].dtype) if len(o) > 2 else o[0] for o in outs],
        scratch_shapes=list(scratch),
        compiler_params=pltpu.CompilerParams(vmem_limit_bytes=limit * 1024 * 1024),
        cost_estimate=pl.CostEstimate(flops=flops, bytes_accessed=moved, transcendentals=0),
    )(*operands)


def shape(dims, dtype):
    return jax.ShapeDtypeStruct(dims, dtype)


def columns(rows, cols, first=0):
    return pl.BlockSpec((rows, cols), lambda h: (0, first + h))


def whole(dims):
    return pl.BlockSpec(dims, lambda h: (0,) * len(dims))


SCALARS = pl.BlockSpec(memory_space=pltpu.SMEM)


def places(dims, axis, z):
    at = lax.broadcasted_iota(jnp.int32, dims, axis) + z * 64
    return jnp.where(at >= 256, at - 256, at).astype(F32)


def decays(rate, z):
    at = places((256, 1), 0, z)
    return jnp.exp(-rate * (at + 1.0)), jnp.exp(-rate * (255.0 - at))


def span_mask(rate, z):
    offset = places((256, 256), 0, z) - places((256, 256), 1, z)
    return jnp.where(offset >= 0.0, jnp.exp(-rate * jnp.maximum(offset, 0.0)), 0.0)


def turn_into(ref, values, cosine, sine, start=0):
    half = DK // 2
    a, b = values[:, :half], values[:, half:]
    ref[:, start : start + half] = (a * cosine - b * sine).astype(ref.dtype)
    ref[:, start + half : start + DK] = (b * cosine + a * sine).astype(ref.dtype)


def in_place_kernel(place, *refs):
    out = refs[-1]
    for k in range(4):
        at = place[0] + k
        at = pl.multiple_of(jnp.where(at >= 4, at - 4, at) * 64, 64)
        out[pl.ds(at, 64), :] = refs[k][...]


def in_place(place, *pieces):
    return run(
        in_place_kernel,
        (1,),
        [SCALARS] + [whole((64, 4096))] * 4,
        [(shape((256, 4096), BF), whole((256, 4096)))],
        [place, *pieces],
    )[0]


def chosen_kernel(home, mine, other, block_out, tokens_grad):
    for flag, ref in ((1, mine), (0, other)):

        @pl.when(home[0] == flag)
        def take(ref=ref):
            block_out[...] = ref[:, :2048]
            tokens_grad[...] = ref[:, 2048:].astype(F32)


def chosen(home, mine, other):
    def block(cols):
        return pl.BlockSpec((64, cols), lambda i: (i, 0))

    return run(
        chosen_kernel,
        (4,),
        [SCALARS, block(4096), block(4096)],
        [(shape((256, 2048), BF), block(2048)), (shape((256, 2048), F32), block(2048))],
        [home, mine, other],
        limit=61,
    )


def scan_kernel(reverse, rate, parts, out):
    decay = jnp.exp(jnp.full((16, DV), -256.0 * rate[0], F32))
    state = jnp.zeros((16, DV), F32)
    for k in range(31, -1, -1) if reverse else range(32):
        out[k] = state.astype(BF)
        state = decay * state + parts[k].astype(F32)


def scan_spans(rate, parts, reverse):
    dims = (32, 16, DV)
    return run(
        functools.partial(scan_kernel, reverse),
        (1,),
        [SCALARS, whole(dims)],
        [(shape(dims, BF), whole(dims))],
        [rate, parts],
    )[0]


def pack_kernel(gains, *refs):
    out, start = refs[-1], 0
    for ref in refs[:-1]:
        out[:, start : start + ref.shape[1]] = ref[...]
        start += ref.shape[1]
        if start == 1536:
            start += 128
    wide = gains[...].astype(F32)
    same = lax.broadcasted_iota(jnp.int32, (64, 64), 0) == lax.broadcasted_iota(
        jnp.int32, (64, 64), 1
    )
    lane = lax.broadcasted_iota(jnp.int32, (64, 128), 1)
    total = jnp.zeros((64, 128), F32)
    for k in range(4):
        column = jnp.sum(jnp.where(same, wide[k : k + 1, :], 0.0), axis=1, keepdims=True)
        total = jnp.where(lane == k, column, total)
    out[:, 1536:1664] = total.astype(BF)


def pack(gains, *parts):
    cols = 128 + sum(p.shape[1] for p in parts)
    return run(
        pack_kernel,
        (1,),
        [whole((4, 64))] + [whole(p.shape) for p in parts],
        [(shape((64, cols), BF), whole((64, cols)))],
        [gains, *parts],
        limit=61,
    )[0]


def norm_kernel(tokens, hat, scale):
    made, spread = norm_parts(tokens[...].astype(F32))
    hat[...] = made
    scale[...] = spread


def norm_tokens(tokens):
    block = pl.BlockSpec((64, 2048), lambda i: (i, 0))
    return run(
        norm_kernel,
        (4,),
        [block],
        [
            (shape((256, 2048), F32), block, "hbm"),
            (shape((256, 1), F32), pl.BlockSpec((64, 1), lambda i: (i, 0)), "hbm"),
        ],
        [tokens],
        limit=61,
    )


def roll_kernel(place, values, out):
    for k in range(4):
        at = place[0] + k
        at = pl.multiple_of(jnp.where(at >= 4, at - 4, at) * 64, 64)
        out[k * 64 : k * 64 + 64, :] = values[pl.ds(at, 64), :]


def roll_rows(place, values):
    return run(
        roll_kernel,
        (1,),
        [SCALARS, whole((256, 2048))],
        [(shape((256, 2048), BF), whole((256, 2048)))],
        [place, values],
    )[0]


def add_kernel(*refs):
    out, start = refs[-1], 0
    for own, other in zip(refs[:-1:2], refs[1:-1:2]):
        cols = own.shape[1]
        total = own[...].astype(F32) + other[...].astype(F32)
        out[:, start : start + cols] = total.astype(BF)
        start += cols


def add_halves(*pairs_of):
    operands = [a for own, other in pairs_of for a in (own, core_swap(other))]
    cols = sum(own.shape[1] for own, other in pairs_of)

    def block(n):
        return pl.BlockSpec((256, n), lambda i: (i, 0))

    return run(
        add_kernel,
        (4,),
        [block(a.shape[1]) for a in operands],
        [(shape((1024, cols), BF), block(cols))],
        operands,
    )[0]


def collected(mine, others):
    total = mine[...]
    for other in others:
        total = total + other[...].astype(F32)
    return total


ROWS = pl.BlockSpec((64, 2048), lambda h: (0, 0))


def resid_kernel(tokens, mine, one, two, three, gains, resid, hat, scale, normed):
    total = tokens[...].astype(F32) + collected(mine, (one, two, three))
    resid[...] = total
    made, spread = norm_parts(total)
    hat[...] = made
    scale[...] = spread
    normed[...] = (made * gains[2:3] + gains[3:4]).astype(BF)


def resid_norm(tokens, mine, others, gains):
    return run(
        resid_kernel,
        (1,),
        [ROWS] * 5 + [whole((8, 2048))],
        [
            (shape((64, 2048), F32), ROWS),
            (shape((64, 2048), F32), ROWS),
            (shape((64, 1), F32), whole((64, 1))),
            (shape((64, 2048), BF), ROWS),
        ],
        [tokens, mine, *others, gains],
    )


def resid_back_kernel(
    out_grad, mine, one, two, three, gains, hat, scale, d_resid, d_attn, vectors
):
    total = collected(mine, (one, two, three))
    made = out_grad[...].astype(F32) + norm_back(total * gains[2:3], hat[...], scale[...])
    d_resid[...] = made
    d_attn[...] = made.astype(BF)
    vectors[0:1] = jnp.sum(total * hat[...], axis=0, keepdims=True)
    vectors[1:2] = jnp.sum(total, axis=0, keepdims=True)


def resid_back(out_grad, mine, others, gains, hat, scale):
    return run(
        resid_back_kernel,
        (1,),
        [ROWS] * 5 + [whole((8, 2048)), ROWS, whole((64, 1))],
        [
            (shape((64, 2048), F32), ROWS),
            (shape((64, 2048), BF), ROWS),
            (shape((2, 2048), F32), whole((2, 2048))),
        ],
        [out_grad, mine, *others, gains, hat, scale],
    )


def rows_kernel(resid, f0, f1, f2, f3, d_resid, d0, d1, d2, d3, gains, hat, scale, out):
    out[:, :2048] = (resid[...] + collected(f0, (f1, f2, f3))).astype(BF)
    total = collected(d0, (d1, d2, d3))
    made = d_resid[...] + norm_back(total * gains[0:1], hat[...], scale[...])
    out[:, 2048:] = made.astype(BF)


def final_rows(resid, ffn, ffn_others, d_resid, mine, others, gains, hat, scale):
    return run(
        rows_kernel,
        (1,),
        [ROWS] * 10 + [whole((8, 2048)), ROWS, pl.BlockSpec((64, 1), lambda h: (0, 0))],
        [(shape((64, 4096), BF), whole((64, 4096)))],
        [resid, ffn, *ffn_others, d_resid, mine, *others, gains, hat, scale],
        limit=61,
    )[0]


def kv_kernel(
    rate,
    place,
    hat,
    gains_own,
    gains_other,
    key_own,
    key_other,
    value_own,
    value_other,
    cosine,
    sine,
    key,
    value,
    fresh,
    normed,
    gains,
    own,
    other,
):
    @pl.when(pl.program_id(0) == 0)
    def norm():
        mine = gains_own[...].astype(F32).T
        yours = gains_other[...].astype(F32).T
        for i in range(4):
            for ref, rows, side in ((own, mine, place[1]), (other, yours, 1 - place[1])):
                at = pl.multiple_of((2 * i + side) * 256, 256)
                rows = rows[:8, i * 256 : i * 256 + 256]
                gains[:, pl.ds(at, 256)] = rows
                out = (hat[:, pl.ds(at, 256)] * rows[0:1] + rows[1:2]).astype(BF)
                normed[:, pl.ds(at, 256)] = out
                ref[:, i * 256 : i * 256 + 256] = out

    qdec, kdec = decays(rate[pl.program_id(0)], place[0])
    raw = nn(own[...], key_own[...]) + nn(other[...], key_other[...])
    turn_into(key, raw, cosine[...], sine[...])
    made = (nn(own[...], value_own[...]) + nn(other[...], value_other[...])).astype(BF)
    value[...] = made
    fresh[...] = tn((kdec * key[...].astype(F32)).astype(BF), made).astype(BF)


def key_value(rate, place, hat, early, early_other, cosine, sine):
    gains = pl.BlockSpec((1024, 128), lambda h: (0, 12))
    return run(
        kv_kernel,
        (2,),
        [
            SCALARS,
            SCALARS,
            whole((256, 2048)),
            gains,
            gains,
            columns(1024, 256),
            columns(1024, 256),
            columns(1024, 512, 1),
            columns(1024, 512, 1),
            whole((256, 128)),
            whole((256, 128)),
        ],
        [
            (shape((256, 512), BF), columns(256, 256)),
            (shape((256, 1024), BF), columns(256, 512)),
            (shape((512, 512), BF), pl.BlockSpec((256, 512), lambda h: (h, 0))),
            (shape((256, 2048), BF), whole((256, 2048))),
            (shape((8, 2048), F32), whole((8, 2048))),
        ],
        [
            rate,
            place,
            hat,
            early,
            early_other,
            early,
            early_other,
            early,
            early_other,
            cosine,
            sine,
        ],
        [pltpu.VMEM((256, 1024), BF), pltpu.VMEM((256, 1024), BF)],
        limit=61,
    )


def query_kernel(
    rate, place, normed, w_query, w_gate, key, value, cosine, sine, query, gate, probs, inner
):
    raw = nn(normed[...], w_query[...])
    turn_into(query, raw, cosine[...], sine[...])
    gate[...] = nn(normed[...], w_gate[...])
    mask = span_mask(rate[pl.program_id(0)], place[0])
    made = (nt(query[...], key[...]) * mask).astype(BF)
    probs[0] = made
    inner[...] = nn(made, value[...])


def query_gate(rate, place, normed1, late, key, value, cosine, sine):
    return run(
        query_kernel,
        (2,),
        [
            SCALARS,
            SCALARS,
            whole((256, 2048)),
            columns(2048, 256, 12),
            columns(2048, 512),
            columns(256, 256),
            columns(256, 512),
            whole((256, 128)),
            whole((256, 128)),
        ],
        [
            (shape((256, 512), BF), columns(256, 256)),
            (shape((256, 1024), F32), columns(256, 512), "hbm"),
            (shape((2, 256, 256), BF), pl.BlockSpec((1, 256, 256), lambda h: (h, 0, 0))),
            (shape((256, 1024), F32), columns(256, 512)),
        ],
        [rate, place, normed1, late, late, key, value, cosine, sine],
        limit=61,
    )


def cut_rows(full, parts):
    parts[0][...] = full[:64]
    for k in range(1, 4):
        parts[k][...] = full[k * 64 : k * 64 + 64].astype(BF)


def row_parts(cols, index):
    spec = pl.BlockSpec((64, cols), index)
    return [(shape((64, 2048), F32 if k == 0 else BF), spec) for k in range(4)]


def retain_kernel(
    rate, place, query, state, inner, gate, w_out, hat, scale, mixed, mine, one, two, three, total
):
    h = pl.program_id(0)
    qdec, kdec = decays(rate[h], place[0])
    retained = inner[...] + qdec * nn(query[...], state[...])
    made, spread = norm_parts(retained)
    hat[...] = made
    scale[0] = spread
    wide = gate[...]
    made = (wide * jax.nn.sigmoid(wide) * made).astype(BF)
    mixed[...] = made
    partial = nt(made, w_out[...])

    @pl.when(h == 0)
    def first():
        total[...] = partial

    @pl.when(h == 1)
    def last():
        cut_rows(total[...] + partial, (mine, one, two, three))


def retain(rate, place, query, state, inner, gate, late):
    return run(
        retain_kernel,
        (2,),
        [
            SCALARS,
            SCALARS,
            columns(256, 256),
            pl.BlockSpec((256, 512), lambda h: (h, 0)),
            columns(256, 512),
            columns(256, 512),
            columns(2048, 512, 2),
        ],
        [
            (shape((256, 1024), F32), columns(256, 512), "hbm"),
            (shape((2, 256, 1), F32), pl.BlockSpec((1, 256, 1), lambda h: (h, 0, 0)), "hbm"),
            (shape((256, 1024), BF), columns(256, 512)),
            *row_parts(2048, lambda h: (0, 0)),
        ],
        [rate, place, query, state, inner, gate, late],
        [pltpu.VMEM((256, 2048), F32)],
        limit=61,
    )


def gathered(pieces, full):
    @pl.when(pl.program_id(0) == 0)
    def join():
        for k, piece in enumerate(pieces):
            full[k * 64 : k * 64 + 64, :] = piece[...]


def up_kernel(
    one, two, three, four, w_up, d_hidden, normed, hidden, d_up, mine, p1, p2, p3, total
):
    j = pl.program_id(0)
    gathered((one, two, three, four), normed)
    raw = nn(normed[...], w_up[...])
    root = 0.7978845608028654
    square = raw * raw
    tanh = jnp.tanh(root * raw * (1.0 + 0.044715 * square))
    half = 0.5 * (1.0 + tanh)
    hidden[...] = (raw * half).astype(BF)
    slope = half + 0.5 * raw * (1.0 - tanh * tanh) * root * (1.0 + 0.134145 * square)
    made = (slope * d_hidden[...]).astype(BF)
    d_up[...] = made
    partial = nt(made, w_up[...])

    @pl.when(j == 0)
    def first():
        total[...] = partial

    @pl.when(j == 1)
    def last():
        cut_rows(total[...] + partial, (mine, p1, p2, p3))


def up_back(pieces, late, d_hidden):
    return run(
        up_kernel,
        (2,),
        [ROWS] * 4 + [columns(2048, 512, 4), columns(256, 512)],
        [
            (shape((256, 2048), BF), whole((256, 2048))),
            (shape((256, 1024), BF), columns(256, 512)),
            (shape((256, 1024), BF), columns(256, 512)),
            *row_parts(2048, lambda h: (0, 0)),
        ],
        [*pieces, late, d_hidden],
        [pltpu.VMEM((256, 2048), F32)],
    )


def mixed_kernel(
    rate, place, one, two, three, four, w_out, gate, hat, scale, query, d_attn, d_gate, d_ret, outgoing
):
    gathered((one, two, three, four), d_attn)
    qdec, kdec = decays(rate[pl.program_id(0)], place[0])
    d_mixed = nn(d_attn[...], w_out[...])
    wide, normed = gate[...], hat[...]
    sig = jax.nn.sigmoid(wide)
    d_gate[...] = (d_mixed * normed * sig * (1.0 + wide * (1.0 - sig))).astype(BF)
    made = norm_back(d_mixed * wide * sig, normed, scale[0]).astype(BF)
    d_ret[...] = made
    outgoing[...] = tn((qdec * query[...].astype(F32)).astype(BF), made).astype(BF)


def mixed_back(rate, place, pieces, late, gate, hat, scale, query):
    return run(
        mixed_kernel,
        (2,),
        [
            SCALARS,
            SCALARS,
            *[ROWS] * 4,
            columns(2048, 512, 2),
            columns(256, 512),
            columns(256, 512),
            pl.BlockSpec((1, 256, 1), lambda h: (h, 0, 0)),
            columns(256, 256),
        ],
        [
            (shape((256, 2048), BF), whole((256, 2048))),
            (shape((256, 1024), BF), columns(256, 512)),
            (shape((256, 1024), BF), columns(256, 512)),
            (shape((512, 512), BF), pl.BlockSpec((256, 512), lambda h: (h, 0))),
        ],
        [rate, place, *pieces, late, gate, hat, scale, query],
        limit=61,
    )


def query_back_kernel(
    rate, place, d_ret, value, key, query, probs, state, cosine, sine, d_query, key_part, value_part
):
    h = pl.program_id(0)
    qdec, kdec = decays(rate[h], place[0])
    mask = span_mask(rate[h], place[0])
    d_scores = (nt(d_ret[...], value[...]) * mask).astype(BF)
    turned = nn(d_scores, key[...]) + qdec * nt(d_ret[...], state[...])
    turn_into(d_query, turned, cosine[...], -sine[...])
    key_part[...] = tn(d_scores, query[...])
    value_part[...] = tn(probs[0], d_ret[...])


def query_back(rate, place, d_ret, value, key, query, probs, state, cosine, sine):
    return run(
        query_back_kernel,
        (2,),
        [
            SCALARS,
            SCALARS,
            columns(256, 512),
            columns(256, 512),
            columns(256, 256),
            columns(256, 256),
            pl.BlockSpec((1, 256, 256), lambda h: (h, 0, 0)),
            pl.BlockSpec((256, 512), lambda h: (h, 0)),
            whole((256, 128)),
            whole((256, 128)),
        ],
        [
            (shape((256, 512), BF), columns(256, 256)),
            (shape((256, 512), F32), columns(256, 256)),
            (shape((256, 1024), F32), columns(256, 512)),
        ],
        [rate, place, d_ret, value, key, query, probs, state, cosine, sine],
        limit=61,
    )


def key_value_back_kernel(
    rate, place, key_part, value_part, key, value, later, cosine, sine, d_both
):
    for h in range(2):
        qdec, kdec = decays(rate[h], place[0])
        keys, values = slice(h * DK, h * DK + DK), slice(h * DV, h * DV + DV)
        carried = later[keys, :]
        d_key = key_part[:, keys] + kdec * nt(value[:, values], carried)
        turn_into(d_both, d_key, cosine[...], -sine[...], h * DK)
        d_value = value_part[:, values] + kdec * nn(key[:, keys], carried)
        d_both[:, 512 + h * DV : 512 + h * DV + DV] = d_value.astype(BF)


def key_value_back(rate, place, key_part, value_part, key, value, later, cosine, sine):
    return run(
        key_value_back_kernel,
        (1,),
        [
            SCALARS,
            SCALARS,
            whole((256, 512)),
            whole((256, 1024)),
            whole((256, 512)),
            whole((256, 1024)),
            whole((512, 512)),
            whole((256, 128)),
            whole((256, 128)),
        ],
        [(shape((256, 1536), BF), whole((256, 1536)))],
        [rate, place, key_part, value_part, key, value, later, cosine, sine],
        limit=61,
    )[0]


def normed_first_kernel(d_query, d_gate, w_query, w_gate, part):
    part[...] = nt(d_query[...], w_query[...]) + nt(d_gate[...], w_gate[...])


def normed_back_first(d_query, d_gate, late):
    return run(
        normed_first_kernel,
        (4,),
        [
            whole((256, 512)),
            whole((256, 1024)),
            pl.BlockSpec((512, 512), lambda i: (i, 6)),
            pl.BlockSpec((512, 1024), lambda i: (i, 0)),
        ],
        [(shape((256, 2048), F32), columns(256, 512))],
        [d_query, d_gate, late, late],
    )[0]


def normed_back_kernel(place, first, d_both, w_own, w_other, hat, mine, one, two, three, vectors):
    left = nt(d_both[...], w_own[:, :1536])
    right = nt(d_both[...], w_other[:, :1536])
    low = place[1] == 0
    total = first[...] + jnp.concatenate(
        [jnp.where(low, left, right), jnp.where(low, right, left)], axis=1
    )
    cut_rows(total, (mine, one, two, three))
    vectors[0:1] = jnp.sum(total * hat[...], axis=0, keepdims=True)
    vectors[1:2] = jnp.sum(total, axis=0, keepdims=True)


def normed_back(place, first, d_both, early, early_other, hat):
    weights = pl.BlockSpec((256, 1664), lambda i: (i, 0))
    return run(
        normed_back_kernel,
        (4,),
        [
            SCALARS,
            columns(256, 512),
            whole((256, 1536)),
            weights,
            weights,
            columns(256, 512),
        ],
        [
            *row_parts(512, lambda i: (0, i)),
            (shape((2, 2048), F32), columns(2, 512)),
        ],
        [place, first, d_both, early, early_other, hat],
    )


def pair_kernel(left_one, right_one, left_two, right_two, out):
    w = pl.program_id(0)

    @pl.when(w == 0)
    def first():
        out[...] = tn(left_one[...], right_one[...]).astype(BF)

    @pl.when(w == 1)
    def second():
        out[...] = tn(left_two[...], right_two[...]).astype(BF)


def grad_pair(left_one, right_one, left_two, right_two):
    def left(w):
        return pl.BlockSpec((256, 512), lambda v, i: (0, jnp.where(v == w, i, 3 * (1 - w))))

    right = pl.BlockSpec((256, 1024), lambda v, i: (0, 0))
    return run(
        pair_kernel,
        (2, 4),
        [left(0), right, left(1), right],
        [(shape((2048, 2048), BF), pl.BlockSpec((512, 1024), lambda v, i: (i, v)))],
        [left_one, right_one, left_two, right_two],
        flops=4 * 256 * 2048 * 1024,
        moved=16 * 2048 * 1024,
    )[0]


def down_kernel(place, out_grad, w_own, w_other, d_hidden):
    total = jnp.zeros(d_hidden.shape, F32)
    for w, side in ((w_own, place[1]), (w_other, 1 - place[1])):
        for i in range(4):
            at = pl.multiple_of((2 * i + side) * 256, 256)
            total = total + nn(out_grad[:, pl.ds(at, 256)], w[i * 256 : i * 256 + 256, :])
    d_hidden[...] = total


def down_back(place, out_grad, w_own, w_other):
    return run(
        down_kernel,
        (2,),
        [SCALARS, whole((256, 2048)), columns(1024, 512), columns(1024, 512)],
        [(shape((256, 1024), F32), columns(256, 512))],
        [place, out_grad, w_own, w_other],
    )[0]


def ffn_kernel(place, hidden, w_own, w_other, mine, one, two, three):
    left, right = nt(hidden[...], w_own[...]), nt(hidden[...], w_other[...])
    low = place[1] == 0
    total = jnp.concatenate([jnp.where(low, left, right), jnp.where(low, right, left)], axis=1)
    cut_rows(total, (mine, one, two, three))


def ffn_parts(place, hidden, w_own, w_other):
    weights = pl.BlockSpec((256, 1024), lambda i: (i, 0))
    return run(
        ffn_kernel,
        (4,),
        [SCALARS, whole((256, 1024)), weights, weights],
        row_parts(512, lambda i: (0, i)),
        [place, hidden, w_own, w_other],
    )


def store_rows(ref, made, side, start):
    i = pl.program_id(0)
    for j in range(4):
        to = jnp.where(side == 0, i * 256 + j * 64, j * 256 + i * 64)
        ref[pl.ds(pl.multiple_of(to, 64), 64), start : start + made.shape[1]] = made[
            j * 64 : j * 64 + 64
        ]


def split_kernel(place, left, *refs):
    rights, own, other = refs[:-2], refs[-2], refs[-1]
    for ref, side in ((own, place[1]), (other, 1 - place[1])):
        rows = left[:, pl.ds(pl.multiple_of(side * 256, 256), 256)]
        start = 0
        for right in rights:
            store_rows(ref, tn(rows, right[...]).astype(BF), side, start)
            start += right.shape[1]


def grad_split(place, left, rights):
    cols = sum(r.shape[1] for r in rights)
    half = (shape((1024, cols), BF), whole((1024, cols)))
    return run(
        split_kernel,
        (4,),
        [SCALARS, columns(256, 512)] + [whole(r.shape) for r in rights],
        [half, half],
        [place, left, *rights],
        limit=61,
    )


def vector_kernel(place, one, two, three, four, own, other):
    total = one[...] + two[...] + three[...] + four[...]
    for ref, side in ((own, 0), (other, 1)):
        rows = jnp.where(place[1] == side, total[:, :256], total[:, 256:])
        rows = jnp.concatenate([rows, jnp.zeros((120, 256), F32)], axis=0)
        store_rows(ref, rows.T.astype(BF), place[1] if side == 0 else 1 - place[1], 0)


def vector_split(place, *vectors):
    half = (shape((1024, 128), BF), whole((1024, 128)))
    return run(
        vector_kernel,
        (4,),
        [SCALARS] + [columns(8, 512)] * 4,
        [half, half],
        [place, *vectors],
    )


def join_kernel(one, two, out):
    start = 0
    for ref in (one, two):
        total = ref[0].astype(F32)
        for k in range(1, 4):
            total = total + ref[k].astype(F32)
        out[:, start : start + total.shape[1]] = total.astype(BF)
        start += total.shape[1]


def join_sums(one, two):
    def block(values):
        return pl.BlockSpec((4, 64, values.shape[2]), lambda i: (0, i, 0))

    cols = one.shape[2] + two.shape[2]
    return run(
        join_kernel,
        (4,),
        [block(one), block(two)],
        [(shape((256, cols), BF), pl.BlockSpec((64, cols), lambda i: (i, 0)))],
        [one, two],
    )[0]


def last_kernel(parts, out):
    total = parts[0].astype(F32)
    for k in range(1, 4):
        total = total + parts[k].astype(F32)
    out[...] = total.astype(BF)


def last_sum(parts):
    dims = parts.shape[1:]
    return run(
        last_kernel,
        (1,),
        [whole(parts.shape)],
        [(shape(dims, BF), whole(dims))],
        [parts],
    )[0]


def widen_kernel(values, *outs):
    start = 0
    for out in outs:
        if out.shape[0] == 64:
            out[...] = values[:, start : start + out.shape[1]].astype(F32)
            start += out.shape[1]
        else:
            out[...] = values[:, start : start + 128].astype(F32).T[:8]


def widen(values, widths, vectors=False):
    outs = [(shape((64, n), F32), whole((64, n))) for n in widths]
    if vectors:
        outs.append((shape((8, 64), F32), whole((8, 64))))
    return run(widen_kernel, (1,), [whole(values.shape)], outs, [values])


def body(
    tokens,
    norm1_gain,
    norm1_bias,
    w_query,
    w_key,
    w_value,
    w_gate,
    w_out,
    norm2_gain,
    norm2_bias,
    w_up,
    w_down,
    decay_rate,
    out_grad,
):
    x, y, c = lax.axis_index("x"), lax.axis_index("y"), lax.axis_index("c")
    zl, zh = lax.axis_index("zl"), lax.axis_index("zh")
    z = zh * 2 + zl
    home = (zh == c).astype(jnp.int32).reshape(1)
    span = x * 8 + c * 4 + y
    place = jnp.stack([z, c, x, y]).astype(jnp.int32)

    gains = jnp.stack([norm1_gain, norm1_bias, norm2_gain, norm2_bias])
    shards = swap_roles(
        pack(gains, w_key, w_value, w_gate, w_out.T, w_up, w_query)
    )
    first, second = shards[:, :1664], shards[:, 1664:]
    rate = swap_roles(decay_rate)
    tokens, kept = lax.optimization_barrier((tokens, shards))
    tokens = swap_roles(tokens)
    third, kept = lax.optimization_barrier((w_down.T, tokens))
    third = jnp.broadcast_to(swap_roles(third)[None], (16, 64, 1024))
    out_grad, kept = lax.optimization_barrier((out_grad, tokens))
    out_grad = swap_roles(out_grad)

    cols = first.shape[1]
    early = lax.all_to_all(
        jnp.broadcast_to(first[None], (16, 64, cols)), ("x", "y"), 0, 0, tiled=True
    ).reshape(1024, cols)
    late = lax.all_gather(second, SPANS, axis=0, tiled=True)

    tokens = roll_rows(place, tokens)
    hat1, scale1 = norm_tokens(tokens)
    out_grad = roll_rows(place, out_grad)
    index = ((jnp.arange(256) + z * 64) % 256).astype(F32)
    half = DK // 2
    position = (span * 256).astype(F32) + index
    freq = 10000.0 ** (-jnp.arange(half).astype(F32) / half)
    angle = position[:, None] * freq[None, :]
    cosine, sine = jnp.cos(angle), jnp.sin(angle)
    early, tokens, hat1, out_grad, third, cosine, sine, rate = lax.optimization_barrier(
        (early, tokens, hat1, out_grad, third, cosine, sine, rate)
    )

    early_other = core_swap(early)
    key, value, fresh, normed1, gains = key_value(
        rate, place, hat1, early, early_other, cosine, sine
    )
    scan_rate = jnp.where(x < 2, rate[0], rate[1]).reshape(1)
    carried = scan_spans(scan_rate, scan_parts(fresh), False)
    state = scan_back(carried)
    query, gate, probs, inner = query_gate(
        rate, place, normed1, late, key, value, cosine, sine
    )
    third, state, query = lax.optimization_barrier((third, state, query))
    down = lax.all_to_all(third, ("x", "y"), 0, 0, tiled=True).reshape(1024, 1024)
    hat, scale, mixed, mine, *parts = retain(rate, place, query, state, inner, gate, late)
    parts = z_collect(parts)
    resid, hat2, scale2, normed2 = resid_norm(tokens[:64], mine, parts, gains)
    down, kept = lax.optimization_barrier((down, normed2))
    down_other = core_swap(down)
    d_hidden = down_back(place, out_grad, down, down_other)
    normed2, hidden, d_up, mine, *parts = up_back(z_gather(normed2), late, d_hidden)
    parts = z_collect(parts)
    grad_wide = grad_pair(normed2, d_up, out_grad, hidden)
    mine, parts, grad_wide = lax.optimization_barrier((mine, parts, grad_wide))
    d_resid, d_attn, vectors2 = resid_back(out_grad[:64], mine, parts, gains, hat2, scale2)
    grad_wide = lax.psum_scatter(grad_wide, SPANS, scatter_dimension=0, tiled=True)
    hidden, d_attn = lax.optimization_barrier((hidden, d_attn))
    ffn, *ffn_others = ffn_parts(place, hidden, down, down_other)
    pieces = z_gather(d_attn)
    pieces, ffn, ffn_others = lax.optimization_barrier((pieces, ffn, ffn_others))
    d_attn, d_gate, d_ret, outgoing = mixed_back(
        rate, place, pieces, late, gate, hat, scale, query
    )
    ffn_others = z_collect(ffn_others)
    parts = scan_parts(outgoing)

    d_query, key_part, value_part = query_back(
        rate, place, d_ret, value, key, query, probs, state, cosine, sine
    )
    out_halves = grad_split(place, d_attn, [mixed])
    gate_halves = grad_split(place, normed1, [d_gate, d_query])
    gate_halves, out_halves, ffn_others = lax.optimization_barrier(
        (gate_halves, out_halves, ffn_others)
    )
    parts, gate_halves, out_halves = lax.optimization_barrier(
        (parts, gate_halves, out_halves)
    )
    later = scan_back(scan_spans(scan_rate, parts, True))
    early_part = add_halves(gate_halves, out_halves)
    d_query, parts = lax.optimization_barrier((d_query, parts))
    d_first = normed_back_first(d_query, d_gate, late)
    early_part, later, d_first = lax.optimization_barrier((early_part, later, d_first))
    early_part = exchange(early_part, FIRST_WAY)

    d_both = key_value_back(
        rate, place, key_part, value_part, key, value, later, cosine, sine
    )
    late_halves = grad_split(place, normed1, [d_both])
    d_both, late_halves = lax.optimization_barrier((d_both, late_halves))
    mine, *parts, vectors = normed_back(place, d_first, d_both, early, early_other, hat1)
    vectors = jnp.concatenate([vectors, vectors2, jnp.zeros((4, 2048), F32)])
    shifted = [z_shift(vectors, shift) for shift in (1, 3, 2)]
    parts = z_collect(parts)
    late_part = add_halves(late_halves, vector_split(place, vectors, *shifted))
    late_part, early_part = lax.optimization_barrier((late_part, early_part))
    late_part = exchange(late_part, FIRST_WAY)

    rows = final_rows(resid, ffn, ffn_others, d_resid, mine, parts, gains, hat1, scale1)
    rows, late_part, grad_wide = lax.optimization_barrier((rows, late_part, grad_wide))
    block_out, tokens_grad = z_gather_home(rows, place, home)

    total = exchange(
        join_sums(early_part.reshape(4, 256, -1), late_part.reshape(4, 256, -1)), SECOND_WAY
    )
    total = swap_roles(last_sum(total.reshape(4, 64, -1)))
    total, block_out, tokens_grad = lax.optimization_barrier((total, block_out, tokens_grad))
    grad_gate, grad_query, grad_out, grad_key, grad_value, vectors = widen(
        total, [1024, 512, 1024, 512, 1024], True
    )
    grad_up, grad_down = widen(swap_roles(grad_wide), [1024, 1024])
    return (
        block_out,
        tokens_grad,
        vectors[0],
        vectors[1],
        grad_query,
        grad_key,
        grad_value,
        grad_gate,
        grad_out.T,
        vectors[2],
        vectors[3],
        grad_up,
        grad_down.T,
    )


def solution(mesh):
    fine = Mesh(mesh.devices.reshape(2, 2, 4, 2, 4), AXES)
    seq, tp = ("x", "zh", "y"), ("zl", "c")
    rows, wide, tall, vector = P(seq, None), P(seq, tp), P(tp, seq), P(seq)
    in_specs = (
        rows,
        vector,
        vector,
        wide,
        wide,
        wide,
        wide,
        tall,
        vector,
        vector,
        wide,
        tall,
        P(tp),
        rows,
    )
    out_specs = (
        rows,
        rows,
        vector,
        vector,
        wide,
        wide,
        wide,
        wide,
        tall,
        vector,
        vector,
        wide,
        tall,
    )
    return jax.shard_map(body, mesh=fine, in_specs=in_specs, out_specs=out_specs, check_vma=False)
```

```python
import functools
import itertools

import jax
import jax.numpy as jnp
from jax import lax
from jax.experimental import pallas as pl
from jax.experimental.pallas import tpu as pltpu
from jax.sharding import Mesh, PartitionSpec as P

DK = 256
DV = 512
AXES = ("zl", "c", "x", "zh", "y")
SIZES = {"zl": 2, "c": 2, "x": 4, "zh": 2, "y": 4}
SPANS = ("x", "c", "y")
CHIPS = ("c", "x", "y")
ALONG_X = [[x * 4 + y for x in range(4)] for y in range(4)]
ALONG_Y = [[x * 4 + y for y in range(4)] for x in range(4)]


def other_core(groups):
    return [[16 + i for i in group] for group in groups]


FIRST_WAY = ALONG_X + other_core(ALONG_Y)
SECOND_WAY = ALONG_Y + other_core(ALONG_X)
BF = jnp.bfloat16
F32 = jnp.float32


def pairs(axes, move):
    def flat(place):
        at = 0
        for axis in axes:
            at = at * SIZES[axis] + place[axis]
        return at

    found = []
    for values in itertools.product(*[range(SIZES[axis]) for axis in axes]):
        place = dict(zip(axes, values))
        target = move(dict(place))
        if target is not None:
            found.append((flat(place), flat(target)))
    return found


def swap_roles(values):
    return lax.ppermute(
        values, ("c", "zh"), pairs(("c", "zh"), lambda p: {"c": p["zh"], "zh": p["c"]})
    )


def z_shift(values, shift):
    def move(place):
        z = (place["zh"] * 2 + place["zl"] + shift) % 4
        return {"zl": z % 2, "zh": z // 2}

    return lax.ppermute(values, ("zl", "zh"), pairs(("zl", "zh"), move))


def z_shift_home(values, shift):
    def move(place):
        z = (place["zh"] * 2 + place["zl"] + shift) % 4
        if z // 2 != place["c"]:
            return None
        return {"zl": z % 2, "zh": z // 2, "c": place["c"]}

    return lax.ppermute(values, ("zl", "c", "zh"), pairs(("zl", "c", "zh"), move))


def core_from_home(values):
    def move(place):
        if place["zh"] != place["c"]:
            return None
        return {"c": 1 - place["c"], "zh": place["zh"]}

    return lax.ppermute(values, ("c", "zh"), pairs(("c", "zh"), move))


def core_swap(values):
    return lax.ppermute(values, "c", [(0, 1), (1, 0)])


def z_collect(parts):
    return [z_shift(parts[shift - 1], shift) for shift in (1, 3, 2)]


def z_gather(values):
    return [values, z_shift(values, 3), z_shift(values, 2), z_shift(values, 1)]


def z_gather_home(values, place, home):
    near, far, across = z_shift_home(values, 3), z_shift_home(values, 1), z_shift_home(values, 2)
    full = in_place(place, values, near, across, far)
    return chosen(home, full, core_from_home(full))


def nn(left, right):
    return jnp.dot(left, right, preferred_element_type=F32)


def nt(left, right):
    return lax.dot_general(left, right, (((1,), (1,)), ((), ())), preferred_element_type=F32)


def tn(left, right):
    return lax.dot_general(left, right, (((0,), (0,)), ((), ())), preferred_element_type=F32)


def norm_parts(values):
    center = values - jnp.mean(values, axis=-1, keepdims=True)
    spread = jnp.mean(center * center, axis=-1, keepdims=True)
    scale = lax.rsqrt(spread + 1e-05)
    return center * scale, scale


def norm_back(grad, hat, scale):
    mean_grad = jnp.mean(grad, axis=-1, keepdims=True)
    mean_both = jnp.mean(grad * hat, axis=-1, keepdims=True)
    return (grad - mean_grad - hat * mean_both) * scale


def scan_parts(fresh):
    return lax.all_to_all(fresh.reshape(32, 16, DV), SPANS, 0, 0, tiled=True)


def scan_back(carried):
    return lax.all_to_all(carried, SPANS, 0, 0, tiled=True).reshape(2 * DK, DV)


def exchange(values, groups):
    return lax.all_to_all(values, CHIPS, 0, 0, axis_index_groups=groups, tiled=True)


def run(kernel, grid, ins, outs, operands, scratch=(), limit=48, flops=1, moved=1):
    return pl.pallas_call(
        kernel,
        grid=grid,
        in_specs=ins,
        out_specs=[o[1] for o in outs],
        out_shape=[pltpu.HBM(o[0].shape, o[0].dtype) if len(o) > 2 else o[0] for o in outs],
        scratch_shapes=list(scratch),
        compiler_params=pltpu.CompilerParams(vmem_limit_bytes=limit * 1024 * 1024),
        cost_estimate=pl.CostEstimate(flops=flops, bytes_accessed=moved, transcendentals=0),
    )(*operands)


def shape(dims, dtype):
    return jax.ShapeDtypeStruct(dims, dtype)


def columns(rows, cols, first=0):
    return pl.BlockSpec((rows, cols), lambda h: (0, first + h))


def whole(dims):
    return pl.BlockSpec(dims, lambda h: (0,) * len(dims))


SCALARS = pl.BlockSpec(memory_space=pltpu.SMEM)


def places(dims, axis, z):
    at = lax.broadcasted_iota(jnp.int32, dims, axis) + z * 64
    return jnp.where(at >= 256, at - 256, at).astype(F32)


def decays(rate, z):
    at = places((256, 1), 0, z)
    return jnp.exp(-rate * (at + 1.0)), jnp.exp(-rate * (255.0 - at))


def span_mask(rate, z):
    offset = places((256, 256), 0, z) - places((256, 256), 1, z)
    return jnp.where(offset >= 0.0, jnp.exp(-rate * jnp.maximum(offset, 0.0)), 0.0)


def turn_into(ref, values, cosine, sine, start=0):
    half = DK // 2
    a, b = values[:, :half], values[:, half:]
    ref[:, start : start + half] = (a * cosine - b * sine).astype(ref.dtype)
    ref[:, start + half : start + DK] = (b * cosine + a * sine).astype(ref.dtype)


def in_place_kernel(place, *refs):
    out = refs[-1]
    for k in range(4):
        at = place[0] + k
        at = pl.multiple_of(jnp.where(at >= 4, at - 4, at) * 64, 64)
        out[pl.ds(at, 64), :] = refs[k][...]


def in_place(place, *pieces):
    return run(
        in_place_kernel,
        (1,),
        [SCALARS] + [whole((64, 4096))] * 4,
        [(shape((256, 4096), BF), whole((256, 4096)))],
        [place, *pieces],
    )[0]


def chosen_kernel(home, mine, other, block_out, tokens_grad):
    for flag, ref in ((1, mine), (0, other)):

        @pl.when(home[0] == flag)
        def take(ref=ref):
            block_out[...] = ref[:, :2048]
            tokens_grad[...] = ref[:, 2048:].astype(F32)


def chosen(home, mine, other):
    def block(cols):
        return pl.BlockSpec((64, cols), lambda i: (i, 0))

    return run(
        chosen_kernel,
        (4,),
        [SCALARS, block(4096), block(4096)],
        [(shape((256, 2048), BF), block(2048)), (shape((256, 2048), F32), block(2048))],
        [home, mine, other],
        limit=61,
    )


def scan_kernel(reverse, rate, parts, out):
    decay = jnp.exp(jnp.full((16, DV), -256.0 * rate[0], F32))
    state = jnp.zeros((16, DV), F32)
    for k in range(31, -1, -1) if reverse else range(32):
        out[k] = state.astype(BF)
        state = decay * state + parts[k].astype(F32)


def scan_spans(rate, parts, reverse):
    dims = (32, 16, DV)
    return run(
        functools.partial(scan_kernel, reverse),
        (1,),
        [SCALARS, whole(dims)],
        [(shape(dims, BF), whole(dims))],
        [rate, parts],
    )[0]


def pack_kernel(gains, *refs):
    out, start = refs[-1], 0
    for ref in refs[:-1]:
        out[:, start : start + ref.shape[1]] = ref[...]
        start += ref.shape[1]
        if start == 1536:
            start += 128
    wide = gains[...].astype(F32)
    same = lax.broadcasted_iota(jnp.int32, (64, 64), 0) == lax.broadcasted_iota(
        jnp.int32, (64, 64), 1
    )
    lane = lax.broadcasted_iota(jnp.int32, (64, 128), 1)
    total = jnp.zeros((64, 128), F32)
    for k in range(4):
        column = jnp.sum(jnp.where(same, wide[k : k + 1, :], 0.0), axis=1, keepdims=True)
        total = jnp.where(lane == k, column, total)
    out[:, 1536:1664] = total.astype(BF)


def pack(gains, *parts):
    cols = 128 + sum(p.shape[1] for p in parts)
    return run(
        pack_kernel,
        (1,),
        [whole((4, 64))] + [whole(p.shape) for p in parts],
        [(shape((64, cols), BF), whole((64, cols)))],
        [gains, *parts],
        limit=61,
    )[0]


def norm_kernel(tokens, hat, scale):
    made, spread = norm_parts(tokens[...].astype(F32))
    hat[...] = made
    scale[...] = spread


def norm_tokens(tokens):
    block = pl.BlockSpec((64, 2048), lambda i: (i, 0))
    return run(
        norm_kernel,
        (4,),
        [block],
        [
            (shape((256, 2048), F32), block, "hbm"),
            (shape((256, 1), F32), pl.BlockSpec((64, 1), lambda i: (i, 0)), "hbm"),
        ],
        [tokens],
        limit=61,
    )


def roll_kernel(place, values, out):
    for k in range(4):
        at = place[0] + k
        at = pl.multiple_of(jnp.where(at >= 4, at - 4, at) * 64, 64)
        out[k * 64 : k * 64 + 64, :] = values[pl.ds(at, 64), :]


def roll_rows(place, values):
    return run(
        roll_kernel,
        (1,),
        [SCALARS, whole((256, 2048))],
        [(shape((256, 2048), BF), whole((256, 2048)))],
        [place, values],
    )[0]


def collected(mine, others):
    total = mine[...]
    for other in others:
        total = total + other[...].astype(F32)
    return total


ROWS = pl.BlockSpec((64, 2048), lambda h: (0, 0))


def resid_kernel(tokens, mine, one, two, three, gains, resid, hat, scale, normed):
    total = tokens[...].astype(F32) + collected(mine, (one, two, three))
    resid[...] = total
    made, spread = norm_parts(total)
    hat[...] = made
    scale[...] = spread
    normed[...] = (made * gains[2:3] + gains[3:4]).astype(BF)


def resid_norm(tokens, mine, others, gains):
    return run(
        resid_kernel,
        (1,),
        [ROWS] * 5 + [whole((8, 2048))],
        [
            (shape((64, 2048), F32), ROWS),
            (shape((64, 2048), F32), ROWS),
            (shape((64, 1), F32), whole((64, 1))),
            (shape((64, 2048), BF), ROWS),
        ],
        [tokens, mine, *others, gains],
    )


def resid_back_kernel(
    out_grad, mine, one, two, three, gains, hat, scale, d_resid, d_attn, vectors
):
    total = collected(mine, (one, two, three))
    made = out_grad[...].astype(F32) + norm_back(total * gains[2:3], hat[...], scale[...])
    d_resid[...] = made
    d_attn[...] = made.astype(BF)
    vectors[0:1] = jnp.sum(total * hat[...], axis=0, keepdims=True)
    vectors[1:2] = jnp.sum(total, axis=0, keepdims=True)


def resid_back(out_grad, mine, others, gains, hat, scale):
    return run(
        resid_back_kernel,
        (1,),
        [ROWS] * 5 + [whole((8, 2048)), ROWS, whole((64, 1))],
        [
            (shape((64, 2048), F32), ROWS),
            (shape((64, 2048), BF), ROWS),
            (shape((2, 2048), F32), whole((2, 2048))),
        ],
        [out_grad, mine, *others, gains, hat, scale],
        limit=61,
    )


def rows_kernel(resid, f0, f1, f2, f3, d_resid, d0, d1, d2, d3, gains, hat, scale, out):
    out[:, :2048] = (resid[...] + collected(f0, (f1, f2, f3))).astype(BF)
    total = collected(d0, (d1, d2, d3))
    made = d_resid[...] + norm_back(total * gains[0:1], hat[...], scale[...])
    out[:, 2048:] = made.astype(BF)


def final_rows(resid, ffn, ffn_others, d_resid, mine, others, gains, hat, scale):
    return run(
        rows_kernel,
        (1,),
        [ROWS] * 10 + [whole((8, 2048)), ROWS, pl.BlockSpec((64, 1), lambda h: (0, 0))],
        [(shape((64, 4096), BF), whole((64, 4096)))],
        [resid, ffn, *ffn_others, d_resid, mine, *others, gains, hat, scale],
        limit=61,
    )[0]


def kv_kernel(
    rate,
    place,
    hat,
    gains_own,
    gains_other,
    key_own,
    key_other,
    value_own,
    value_other,
    cosine,
    sine,
    key,
    value,
    fresh,
    normed,
    gains,
    own,
    other,
):
    @pl.when(pl.program_id(0) == 0)
    def norm():
        mine = gains_own[...].astype(F32).T
        yours = gains_other[...].astype(F32).T
        for i in range(4):
            for ref, rows, side in ((own, mine, place[1]), (other, yours, 1 - place[1])):
                at = pl.multiple_of((2 * i + side) * 256, 256)
                rows = rows[:8, i * 256 : i * 256 + 256]
                gains[:, pl.ds(at, 256)] = rows
                out = (hat[:, pl.ds(at, 256)] * rows[0:1] + rows[1:2]).astype(BF)
                normed[:, pl.ds(at, 256)] = out
                ref[:, i * 256 : i * 256 + 256] = out

    qdec, kdec = decays(rate[pl.program_id(0)], place[0])
    raw = nn(own[...], key_own[...]) + nn(other[...], key_other[...])
    turn_into(key, raw, cosine[...], sine[...])
    made = (nn(own[...], value_own[...]) + nn(other[...], value_other[...])).astype(BF)
    value[...] = made
    fresh[...] = tn((kdec * key[...].astype(F32)).astype(BF), made).astype(BF)


def key_value(rate, place, hat, early, early_other, cosine, sine):
    gains = pl.BlockSpec((1024, 128), lambda h: (0, 12))
    return run(
        kv_kernel,
        (2,),
        [
            SCALARS,
            SCALARS,
            whole((256, 2048)),
            gains,
            gains,
            columns(1024, 256),
            columns(1024, 256),
            columns(1024, 512, 1),
            columns(1024, 512, 1),
            whole((256, 128)),
            whole((256, 128)),
        ],
        [
            (shape((256, 512), BF), columns(256, 256)),
            (shape((256, 1024), BF), columns(256, 512)),
            (shape((512, 512), BF), pl.BlockSpec((256, 512), lambda h: (h, 0))),
            (shape((256, 2048), BF), whole((256, 2048))),
            (shape((8, 2048), F32), whole((8, 2048))),
        ],
        [
            rate,
            place,
            hat,
            early,
            early_other,
            early,
            early_other,
            early,
            early_other,
            cosine,
            sine,
        ],
        [pltpu.VMEM((256, 1024), BF), pltpu.VMEM((256, 1024), BF)],
        limit=61,
    )


def query_kernel(
    rate, place, normed, w_query, w_gate, key, value, cosine, sine, query, gate, probs, inner
):
    raw = nn(normed[...], w_query[...])
    turn_into(query, raw, cosine[...], sine[...])
    gate[...] = nn(normed[...], w_gate[...])
    mask = span_mask(rate[pl.program_id(0)], place[0])
    made = (nt(query[...], key[...]) * mask).astype(BF)
    probs[0] = made
    inner[...] = nn(made, value[...])


def query_gate(rate, place, normed1, late, key, value, cosine, sine):
    return run(
        query_kernel,
        (2,),
        [
            SCALARS,
            SCALARS,
            whole((256, 2048)),
            columns(2048, 256, 12),
            columns(2048, 512),
            columns(256, 256),
            columns(256, 512),
            whole((256, 128)),
            whole((256, 128)),
        ],
        [
            (shape((256, 512), BF), columns(256, 256)),
            (shape((256, 1024), F32), columns(256, 512), "hbm"),
            (shape((2, 256, 256), BF), pl.BlockSpec((1, 256, 256), lambda h: (h, 0, 0))),
            (shape((256, 1024), F32), columns(256, 512)),
        ],
        [rate, place, normed1, late, late, key, value, cosine, sine],
        limit=61,
    )


def cut_rows(full, parts):
    parts[0][...] = full[:64]
    for k in range(1, 4):
        parts[k][...] = full[k * 64 : k * 64 + 64].astype(BF)


def row_parts(cols, index):
    spec = pl.BlockSpec((64, cols), index)
    return [(shape((64, 2048), F32 if k == 0 else BF), spec) for k in range(4)]


def retain_kernel(
    rate, place, query, state, inner, gate, w_out, hat, scale, mixed, mine, one, two, three, total
):
    h = pl.program_id(0)
    qdec, kdec = decays(rate[h], place[0])
    retained = inner[...] + qdec * nn(query[...], state[...])
    made, spread = norm_parts(retained)
    hat[...] = made
    scale[0] = spread
    wide = gate[...]
    made = (wide * jax.nn.sigmoid(wide) * made).astype(BF)
    mixed[...] = made
    partial = nt(made, w_out[...])

    @pl.when(h == 0)
    def first():
        total[...] = partial

    @pl.when(h == 1)
    def last():
        cut_rows(total[...] + partial, (mine, one, two, three))


def retain(rate, place, query, state, inner, gate, late):
    return run(
        retain_kernel,
        (2,),
        [
            SCALARS,
            SCALARS,
            columns(256, 256),
            pl.BlockSpec((256, 512), lambda h: (h, 0)),
            columns(256, 512),
            columns(256, 512),
            columns(2048, 512, 2),
        ],
        [
            (shape((256, 1024), F32), columns(256, 512), "hbm"),
            (shape((2, 256, 1), F32), pl.BlockSpec((1, 256, 1), lambda h: (h, 0, 0)), "hbm"),
            (shape((256, 1024), BF), columns(256, 512)),
            *row_parts(2048, lambda h: (0, 0)),
        ],
        [rate, place, query, state, inner, gate, late],
        [pltpu.VMEM((256, 2048), F32)],
        limit=61,
    )


def gathered(pieces, full):
    @pl.when(pl.program_id(0) == 0)
    def join():
        for k, piece in enumerate(pieces):
            full[k * 64 : k * 64 + 64, :] = piece[...]


def up_kernel(
    one, two, three, four, w_up, d_hidden, normed, hidden, d_up, mine, p1, p2, p3, total
):
    j = pl.program_id(0)
    gathered((one, two, three, four), normed)
    raw = nn(normed[...], w_up[...])
    root = 0.7978845608028654
    square = raw * raw
    tanh = jnp.tanh(root * raw * (1.0 + 0.044715 * square))
    half = 0.5 * (1.0 + tanh)
    hidden[...] = (raw * half).astype(BF)
    slope = half + 0.5 * raw * (1.0 - tanh * tanh) * root * (1.0 + 0.134145 * square)
    made = (slope * d_hidden[...]).astype(BF)
    d_up[...] = made
    partial = nt(made, w_up[...])

    @pl.when(j == 0)
    def first():
        total[...] = partial

    @pl.when(j == 1)
    def last():
        cut_rows(total[...] + partial, (mine, p1, p2, p3))


def up_back(pieces, late, d_hidden):
    return run(
        up_kernel,
        (2,),
        [ROWS] * 4 + [columns(2048, 512, 4), columns(256, 512)],
        [
            (shape((256, 2048), BF), whole((256, 2048))),
            (shape((256, 1024), BF), columns(256, 512)),
            (shape((256, 1024), BF), columns(256, 512)),
            *row_parts(2048, lambda h: (0, 0)),
        ],
        [*pieces, late, d_hidden],
        [pltpu.VMEM((256, 2048), F32)],
    )


def mixed_kernel(
    rate, place, one, two, three, four, w_out, gate, hat, scale, query, d_attn, d_gate, d_ret, outgoing
):
    gathered((one, two, three, four), d_attn)
    qdec, kdec = decays(rate[pl.program_id(0)], place[0])
    d_mixed = nn(d_attn[...], w_out[...])
    wide, normed = gate[...], hat[...]
    sig = jax.nn.sigmoid(wide)
    d_gate[...] = (d_mixed * normed * sig * (1.0 + wide * (1.0 - sig))).astype(BF)
    made = norm_back(d_mixed * wide * sig, normed, scale[0]).astype(BF)
    d_ret[...] = made
    outgoing[...] = tn((qdec * query[...].astype(F32)).astype(BF), made).astype(BF)


def mixed_back(rate, place, pieces, late, gate, hat, scale, query):
    return run(
        mixed_kernel,
        (2,),
        [
            SCALARS,
            SCALARS,
            *[ROWS] * 4,
            columns(2048, 512, 2),
            columns(256, 512),
            columns(256, 512),
            pl.BlockSpec((1, 256, 1), lambda h: (h, 0, 0)),
            columns(256, 256),
        ],
        [
            (shape((256, 2048), BF), whole((256, 2048))),
            (shape((256, 1024), BF), columns(256, 512)),
            (shape((256, 1024), BF), columns(256, 512)),
            (shape((512, 512), BF), pl.BlockSpec((256, 512), lambda h: (h, 0))),
        ],
        [rate, place, *pieces, late, gate, hat, scale, query],
        limit=61,
    )


def query_back_kernel(
    rate, place, d_ret, value, key, query, probs, state, cosine, sine, d_query, key_part, value_part
):
    h = pl.program_id(0)
    qdec, kdec = decays(rate[h], place[0])
    mask = span_mask(rate[h], place[0])
    d_scores = (nt(d_ret[...], value[...]) * mask).astype(BF)
    turned = nn(d_scores, key[...]) + qdec * nt(d_ret[...], state[...])
    turn_into(d_query, turned, cosine[...], -sine[...])
    key_part[...] = tn(d_scores, query[...])
    value_part[...] = tn(probs[0], d_ret[...])


def query_back(rate, place, d_ret, value, key, query, probs, state, cosine, sine):
    return run(
        query_back_kernel,
        (2,),
        [
            SCALARS,
            SCALARS,
            columns(256, 512),
            columns(256, 512),
            columns(256, 256),
            columns(256, 256),
            pl.BlockSpec((1, 256, 256), lambda h: (h, 0, 0)),
            pl.BlockSpec((256, 512), lambda h: (h, 0)),
            whole((256, 128)),
            whole((256, 128)),
        ],
        [
            (shape((256, 512), BF), columns(256, 256)),
            (shape((256, 512), F32), columns(256, 256)),
            (shape((256, 1024), F32), columns(256, 512)),
        ],
        [rate, place, d_ret, value, key, query, probs, state, cosine, sine],
        limit=61,
    )


def key_value_back_kernel(
    rate, place, key_part, value_part, key, value, later, cosine, sine, d_both
):
    for h in range(2):
        qdec, kdec = decays(rate[h], place[0])
        keys, values = slice(h * DK, h * DK + DK), slice(h * DV, h * DV + DV)
        carried = later[keys, :]
        d_key = key_part[:, keys] + kdec * nt(value[:, values], carried)
        turn_into(d_both, d_key, cosine[...], -sine[...], h * DK)
        d_value = value_part[:, values] + kdec * nn(key[:, keys], carried)
        d_both[:, 512 + h * DV : 512 + h * DV + DV] = d_value.astype(BF)


def key_value_back(rate, place, key_part, value_part, key, value, later, cosine, sine):
    return run(
        key_value_back_kernel,
        (1,),
        [
            SCALARS,
            SCALARS,
            whole((256, 512)),
            whole((256, 1024)),
            whole((256, 512)),
            whole((256, 1024)),
            whole((512, 512)),
            whole((256, 128)),
            whole((256, 128)),
        ],
        [(shape((256, 1536), BF), whole((256, 1536)))],
        [rate, place, key_part, value_part, key, value, later, cosine, sine],
        limit=61,
    )[0]


def normed_first_kernel(d_query, d_gate, w_query, w_gate, part):
    part[...] = nt(d_query[...], w_query[...]) + nt(d_gate[...], w_gate[...])


def normed_back_first(d_query, d_gate, late):
    return run(
        normed_first_kernel,
        (4,),
        [
            whole((256, 512)),
            whole((256, 1024)),
            pl.BlockSpec((512, 512), lambda i: (i, 6)),
            pl.BlockSpec((512, 1024), lambda i: (i, 0)),
        ],
        [(shape((256, 2048), F32), columns(256, 512))],
        [d_query, d_gate, late, late],
    )[0]


def normed_back_kernel(place, first, d_both, w_own, w_other, hat, mine, one, two, three, vectors):
    left = nt(d_both[...], w_own[:, :1536])
    right = nt(d_both[...], w_other[:, :1536])
    low = place[1] == 0
    total = first[...] + jnp.concatenate(
        [jnp.where(low, left, right), jnp.where(low, right, left)], axis=1
    )
    cut_rows(total, (mine, one, two, three))
    vectors[0:1] = jnp.sum(total * hat[...], axis=0, keepdims=True)
    vectors[1:2] = jnp.sum(total, axis=0, keepdims=True)


def normed_back(place, first, d_both, early, early_other, hat):
    weights = pl.BlockSpec((256, 1664), lambda i: (i, 0))
    return run(
        normed_back_kernel,
        (4,),
        [
            SCALARS,
            columns(256, 512),
            whole((256, 1536)),
            weights,
            weights,
            columns(256, 512),
        ],
        [
            *row_parts(512, lambda i: (0, i)),
            (shape((2, 2048), F32), columns(2, 512)),
        ],
        [place, first, d_both, early, early_other, hat],
    )


def pair_kernel(left_one, right_one, left_two, right_two, out):
    w = pl.program_id(0)

    @pl.when(w == 0)
    def first():
        out[...] = tn(left_one[...], right_one[...]).astype(BF)

    @pl.when(w == 1)
    def second():
        out[...] = tn(left_two[...], right_two[...]).astype(BF)


def grad_pair(left_one, right_one, left_two, right_two):
    def left(w):
        return pl.BlockSpec((256, 512), lambda v, i: (0, jnp.where(v == w, i, 3 * (1 - w))))

    right = pl.BlockSpec((256, 1024), lambda v, i: (0, 0))
    return run(
        pair_kernel,
        (2, 4),
        [left(0), right, left(1), right],
        [(shape((2048, 2048), BF), pl.BlockSpec((512, 1024), lambda v, i: (i, v)))],
        [left_one, right_one, left_two, right_two],
        flops=4 * 256 * 2048 * 1024,
        moved=16 * 2048 * 1024,
    )[0]


def down_kernel(place, out_grad, w_own, w_other, d_hidden):
    total = jnp.zeros(d_hidden.shape, F32)
    for w, side in ((w_own, place[1]), (w_other, 1 - place[1])):
        for i in range(4):
            at = pl.multiple_of((2 * i + side) * 256, 256)
            total = total + nn(out_grad[:, pl.ds(at, 256)], w[i * 256 : i * 256 + 256, :])
    d_hidden[...] = total


def down_back(place, out_grad, w_own, w_other):
    return run(
        down_kernel,
        (2,),
        [SCALARS, whole((256, 2048)), columns(1024, 512), columns(1024, 512)],
        [(shape((256, 1024), F32), columns(256, 512))],
        [place, out_grad, w_own, w_other],
    )[0]


def ffn_kernel(place, hidden, w_own, w_other, mine, one, two, three):
    left, right = nt(hidden[...], w_own[...]), nt(hidden[...], w_other[...])
    low = place[1] == 0
    total = jnp.concatenate([jnp.where(low, left, right), jnp.where(low, right, left)], axis=1)
    cut_rows(total, (mine, one, two, three))


def ffn_parts(place, hidden, w_own, w_other):
    weights = pl.BlockSpec((256, 1024), lambda i: (i, 0))
    return run(
        ffn_kernel,
        (4,),
        [SCALARS, whole((256, 1024)), weights, weights],
        row_parts(512, lambda i: (0, i)),
        [place, hidden, w_own, w_other],
    )


def store_rows(ref, made, side, start):
    i = pl.program_id(0)
    for j in range(4):
        to = jnp.where(side == 0, i * 256 + j * 64, j * 256 + i * 64)
        ref[pl.ds(pl.multiple_of(to, 64), 64), start : start + made.shape[1]] = made[
            j * 64 : j * 64 + 64
        ]


def row_offsets(side):
    i = pl.program_id(0)
    for j in range(4):
        to = jnp.where(side == 0, i * 256 + j * 64, j * 256 + i * 64)
        yield slice(j * 64, j * 64 + 64), pl.ds(pl.multiple_of(to, 64), 64)


def other_kernel(place, left, *refs):
    rights, other = refs[:-1], refs[-1]
    side = 1 - place[1]
    rows = left[:, pl.ds(pl.multiple_of(side * 256, 256), 256)]
    start = 0
    for right in rights:
        store_rows(other, tn(rows, right[...]).astype(BF), side, start)
        start += right.shape[1]


def grad_other(place, left, rights):
    cols = sum(r.shape[1] for r in rights)
    return run(
        other_kernel,
        (4,),
        [SCALARS, columns(256, 512)] + [whole(r.shape) for r in rights],
        [(shape((1024, cols), BF), whole((1024, cols)))],
        [place, left, *rights],
        limit=61,
    )[0]


def own_kernel(sizes, place, *refs):
    out, refs, start = refs[-1], list(refs[:-1]), 0
    side = place[1]
    for size in sizes:
        left, rights, given = refs[0], refs[1 : 1 + size], refs[1 + size]
        refs, local = refs[2 + size :], 0
        rows = left[:, pl.ds(pl.multiple_of(side * 256, 256), 256)]
        for right in rights:
            made, cols = tn(rows, right[...]), right.shape[1]
            for take, to in row_offsets(side):
                total = made[take] + given[to, local : local + cols].astype(F32)
                out[to, start : start + cols] = total.astype(BF)
            start, local = start + cols, local + cols
    if refs:
        for take, to in row_offsets(side):
            total = refs[0][to, :].astype(F32) + refs[1][to, :].astype(F32)
            out[to, start:] = total.astype(BF)


def grad_own(place, groups, more=()):
    specs, operands, sizes, cols = [SCALARS], [place], [], sum(m.shape[1] for m in more[:1])
    for left, rights, given in groups:
        specs += [columns(256, 512)] + [whole(r.shape) for r in rights] + [whole(given.shape)]
        operands += [left, *rights, given]
        sizes.append(len(rights))
        cols += given.shape[1]
    specs += [whole(m.shape) for m in more]
    return run(
        functools.partial(own_kernel, tuple(sizes)),
        (4,),
        specs,
        [(shape((1024, cols), BF), whole((1024, cols)), "hbm")],
        operands + list(more),
        limit=61,
    )[0]


def vector_kernel(place, one, two, three, four, own, other):
    total = one[...] + two[...] + three[...] + four[...]
    for ref, side in ((own, 0), (other, 1)):
        rows = jnp.where(place[1] == side, total[:, :256], total[:, 256:])
        rows = jnp.concatenate([rows, jnp.zeros((120, 256), F32)], axis=0)
        store_rows(ref, rows.T.astype(BF), place[1] if side == 0 else 1 - place[1], 0)


def vector_split(place, *vectors):
    half = (shape((1024, 128), BF), whole((1024, 128)))
    return run(
        vector_kernel,
        (4,),
        [SCALARS] + [columns(8, 512)] * 4,
        [half, half],
        [place, *vectors],
    )


def four_sum(ref):
    total = ref[0].astype(F32)
    for k in range(1, 4):
        total = total + ref[k].astype(F32)
    return total.astype(BF)


def early_kernel(parts, out):
    out[:, out.shape[1] - parts.shape[2] :] = four_sum(parts)


def early_sum(parts, cols):
    return run(
        early_kernel,
        (4,),
        [pl.BlockSpec((4, 64, parts.shape[2]), lambda i: (0, i, 0))],
        [(shape((256, cols), BF), pl.BlockSpec((64, cols), lambda i: (i, 0)), "hbm")],
        [parts],
        limit=61,
    )[0]


def late_kernel(kept, parts, out):
    out[...] = four_sum(parts)


def late_sum(wide, parts):
    cols = parts.shape[2]
    return pl.pallas_call(
        late_kernel,
        grid=(4,),
        in_specs=[
            pl.BlockSpec(memory_space=pl.ANY),
            pl.BlockSpec((4, 64, cols), lambda i: (0, i, 0)),
        ],
        out_specs=pl.BlockSpec((64, cols), lambda i: (i, 0)),
        out_shape=pltpu.HBM(wide.shape, BF),
        input_output_aliases={0: 0},
        compiler_params=pltpu.CompilerParams(vmem_limit_bytes=48 * 1024 * 1024),
        cost_estimate=pl.CostEstimate(flops=1, bytes_accessed=1, transcendentals=0),
    )(wide, parts)


def last_kernel(parts, out):
    total = parts[0].astype(F32)
    for k in range(1, 4):
        total = total + parts[k].astype(F32)
    out[...] = total.astype(BF)


def last_sum(parts):
    dims = parts.shape[1:]
    return run(
        last_kernel,
        (1,),
        [whole(parts.shape)],
        [(shape(dims, BF), whole(dims))],
        [parts],
    )[0]


def widen_kernel(values, *outs):
    start = 0
    for out in outs:
        if out.shape[0] == 64:
            out[...] = values[:, start : start + out.shape[1]].astype(F32)
            start += out.shape[1]
        else:
            out[...] = values[:, start : start + 128].astype(F32).T[:8]
            start += 128


def widen(values, widths):
    dims = [(64, n) if n else (8, 64) for n in widths]
    outs = [(shape(d, F32), whole(d)) for d in dims]
    return run(widen_kernel, (1,), [whole(values.shape)], outs, [values])


def body(
    tokens,
    norm1_gain,
    norm1_bias,
    w_query,
    w_key,
    w_value,
    w_gate,
    w_out,
    norm2_gain,
    norm2_bias,
    w_up,
    w_down,
    decay_rate,
    out_grad,
):
    x, y, c = lax.axis_index("x"), lax.axis_index("y"), lax.axis_index("c")
    zl, zh = lax.axis_index("zl"), lax.axis_index("zh")
    z = zh * 2 + zl
    home = (zh == c).astype(jnp.int32).reshape(1)
    span = x * 8 + c * 4 + y
    place = jnp.stack([z, c, x, y]).astype(jnp.int32)

    gains = jnp.stack([norm1_gain, norm1_bias, norm2_gain, norm2_bias])
    shards = swap_roles(
        pack(gains, w_key, w_value, w_gate, w_out.T, w_up, w_query)
    )
    first, second = shards[:, :1664], shards[:, 1664:]
    rate = swap_roles(decay_rate)
    tokens, kept = lax.optimization_barrier((tokens, shards))
    tokens = swap_roles(tokens)
    third, kept = lax.optimization_barrier((w_down.T, tokens))
    third = jnp.broadcast_to(swap_roles(third)[None], (16, 64, 1024))
    out_grad, kept = lax.optimization_barrier((out_grad, tokens))
    out_grad = swap_roles(out_grad)

    cols = first.shape[1]
    early = lax.all_to_all(
        jnp.broadcast_to(first[None], (16, 64, cols)), ("x", "y"), 0, 0, tiled=True
    ).reshape(1024, cols)
    late = lax.all_gather(second, SPANS, axis=0, tiled=True)

    tokens = roll_rows(place, tokens)
    hat1, scale1 = norm_tokens(tokens)
    out_grad = roll_rows(place, out_grad)
    index = ((jnp.arange(256) + z * 64) % 256).astype(F32)
    half = DK // 2
    position = (span * 256).astype(F32) + index
    freq = 10000.0 ** (-jnp.arange(half).astype(F32) / half)
    angle = position[:, None] * freq[None, :]
    cosine, sine = jnp.cos(angle), jnp.sin(angle)
    early, tokens, hat1, out_grad, third, cosine, sine, rate = lax.optimization_barrier(
        (early, tokens, hat1, out_grad, third, cosine, sine, rate)
    )

    early_other = core_swap(early)
    key, value, fresh, normed1, gains = key_value(
        rate, place, hat1, early, early_other, cosine, sine
    )
    scan_rate = jnp.where(x < 2, rate[0], rate[1]).reshape(1)
    carried = scan_spans(scan_rate, scan_parts(fresh), False)
    state = scan_back(carried)
    query, gate, probs, inner = query_gate(
        rate, place, normed1, late, key, value, cosine, sine
    )
    third, state, query = lax.optimization_barrier((third, state, query))
    down = lax.all_to_all(third, ("x", "y"), 0, 0, tiled=True).reshape(1024, 1024)
    hat, scale, mixed, mine, *parts = retain(rate, place, query, state, inner, gate, late)
    parts = z_collect(parts)
    resid, hat2, scale2, normed2 = resid_norm(tokens[:64], mine, parts, gains)
    down, kept = lax.optimization_barrier((down, normed2))
    down_other = core_swap(down)
    d_hidden = down_back(place, out_grad, down, down_other)
    normed2, hidden, d_up, mine, *parts = up_back(z_gather(normed2), late, d_hidden)
    parts = z_collect(parts)
    grad_wide = grad_pair(normed2, d_up, out_grad, hidden)
    mine, parts, grad_wide = lax.optimization_barrier((mine, parts, grad_wide))
    d_resid, d_attn, vectors2 = resid_back(out_grad, mine, parts, gains, hat2, scale2)
    grad_wide = lax.psum_scatter(grad_wide, SPANS, scatter_dimension=0, tiled=True)
    hidden, d_attn = lax.optimization_barrier((hidden, d_attn))
    ffn, *ffn_others = ffn_parts(place, hidden, down, down_other)
    pieces = z_gather(d_attn)
    pieces, ffn, ffn_others = lax.optimization_barrier((pieces, ffn, ffn_others))
    d_attn, d_gate, d_ret, outgoing = mixed_back(
        rate, place, pieces, late, gate, hat, scale, query
    )
    ffn_others = z_collect(ffn_others)
    parts = scan_parts(outgoing)

    d_query, key_part, value_part = query_back(
        rate, place, d_ret, value, key, query, probs, state, cosine, sine
    )
    out_other = grad_other(place, d_attn, [mixed])
    gate_other = grad_other(place, normed1, [d_gate, d_query])
    gate_other, out_other, ffn_others = lax.optimization_barrier(
        (gate_other, out_other, ffn_others)
    )
    parts, gate_other, out_other = lax.optimization_barrier((parts, gate_other, out_other))
    later = scan_back(scan_spans(scan_rate, parts, True))
    early_part = grad_own(
        place,
        [
            (normed1, [d_gate, d_query], core_swap(gate_other)),
            (d_attn, [mixed], core_swap(out_other)),
        ],
    )
    d_query, parts = lax.optimization_barrier((d_query, parts))
    d_first = normed_back_first(d_query, d_gate, late)
    early_part, later, d_first = lax.optimization_barrier((early_part, later, d_first))
    early_part = exchange(early_part, FIRST_WAY)

    d_both = key_value_back(
        rate, place, key_part, value_part, key, value, later, cosine, sine
    )
    late_other = grad_other(place, normed1, [d_both])
    d_both, late_other = lax.optimization_barrier((d_both, late_other))
    late_other = core_swap(late_other)
    mine, *parts, vectors = normed_back(place, d_first, d_both, early, early_other, hat1)
    vectors = jnp.concatenate([vectors, vectors2, jnp.zeros((4, 2048), F32)])
    shifted = [z_shift(vectors, shift) for shift in (1, 3, 2)]
    parts = z_collect(parts)
    vector_own, vector_other = vector_split(place, vectors, *shifted)
    late_part = grad_own(
        place, [(normed1, [d_both], late_other)], (vector_own, core_swap(vector_other))
    )
    late_part, early_part = lax.optimization_barrier((late_part, early_part))
    late_part = exchange(late_part, FIRST_WAY)

    joined = early_sum(early_part.reshape(4, 256, -1), 4224)
    parts, grad_wide, joined = lax.optimization_barrier((parts, grad_wide, joined))
    rows = final_rows(resid, ffn, ffn_others, d_resid, mine, parts, gains, hat1, scale1)
    kept, late_part = lax.optimization_barrier((rows, late_part))
    block_out, tokens_grad = z_gather_home(rows, place, home)

    total = exchange(late_sum(joined, late_part.reshape(4, 256, -1)), SECOND_WAY)
    total, grad_wide = lax.optimization_barrier((total, swap_roles(grad_wide)))
    total = swap_roles(last_sum(total.reshape(4, 64, -1)))
    total, block_out, tokens_grad = lax.optimization_barrier((total, block_out, tokens_grad))
    grad_key, grad_value, vectors, grad_gate, grad_query, grad_out = widen(
        total, [512, 1024, 0, 1024, 512, 1024]
    )
    grad_up, grad_down = widen(grad_wide, [1024, 1024])
    return (
        block_out,
        tokens_grad,
        vectors[0],
        vectors[1],
        grad_query,
        grad_key,
        grad_value,
        grad_gate,
        grad_out.T,
        vectors[2],
        vectors[3],
        grad_up,
        grad_down.T,
    )


def solution(mesh):
    fine = Mesh(mesh.devices.reshape(2, 2, 4, 2, 4), AXES)
    seq, tp = ("x", "zh", "y"), ("zl", "c")
    rows, wide, tall, vector = P(seq, None), P(seq, tp), P(tp, seq), P(seq)
    in_specs = (
        rows,
        vector,
        vector,
        wide,
        wide,
        wide,
        wide,
        tall,
        vector,
        vector,
        wide,
        tall,
        P(tp),
        rows,
    )
    out_specs = (
        rows,
        rows,
        vector,
        vector,
        wide,
        wide,
        wide,
        wide,
        tall,
        vector,
        vector,
        wide,
        tall,
    )
    return jax.shard_map(body, mesh=fine, in_specs=in_specs, out_specs=out_specs, check_vma=False)
```

```python
import functools
import itertools

import jax
import jax.numpy as jnp
from jax import lax
from jax.experimental import pallas as pl
from jax.experimental.pallas import tpu as pltpu
from jax.sharding import Mesh, PartitionSpec as P

DK = 256
DV = 512
AXES = ("zl", "c", "x", "zh", "y")
SIZES = {"zl": 2, "c": 2, "x": 4, "zh": 2, "y": 4}
SPANS = ("x", "c", "y")
CHIPS = ("c", "x", "y")
ALONG_X = [[x * 4 + y for x in range(4)] for y in range(4)]
ALONG_Y = [[x * 4 + y for y in range(4)] for x in range(4)]


def other_core(groups):
    return [[16 + i for i in group] for group in groups]


FIRST_WAY = ALONG_X + other_core(ALONG_Y)
SECOND_WAY = ALONG_Y + other_core(ALONG_X)
BF = jnp.bfloat16
F32 = jnp.float32


def pairs(axes, move):
    def flat(place):
        at = 0
        for axis in axes:
            at = at * SIZES[axis] + place[axis]
        return at

    found = []
    for values in itertools.product(*[range(SIZES[axis]) for axis in axes]):
        place = dict(zip(axes, values))
        target = move(dict(place))
        if target is not None:
            found.append((flat(place), flat(target)))
    return found


def swap_roles(values):
    return lax.ppermute(
        values, ("c", "zh"), pairs(("c", "zh"), lambda p: {"c": p["zh"], "zh": p["c"]})
    )


def z_shift(values, shift):
    def move(place):
        z = (place["zh"] * 2 + place["zl"] + shift) % 4
        return {"zl": z % 2, "zh": z // 2}

    return lax.ppermute(values, ("zl", "zh"), pairs(("zl", "zh"), move))


def z_shift_home(values, shift):
    def move(place):
        z = (place["zh"] * 2 + place["zl"] + shift) % 4
        if z // 2 != place["c"]:
            return None
        return {"zl": z % 2, "zh": z // 2, "c": place["c"]}

    return lax.ppermute(values, ("zl", "c", "zh"), pairs(("zl", "c", "zh"), move))


def core_from_home(values):
    def move(place):
        if place["zh"] != place["c"]:
            return None
        return {"c": 1 - place["c"], "zh": place["zh"]}

    return lax.ppermute(values, ("c", "zh"), pairs(("c", "zh"), move))


def core_swap(values):
    return lax.ppermute(values, "c", [(0, 1), (1, 0)])


def z_collect(parts):
    return [z_shift(parts[shift - 1], shift) for shift in (1, 3, 2)]


def z_gather(values):
    return [values, z_shift(values, 3), z_shift(values, 2), z_shift(values, 1)]


def z_gather_home(values, place, home):
    near, far, across = z_shift_home(values, 3), z_shift_home(values, 1), z_shift_home(values, 2)
    full = in_place(place, values, near, across, far)
    return chosen(home, full, core_from_home(full))


def nn(left, right):
    return jnp.dot(left, right, preferred_element_type=F32)


def nt(left, right):
    return lax.dot_general(left, right, (((1,), (1,)), ((), ())), preferred_element_type=F32)


def tn(left, right):
    return lax.dot_general(left, right, (((0,), (0,)), ((), ())), preferred_element_type=F32)


def norm_parts(values):
    center = values - jnp.mean(values, axis=-1, keepdims=True)
    spread = jnp.mean(center * center, axis=-1, keepdims=True)
    scale = lax.rsqrt(spread + 1e-05)
    return center * scale, scale


def norm_back(grad, hat, scale):
    mean_grad = jnp.mean(grad, axis=-1, keepdims=True)
    mean_both = jnp.mean(grad * hat, axis=-1, keepdims=True)
    return (grad - mean_grad - hat * mean_both) * scale


def scan_parts(fresh):
    return lax.all_to_all(fresh.reshape(32, 16, DV), SPANS, 0, 0, tiled=True)


def scan_back(carried):
    return lax.all_to_all(carried, SPANS, 0, 0, tiled=True).reshape(2 * DK, DV)


def exchange(values, groups):
    return lax.all_to_all(values, CHIPS, 0, 0, axis_index_groups=groups, tiled=True)


def run(kernel, grid, ins, outs, operands, scratch=(), limit=48, flops=1, moved=1):
    return pl.pallas_call(
        kernel,
        grid=grid,
        in_specs=ins,
        out_specs=[o[1] for o in outs],
        out_shape=[pltpu.HBM(o[0].shape, o[0].dtype) if len(o) > 2 else o[0] for o in outs],
        scratch_shapes=list(scratch),
        compiler_params=pltpu.CompilerParams(vmem_limit_bytes=limit * 1024 * 1024),
        cost_estimate=pl.CostEstimate(flops=flops, bytes_accessed=moved, transcendentals=0),
    )(*operands)


def shape(dims, dtype):
    return jax.ShapeDtypeStruct(dims, dtype)


def columns(rows, cols, first=0):
    return pl.BlockSpec((rows, cols), lambda h: (0, first + h))


def whole(dims):
    return pl.BlockSpec(dims, lambda h: (0,) * len(dims))


SCALARS = pl.BlockSpec(memory_space=pltpu.SMEM)


def places(dims, axis, z):
    at = lax.broadcasted_iota(jnp.int32, dims, axis) + z * 64
    return jnp.where(at >= 256, at - 256, at).astype(F32)


def decays(rate, z):
    at = places((256, 1), 0, z)
    return jnp.exp(-rate * (at + 1.0)), jnp.exp(-rate * (255.0 - at))


def span_mask(rate, z):
    offset = places((256, 256), 0, z) - places((256, 256), 1, z)
    return jnp.where(offset >= 0.0, jnp.exp(-rate * jnp.maximum(offset, 0.0)), 0.0)


def turn_into(ref, values, cosine, sine, start=0):
    half = DK // 2
    a, b = values[:, :half], values[:, half:]
    ref[:, start : start + half] = (a * cosine - b * sine).astype(ref.dtype)
    ref[:, start + half : start + DK] = (b * cosine + a * sine).astype(ref.dtype)


def in_place_kernel(place, *refs):
    out = refs[-1]
    for k in range(4):
        at = place[0] + k
        at = pl.multiple_of(jnp.where(at >= 4, at - 4, at) * 64, 64)
        out[pl.ds(at, 64), :] = refs[k][...]


def in_place(place, *pieces):
    return run(
        in_place_kernel,
        (1,),
        [SCALARS] + [whole((64, 4096))] * 4,
        [(shape((256, 4096), BF), whole((256, 4096)))],
        [place, *pieces],
    )[0]


def chosen_kernel(home, mine, other, block_out, tokens_grad):
    for flag, ref in ((1, mine), (0, other)):

        @pl.when(home[0] == flag)
        def take(ref=ref):
            block_out[...] = ref[:, :2048]
            tokens_grad[...] = ref[:, 2048:].astype(F32)


def chosen(home, mine, other):
    def block(cols):
        return pl.BlockSpec((64, cols), lambda i: (i, 0))

    return run(
        chosen_kernel,
        (4,),
        [SCALARS, block(4096), block(4096)],
        [(shape((256, 2048), BF), block(2048)), (shape((256, 2048), F32), block(2048))],
        [home, mine, other],
        limit=61,
    )


def scan_kernel(reverse, rate, parts, out):
    decay = jnp.exp(jnp.full((16, DV), -256.0 * rate[0], F32))
    state = jnp.zeros((16, DV), F32)
    for k in range(31, -1, -1) if reverse else range(32):
        out[k] = state.astype(BF)
        state = decay * state + parts[k].astype(F32)


def scan_spans(rate, parts, reverse):
    dims = (32, 16, DV)
    return run(
        functools.partial(scan_kernel, reverse),
        (1,),
        [SCALARS, whole(dims)],
        [(shape(dims, BF), whole(dims))],
        [rate, parts],
    )[0]


def pack_kernel(gains, *refs):
    out, start = refs[-1], 0
    for ref in refs[:-1]:
        out[:, start : start + ref.shape[1]] = ref[...]
        start += ref.shape[1]
        if start == 1536:
            start += 128
    wide = gains[...].astype(F32)
    same = lax.broadcasted_iota(jnp.int32, (64, 64), 0) == lax.broadcasted_iota(
        jnp.int32, (64, 64), 1
    )
    lane = lax.broadcasted_iota(jnp.int32, (64, 128), 1)
    total = jnp.zeros((64, 128), F32)
    for k in range(4):
        column = jnp.sum(jnp.where(same, wide[k : k + 1, :], 0.0), axis=1, keepdims=True)
        total = jnp.where(lane == k, column, total)
    out[:, 1536:1664] = total.astype(BF)


def pack(gains, *parts):
    cols = 128 + sum(p.shape[1] for p in parts)
    return run(
        pack_kernel,
        (1,),
        [whole((4, 64))] + [whole(p.shape) for p in parts],
        [(shape((64, cols), BF), whole((64, cols)))],
        [gains, *parts],
        limit=61,
    )[0]


def norm_kernel(tokens, hat, scale):
    made, spread = norm_parts(tokens[...].astype(F32))
    hat[...] = made
    scale[...] = spread


def norm_tokens(tokens):
    block = pl.BlockSpec((64, 2048), lambda i: (i, 0))
    return run(
        norm_kernel,
        (4,),
        [block],
        [
            (shape((256, 2048), F32), block, "hbm"),
            (shape((256, 1), F32), pl.BlockSpec((64, 1), lambda i: (i, 0)), "hbm"),
        ],
        [tokens],
        limit=61,
    )


def roll_kernel(place, values, out):
    for k in range(4):
        at = place[0] + k
        at = pl.multiple_of(jnp.where(at >= 4, at - 4, at) * 64, 64)
        out[k * 64 : k * 64 + 64, :] = values[pl.ds(at, 64), :]


def roll_rows(place, values):
    return run(
        roll_kernel,
        (1,),
        [SCALARS, whole((256, 2048))],
        [(shape((256, 2048), BF), whole((256, 2048)))],
        [place, values],
    )[0]


def collected(mine, others):
    total = mine[...]
    for other in others:
        total = total + other[...].astype(F32)
    return total


ROWS = pl.BlockSpec((64, 2048), lambda h: (0, 0))


def resid_kernel(tokens, mine, one, two, three, gains, resid, hat, scale, normed):
    total = tokens[...].astype(F32) + collected(mine, (one, two, three))
    resid[...] = total
    made, spread = norm_parts(total)
    hat[...] = made
    scale[...] = spread
    normed[...] = (made * gains[2:3] + gains[3:4]).astype(BF)


def resid_norm(tokens, mine, others, gains):
    return run(
        resid_kernel,
        (1,),
        [ROWS] * 5 + [whole((8, 2048))],
        [
            (shape((64, 2048), F32), ROWS),
            (shape((64, 2048), F32), ROWS),
            (shape((64, 1), F32), whole((64, 1))),
            (shape((64, 2048), BF), ROWS),
        ],
        [tokens, mine, *others, gains],
    )


def resid_back_kernel(
    out_grad, mine, one, two, three, gains, hat, scale, d_resid, d_attn, vectors
):
    total = collected(mine, (one, two, three))
    made = out_grad[...].astype(F32) + norm_back(total * gains[2:3], hat[...], scale[...])
    d_resid[...] = made
    d_attn[...] = made.astype(BF)
    vectors[0:1] = jnp.sum(total * hat[...], axis=0, keepdims=True)
    vectors[1:2] = jnp.sum(total, axis=0, keepdims=True)


def resid_back(out_grad, mine, others, gains, hat, scale):
    return run(
        resid_back_kernel,
        (1,),
        [ROWS] * 5 + [whole((8, 2048)), ROWS, whole((64, 1))],
        [
            (shape((64, 2048), F32), ROWS),
            (shape((64, 2048), BF), ROWS),
            (shape((2, 2048), F32), whole((2, 2048))),
        ],
        [out_grad, mine, *others, gains, hat, scale],
        limit=61,
    )


def rows_kernel(resid, f0, f1, f2, f3, d_resid, d0, d1, d2, d3, gains, hat, scale, out):
    out[:, :2048] = (resid[...] + collected(f0, (f1, f2, f3))).astype(BF)
    total = collected(d0, (d1, d2, d3))
    made = d_resid[...] + norm_back(total * gains[0:1], hat[...], scale[...])
    out[:, 2048:] = made.astype(BF)


def final_rows(resid, ffn, ffn_others, d_resid, mine, others, gains, hat, scale):
    return run(
        rows_kernel,
        (1,),
        [ROWS] * 10 + [whole((8, 2048)), ROWS, pl.BlockSpec((64, 1), lambda h: (0, 0))],
        [(shape((64, 4096), BF), whole((64, 4096)))],
        [resid, ffn, *ffn_others, d_resid, mine, *others, gains, hat, scale],
        limit=61,
    )[0]


def kv_kernel(
    rate,
    place,
    hat,
    gains_own,
    gains_other,
    key_own,
    key_other,
    value_own,
    value_other,
    cosine,
    sine,
    key,
    value,
    fresh,
    normed,
    gains,
    own,
    other,
):
    @pl.when(pl.program_id(0) == 0)
    def norm():
        mine = gains_own[...].astype(F32).T
        yours = gains_other[...].astype(F32).T
        for i in range(4):
            for ref, rows, side in ((own, mine, place[1]), (other, yours, 1 - place[1])):
                at = pl.multiple_of((2 * i + side) * 256, 256)
                rows = rows[:8, i * 256 : i * 256 + 256]
                gains[:, pl.ds(at, 256)] = rows
                out = (hat[:, pl.ds(at, 256)] * rows[0:1] + rows[1:2]).astype(BF)
                normed[:, pl.ds(at, 256)] = out
                ref[:, i * 256 : i * 256 + 256] = out

    qdec, kdec = decays(rate[pl.program_id(0)], place[0])
    raw = nn(own[...], key_own[...]) + nn(other[...], key_other[...])
    turn_into(key, raw, cosine[...], sine[...])
    made = (nn(own[...], value_own[...]) + nn(other[...], value_other[...])).astype(BF)
    value[...] = made
    fresh[...] = tn((kdec * key[...].astype(F32)).astype(BF), made).astype(BF)


def key_value(rate, place, hat, early, early_other, cosine, sine):
    gains = pl.BlockSpec((1024, 128), lambda h: (0, 12))
    return run(
        kv_kernel,
        (2,),
        [
            SCALARS,
            SCALARS,
            whole((256, 2048)),
            gains,
            gains,
            columns(1024, 256),
            columns(1024, 256),
            columns(1024, 512, 1),
            columns(1024, 512, 1),
            whole((256, 128)),
            whole((256, 128)),
        ],
        [
            (shape((256, 512), BF), columns(256, 256)),
            (shape((256, 1024), BF), columns(256, 512)),
            (shape((512, 512), BF), pl.BlockSpec((256, 512), lambda h: (h, 0))),
            (shape((256, 2048), BF), whole((256, 2048))),
            (shape((8, 2048), F32), whole((8, 2048))),
        ],
        [
            rate,
            place,
            hat,
            early,
            early_other,
            early,
            early_other,
            early,
            early_other,
            cosine,
            sine,
        ],
        [pltpu.VMEM((256, 1024), BF), pltpu.VMEM((256, 1024), BF)],
        limit=61,
    )


def query_kernel(
    rate, place, normed, w_query, w_gate, key, value, cosine, sine, query, gate, probs, inner
):
    raw = nn(normed[...], w_query[...])
    turn_into(query, raw, cosine[...], sine[...])
    gate[...] = nn(normed[...], w_gate[...])
    mask = span_mask(rate[pl.program_id(0)], place[0])
    made = (nt(query[...], key[...]) * mask).astype(BF)
    probs[0] = made
    inner[...] = nn(made, value[...])


def query_gate(rate, place, normed1, late, key, value, cosine, sine):
    return run(
        query_kernel,
        (2,),
        [
            SCALARS,
            SCALARS,
            whole((256, 2048)),
            columns(2048, 256, 12),
            columns(2048, 512),
            columns(256, 256),
            columns(256, 512),
            whole((256, 128)),
            whole((256, 128)),
        ],
        [
            (shape((256, 512), BF), columns(256, 256)),
            (shape((256, 1024), F32), columns(256, 512), "hbm"),
            (shape((2, 256, 256), BF), pl.BlockSpec((1, 256, 256), lambda h: (h, 0, 0))),
            (shape((256, 1024), F32), columns(256, 512)),
        ],
        [rate, place, normed1, late, late, key, value, cosine, sine],
        limit=61,
    )


def cut_rows(full, parts):
    parts[0][...] = full[:64]
    for k in range(1, 4):
        parts[k][...] = full[k * 64 : k * 64 + 64].astype(BF)


def row_parts(cols, index):
    spec = pl.BlockSpec((64, cols), index)
    return [(shape((64, 2048), F32 if k == 0 else BF), spec) for k in range(4)]


def retain_kernel(
    rate, place, query, state, inner, gate, w_out, hat, scale, mixed, mine, one, two, three, total
):
    h = pl.program_id(0)
    qdec, kdec = decays(rate[h], place[0])
    retained = inner[...] + qdec * nn(query[...], state[...])
    made, spread = norm_parts(retained)
    hat[...] = made
    scale[0] = spread
    wide = gate[...]
    made = (wide * jax.nn.sigmoid(wide) * made).astype(BF)
    mixed[...] = made
    partial = nt(made, w_out[...])

    @pl.when(h == 0)
    def first():
        total[...] = partial

    @pl.when(h == 1)
    def last():
        cut_rows(total[...] + partial, (mine, one, two, three))


def retain(rate, place, query, state, inner, gate, late):
    return run(
        retain_kernel,
        (2,),
        [
            SCALARS,
            SCALARS,
            columns(256, 256),
            pl.BlockSpec((256, 512), lambda h: (h, 0)),
            columns(256, 512),
            columns(256, 512),
            columns(2048, 512, 2),
        ],
        [
            (shape((256, 1024), F32), columns(256, 512), "hbm"),
            (shape((2, 256, 1), F32), pl.BlockSpec((1, 256, 1), lambda h: (h, 0, 0)), "hbm"),
            (shape((256, 1024), BF), columns(256, 512)),
            *row_parts(2048, lambda h: (0, 0)),
        ],
        [rate, place, query, state, inner, gate, late],
        [pltpu.VMEM((256, 2048), F32)],
        limit=61,
    )


def gathered(pieces, full):
    @pl.when(pl.program_id(0) == 0)
    def join():
        for k, piece in enumerate(pieces):
            full[k * 64 : k * 64 + 64, :] = piece[...]


def up_kernel(
    one, two, three, four, w_up, d_hidden, normed, hidden, d_up, mine, p1, p2, p3, total
):
    j = pl.program_id(0)
    gathered((one, two, three, four), normed)
    raw = nn(normed[...], w_up[...])
    root = 0.7978845608028654
    square = raw * raw
    tanh = jnp.tanh(root * raw * (1.0 + 0.044715 * square))
    half = 0.5 * (1.0 + tanh)
    hidden[...] = (raw * half).astype(BF)
    slope = half + 0.5 * raw * (1.0 - tanh * tanh) * root * (1.0 + 0.134145 * square)
    made = (slope * d_hidden[...]).astype(BF)
    d_up[...] = made
    partial = nt(made, w_up[...])

    @pl.when(j == 0)
    def first():
        total[...] = partial

    @pl.when(j == 1)
    def last():
        cut_rows(total[...] + partial, (mine, p1, p2, p3))


def up_back(pieces, late, d_hidden):
    return run(
        up_kernel,
        (2,),
        [ROWS] * 4 + [columns(2048, 512, 4), columns(256, 512)],
        [
            (shape((256, 2048), BF), whole((256, 2048))),
            (shape((256, 1024), BF), columns(256, 512)),
            (shape((256, 1024), BF), columns(256, 512)),
            *row_parts(2048, lambda h: (0, 0)),
        ],
        [*pieces, late, d_hidden],
        [pltpu.VMEM((256, 2048), F32)],
    )


def mixed_kernel(
    rate, place, one, two, three, four, w_out, gate, hat, scale, query, d_attn, d_gate, d_ret, outgoing
):
    gathered((one, two, three, four), d_attn)
    qdec, kdec = decays(rate[pl.program_id(0)], place[0])
    d_mixed = nn(d_attn[...], w_out[...])
    wide, normed = gate[...], hat[...]
    sig = jax.nn.sigmoid(wide)
    d_gate[...] = (d_mixed * normed * sig * (1.0 + wide * (1.0 - sig))).astype(BF)
    made = norm_back(d_mixed * wide * sig, normed, scale[0]).astype(BF)
    d_ret[...] = made
    outgoing[...] = tn((qdec * query[...].astype(F32)).astype(BF), made).astype(BF)


def mixed_back(rate, place, pieces, late, gate, hat, scale, query):
    return run(
        mixed_kernel,
        (2,),
        [
            SCALARS,
            SCALARS,
            *[ROWS] * 4,
            columns(2048, 512, 2),
            columns(256, 512),
            columns(256, 512),
            pl.BlockSpec((1, 256, 1), lambda h: (h, 0, 0)),
            columns(256, 256),
        ],
        [
            (shape((256, 2048), BF), whole((256, 2048))),
            (shape((256, 1024), BF), columns(256, 512)),
            (shape((256, 1024), BF), columns(256, 512)),
            (shape((512, 512), BF), pl.BlockSpec((256, 512), lambda h: (h, 0))),
        ],
        [rate, place, *pieces, late, gate, hat, scale, query],
        limit=61,
    )


def query_back_kernel(
    rate, place, d_ret, value, key, query, probs, state, cosine, sine, d_query, key_part, value_part
):
    h = pl.program_id(0)
    qdec, kdec = decays(rate[h], place[0])
    mask = span_mask(rate[h], place[0])
    d_scores = (nt(d_ret[...], value[...]) * mask).astype(BF)
    turned = nn(d_scores, key[...]) + qdec * nt(d_ret[...], state[...])
    turn_into(d_query, turned, cosine[...], -sine[...])
    key_part[...] = tn(d_scores, query[...])
    value_part[...] = tn(probs[0], d_ret[...])


def query_back(rate, place, d_ret, value, key, query, probs, state, cosine, sine):
    return run(
        query_back_kernel,
        (2,),
        [
            SCALARS,
            SCALARS,
            columns(256, 512),
            columns(256, 512),
            columns(256, 256),
            columns(256, 256),
            pl.BlockSpec((1, 256, 256), lambda h: (h, 0, 0)),
            pl.BlockSpec((256, 512), lambda h: (h, 0)),
            whole((256, 128)),
            whole((256, 128)),
        ],
        [
            (shape((256, 512), BF), columns(256, 256)),
            (shape((256, 512), F32), columns(256, 256)),
            (shape((256, 1024), F32), columns(256, 512)),
        ],
        [rate, place, d_ret, value, key, query, probs, state, cosine, sine],
        limit=61,
    )


def key_value_back_kernel(
    rate, place, key_part, value_part, key, value, later, cosine, sine, d_both
):
    for h in range(2):
        qdec, kdec = decays(rate[h], place[0])
        keys, values = slice(h * DK, h * DK + DK), slice(h * DV, h * DV + DV)
        carried = later[keys, :]
        d_key = key_part[:, keys] + kdec * nt(value[:, values], carried)
        turn_into(d_both, d_key, cosine[...], -sine[...], h * DK)
        d_value = value_part[:, values] + kdec * nn(key[:, keys], carried)
        d_both[:, 512 + h * DV : 512 + h * DV + DV] = d_value.astype(BF)


def key_value_back(rate, place, key_part, value_part, key, value, later, cosine, sine):
    return run(
        key_value_back_kernel,
        (1,),
        [
            SCALARS,
            SCALARS,
            whole((256, 512)),
            whole((256, 1024)),
            whole((256, 512)),
            whole((256, 1024)),
            whole((512, 512)),
            whole((256, 128)),
            whole((256, 128)),
        ],
        [(shape((256, 1536), BF), whole((256, 1536)))],
        [rate, place, key_part, value_part, key, value, later, cosine, sine],
        limit=61,
    )[0]


def normed_first_kernel(d_query, d_gate, w_query, w_gate, part):
    part[...] = nt(d_query[...], w_query[...]) + nt(d_gate[...], w_gate[...])


def normed_back_first(d_query, d_gate, late):
    return run(
        normed_first_kernel,
        (4,),
        [
            whole((256, 512)),
            whole((256, 1024)),
            pl.BlockSpec((512, 512), lambda i: (i, 6)),
            pl.BlockSpec((512, 1024), lambda i: (i, 0)),
        ],
        [(shape((256, 2048), F32), columns(256, 512))],
        [d_query, d_gate, late, late],
    )[0]


def normed_back_kernel(place, first, d_both, w_own, w_other, hat, mine, one, two, three, vectors):
    left = nt(d_both[...], w_own[:, :1536])
    right = nt(d_both[...], w_other[:, :1536])
    low = place[1] == 0
    total = first[...] + jnp.concatenate(
        [jnp.where(low, left, right), jnp.where(low, right, left)], axis=1
    )
    cut_rows(total, (mine, one, two, three))
    vectors[0:1] = jnp.sum(total * hat[...], axis=0, keepdims=True)
    vectors[1:2] = jnp.sum(total, axis=0, keepdims=True)


def normed_back(place, first, d_both, early, early_other, hat):
    weights = pl.BlockSpec((256, 1664), lambda i: (i, 0))
    return run(
        normed_back_kernel,
        (4,),
        [
            SCALARS,
            columns(256, 512),
            whole((256, 1536)),
            weights,
            weights,
            columns(256, 512),
        ],
        [
            *[(*part, "hbm") for part in row_parts(512, lambda i: (0, i))],
            (shape((2, 2048), F32), columns(2, 512)),
        ],
        [place, first, d_both, early, early_other, hat],
    )


def pair_kernel(left_one, right_one, left_two, right_two, out):
    w = pl.program_id(0)

    @pl.when(w == 0)
    def first():
        out[...] = tn(left_one[...], right_one[...]).astype(BF)

    @pl.when(w == 1)
    def second():
        out[...] = tn(left_two[...], right_two[...]).astype(BF)


def grad_pair(left_one, right_one, left_two, right_two):
    def left(w):
        return pl.BlockSpec((256, 512), lambda v, i: (0, jnp.where(v == w, i, 3 * (1 - w))))

    right = pl.BlockSpec((256, 1024), lambda v, i: (0, 0))
    return run(
        pair_kernel,
        (2, 4),
        [left(0), right, left(1), right],
        [(shape((2048, 2048), BF), pl.BlockSpec((512, 1024), lambda v, i: (i, v)))],
        [left_one, right_one, left_two, right_two],
        flops=4 * 256 * 2048 * 1024,
        moved=16 * 2048 * 1024,
    )[0]


def down_kernel(place, out_grad, w_own, w_other, d_hidden):
    total = jnp.zeros(d_hidden.shape, F32)
    for w, side in ((w_own, place[1]), (w_other, 1 - place[1])):
        for i in range(4):
            at = pl.multiple_of((2 * i + side) * 256, 256)
            total = total + nn(out_grad[:, pl.ds(at, 256)], w[i * 256 : i * 256 + 256, :])
    d_hidden[...] = total


def down_back(place, out_grad, w_own, w_other):
    return run(
        down_kernel,
        (2,),
        [SCALARS, whole((256, 2048)), columns(1024, 512), columns(1024, 512)],
        [(shape((256, 1024), F32), columns(256, 512))],
        [place, out_grad, w_own, w_other],
    )[0]


def ffn_kernel(place, hidden, w_own, w_other, mine, one, two, three):
    left, right = nt(hidden[...], w_own[...]), nt(hidden[...], w_other[...])
    low = place[1] == 0
    total = jnp.concatenate([jnp.where(low, left, right), jnp.where(low, right, left)], axis=1)
    cut_rows(total, (mine, one, two, three))


def ffn_parts(place, hidden, w_own, w_other):
    weights = pl.BlockSpec((256, 1024), lambda i: (i, 0))
    return run(
        ffn_kernel,
        (4,),
        [SCALARS, whole((256, 1024)), weights, weights],
        row_parts(512, lambda i: (0, i)),
        [place, hidden, w_own, w_other],
    )


def store_rows(ref, made, side, start):
    i = pl.program_id(0)
    for j in range(4):
        to = jnp.where(side == 0, i * 256 + j * 64, j * 256 + i * 64)
        ref[pl.ds(pl.multiple_of(to, 64), 64), start : start + made.shape[1]] = made[
            j * 64 : j * 64 + 64
        ]


def row_offsets(side):
    i = pl.program_id(0)
    for j in range(4):
        to = jnp.where(side == 0, i * 256 + j * 64, j * 256 + i * 64)
        yield slice(j * 64, j * 64 + 64), pl.ds(pl.multiple_of(to, 64), 64)


def other_kernel(place, left, *refs):
    rights, other = refs[:-1], refs[-1]
    side = 1 - place[1]
    rows = left[:, pl.ds(pl.multiple_of(side * 256, 256), 256)]
    start = 0
    for right in rights:
        store_rows(other, tn(rows, right[...]).astype(BF), side, start)
        start += right.shape[1]


def grad_other(place, left, rights):
    cols = sum(r.shape[1] for r in rights)
    return run(
        other_kernel,
        (4,),
        [SCALARS, columns(256, 512)] + [whole(r.shape) for r in rights],
        [(shape((1024, cols), BF), whole((1024, cols)))],
        [place, left, *rights],
        limit=61,
    )[0]


def own_kernel(sizes, place, *refs):
    out, refs, start = refs[-1], list(refs[:-1]), 0
    side = place[1]
    for size in sizes:
        left, rights, given = refs[0], refs[1 : 1 + size], refs[1 + size]
        refs, local = refs[2 + size :], 0
        rows = left[:, pl.ds(pl.multiple_of(side * 256, 256), 256)]
        for right in rights:
            made, cols = tn(rows, right[...]), right.shape[1]
            for take, to in row_offsets(side):
                total = made[take] + given[to, local : local + cols].astype(F32)
                out[to, start : start + cols] = total.astype(BF)
            start, local = start + cols, local + cols


def grad_own(place, groups, more=0):
    specs, operands, sizes, cols = [SCALARS], [place], [], more
    for left, rights, given in groups:
        specs += [columns(256, 512)] + [whole(r.shape) for r in rights] + [whole(given.shape)]
        operands += [left, *rights, given]
        sizes.append(len(rights))
        cols += given.shape[1]
    return run(
        functools.partial(own_kernel, tuple(sizes)),
        (4,),
        specs,
        [(shape((1024, cols), BF), whole((1024, cols)), "hbm")],
        operands,
        limit=61,
    )[0]


def vector_kernel(place, kept, one, two, three, four, out):
    wide = jnp.zeros((120, 256), F32)
    for i in range(4):
        at = pl.ds(pl.multiple_of((2 * i + place[1]) * 256, 256), 256)
        rows = one[:, at] + two[:, at] + three[:, at] + four[:, at]
        made = jnp.concatenate([rows, wide], axis=0).T.astype(BF)
        for j in range(4):
            to = jnp.where(place[1] == 0, i * 256 + j * 64, j * 256 + i * 64)
            out[pl.ds(pl.multiple_of(to, 64), 64), :] = made[j * 64 : j * 64 + 64]


def with_vectors(place, wide, *vectors):
    last = wide.shape[1] // 128 - 1
    return pl.pallas_call(
        vector_kernel,
        grid=(1,),
        in_specs=[SCALARS, pl.BlockSpec(memory_space=pl.ANY)] + [whole((8, 2048))] * 4,
        out_specs=pl.BlockSpec((1024, 128), lambda i: (0, last)),
        out_shape=pltpu.HBM(wide.shape, BF),
        input_output_aliases={1: 0},
        compiler_params=pltpu.CompilerParams(vmem_limit_bytes=48 * 1024 * 1024),
        cost_estimate=pl.CostEstimate(flops=1, bytes_accessed=1, transcendentals=0),
    )(place, wide, *vectors)


def four_sum(ref):
    total = ref[0].astype(F32)
    for k in range(1, 4):
        total = total + ref[k].astype(F32)
    return total.astype(BF)


def early_kernel(parts, out):
    out[:, out.shape[1] - parts.shape[2] :] = four_sum(parts)


def early_sum(parts, cols):
    return run(
        early_kernel,
        (4,),
        [pl.BlockSpec((4, 64, parts.shape[2]), lambda i: (0, i, 0))],
        [(shape((256, cols), BF), pl.BlockSpec((64, cols), lambda i: (i, 0)), "hbm")],
        [parts],
        limit=61,
    )[0]


def late_kernel(kept, parts, out):
    out[...] = four_sum(parts)


def late_sum(wide, parts):
    cols = parts.shape[2]
    return pl.pallas_call(
        late_kernel,
        grid=(4,),
        in_specs=[
            pl.BlockSpec(memory_space=pl.ANY),
            pl.BlockSpec((4, 64, cols), lambda i: (0, i, 0)),
        ],
        out_specs=pl.BlockSpec((64, cols), lambda i: (i, 0)),
        out_shape=pltpu.HBM(wide.shape, BF),
        input_output_aliases={0: 0},
        compiler_params=pltpu.CompilerParams(vmem_limit_bytes=48 * 1024 * 1024),
        cost_estimate=pl.CostEstimate(flops=1, bytes_accessed=1, transcendentals=0),
    )(wide, parts)


def last_kernel(parts, out):
    total = parts[0].astype(F32)
    for k in range(1, 4):
        total = total + parts[k].astype(F32)
    out[...] = total.astype(BF)


def last_sum(parts):
    dims = parts.shape[1:]
    return run(
        last_kernel,
        (1,),
        [whole(parts.shape)],
        [(shape(dims, BF), whole(dims))],
        [parts],
    )[0]


def widen_kernel(values, *outs):
    start = 0
    for out in outs:
        if out.shape[0] == 64:
            out[...] = values[:, start : start + out.shape[1]].astype(F32)
            start += out.shape[1]
        else:
            out[...] = values[:, start : start + 128].astype(F32).T[:8]
            start += 128


def widen(values, widths):
    dims = [(64, n) if n else (8, 64) for n in widths]
    outs = [(shape(d, F32), whole(d)) for d in dims]
    return run(widen_kernel, (1,), [whole(values.shape)], outs, [values])


def body(
    tokens,
    norm1_gain,
    norm1_bias,
    w_query,
    w_key,
    w_value,
    w_gate,
    w_out,
    norm2_gain,
    norm2_bias,
    w_up,
    w_down,
    decay_rate,
    out_grad,
):
    x, y, c = lax.axis_index("x"), lax.axis_index("y"), lax.axis_index("c")
    zl, zh = lax.axis_index("zl"), lax.axis_index("zh")
    z = zh * 2 + zl
    home = (zh == c).astype(jnp.int32).reshape(1)
    span = x * 8 + c * 4 + y
    place = jnp.stack([z, c, x, y]).astype(jnp.int32)

    gains = jnp.stack([norm1_gain, norm1_bias, norm2_gain, norm2_bias])
    shards = swap_roles(
        pack(gains, w_key, w_value, w_gate, w_out.T, w_up, w_query)
    )
    first, second = shards[:, :1664], shards[:, 1664:]
    rate = swap_roles(decay_rate)
    tokens, kept = lax.optimization_barrier((tokens, shards))
    tokens = swap_roles(tokens)
    third, kept = lax.optimization_barrier((w_down.T, tokens))
    third = jnp.broadcast_to(swap_roles(third)[None], (16, 64, 1024))
    out_grad, kept = lax.optimization_barrier((out_grad, tokens))
    out_grad = swap_roles(out_grad)

    cols = first.shape[1]
    early = lax.all_to_all(
        jnp.broadcast_to(first[None], (16, 64, cols)), ("x", "y"), 0, 0, tiled=True
    ).reshape(1024, cols)
    late = lax.all_gather(second, SPANS, axis=0, tiled=True)

    tokens = roll_rows(place, tokens)
    hat1, scale1 = norm_tokens(tokens)
    out_grad = roll_rows(place, out_grad)
    index = ((jnp.arange(256) + z * 64) % 256).astype(F32)
    half = DK // 2
    position = (span * 256).astype(F32) + index
    freq = 10000.0 ** (-jnp.arange(half).astype(F32) / half)
    angle = position[:, None] * freq[None, :]
    cosine, sine = jnp.cos(angle), jnp.sin(angle)
    early, tokens, hat1, out_grad, third, cosine, sine, rate = lax.optimization_barrier(
        (early, tokens, hat1, out_grad, third, cosine, sine, rate)
    )

    early_other = core_swap(early)
    key, value, fresh, normed1, gains = key_value(
        rate, place, hat1, early, early_other, cosine, sine
    )
    scan_rate = jnp.where(x < 2, rate[0], rate[1]).reshape(1)
    carried = scan_spans(scan_rate, scan_parts(fresh), False)
    state = scan_back(carried)
    query, gate, probs, inner = query_gate(
        rate, place, normed1, late, key, value, cosine, sine
    )
    third, state, query = lax.optimization_barrier((third, state, query))
    down = lax.all_to_all(third, ("x", "y"), 0, 0, tiled=True).reshape(1024, 1024)
    hat, scale, mixed, mine, *parts = retain(rate, place, query, state, inner, gate, late)
    parts = z_collect(parts)
    resid, hat2, scale2, normed2 = resid_norm(tokens[:64], mine, parts, gains)
    down, kept = lax.optimization_barrier((down, normed2))
    down_other = core_swap(down)
    d_hidden = down_back(place, out_grad, down, down_other)
    normed2, hidden, d_up, mine, *parts = up_back(z_gather(normed2), late, d_hidden)
    parts = z_collect(parts)
    grad_wide = grad_pair(normed2, d_up, out_grad, hidden)
    mine, parts, grad_wide = lax.optimization_barrier((mine, parts, grad_wide))
    d_resid, d_attn, vectors2 = resid_back(out_grad, mine, parts, gains, hat2, scale2)
    grad_wide = lax.psum_scatter(grad_wide, SPANS, scatter_dimension=0, tiled=True)
    hidden, d_attn = lax.optimization_barrier((hidden, d_attn))
    ffn, *ffn_others = ffn_parts(place, hidden, down, down_other)
    pieces = z_gather(d_attn)
    pieces, ffn, ffn_others = lax.optimization_barrier((pieces, ffn, ffn_others))
    d_attn, d_gate, d_ret, outgoing = mixed_back(
        rate, place, pieces, late, gate, hat, scale, query
    )
    ffn_others = z_collect(ffn_others)
    parts = scan_parts(outgoing)

    d_query, key_part, value_part = query_back(
        rate, place, d_ret, value, key, query, probs, state, cosine, sine
    )
    out_other = grad_other(place, d_attn, [mixed])
    gate_other = grad_other(place, normed1, [d_gate, d_query])
    gate_other, out_other, ffn_others = lax.optimization_barrier(
        (gate_other, out_other, ffn_others)
    )
    parts, gate_other, out_other = lax.optimization_barrier((parts, gate_other, out_other))
    later = scan_back(scan_spans(scan_rate, parts, True))
    early_part = grad_own(
        place,
        [
            (normed1, [d_gate, d_query], core_swap(gate_other)),
            (d_attn, [mixed], core_swap(out_other)),
        ],
    )
    d_query, parts = lax.optimization_barrier((d_query, parts))
    d_first = normed_back_first(d_query, d_gate, late)
    early_part, later, d_first = lax.optimization_barrier((early_part, later, d_first))
    early_part = exchange(early_part, FIRST_WAY)

    d_both = key_value_back(
        rate, place, key_part, value_part, key, value, later, cosine, sine
    )
    late_other = grad_other(place, normed1, [d_both])
    d_both, late_other = lax.optimization_barrier((d_both, late_other))
    late_other = core_swap(late_other)
    mine, *parts, vectors = normed_back(place, d_first, d_both, early, early_other, hat1)
    vectors = jnp.concatenate([vectors, vectors2, jnp.zeros((4, 2048), F32)])
    vectors = vectors + core_swap(vectors)
    shifted = [z_shift(vectors, shift) for shift in (1, 3, 2)]
    parts = z_collect(parts)
    late_part = grad_own(place, [(normed1, [d_both], late_other)], 128)
    late_part, shifted = lax.optimization_barrier((late_part, shifted))
    late_part = with_vectors(place, late_part, vectors, *shifted)
    late_part, early_part = lax.optimization_barrier((late_part, early_part))
    late_part = exchange(late_part, FIRST_WAY)

    joined = early_sum(early_part.reshape(4, 256, -1), 4224)
    parts, grad_wide, joined = lax.optimization_barrier((parts, grad_wide, joined))
    rows = final_rows(resid, ffn, ffn_others, d_resid, mine, parts, gains, hat1, scale1)
    kept, late_part = lax.optimization_barrier((rows, late_part))
    block_out, tokens_grad = z_gather_home(rows, place, home)

    total = exchange(late_sum(joined, late_part.reshape(4, 256, -1)), SECOND_WAY)
    total, grad_wide = lax.optimization_barrier((total, swap_roles(grad_wide)))
    total = swap_roles(last_sum(total.reshape(4, 64, -1)))
    total, block_out, tokens_grad = lax.optimization_barrier((total, block_out, tokens_grad))
    grad_key, grad_value, vectors, grad_gate, grad_query, grad_out = widen(
        total, [512, 1024, 0, 1024, 512, 1024]
    )
    grad_up, grad_down = widen(grad_wide, [1024, 1024])
    return (
        block_out,
        tokens_grad,
        vectors[0],
        vectors[1],
        grad_query,
        grad_key,
        grad_value,
        grad_gate,
        grad_out.T,
        vectors[2],
        vectors[3],
        grad_up,
        grad_down.T,
    )


def solution(mesh):
    fine = Mesh(mesh.devices.reshape(2, 2, 4, 2, 4), AXES)
    seq, tp = ("x", "zh", "y"), ("zl", "c")
    rows, wide, tall, vector = P(seq, None), P(seq, tp), P(tp, seq), P(seq)
    in_specs = (
        rows,
        vector,
        vector,
        wide,
        wide,
        wide,
        wide,
        tall,
        vector,
        vector,
        wide,
        tall,
        P(tp),
        rows,
    )
    out_specs = (
        rows,
        rows,
        vector,
        vector,
        wide,
        wide,
        wide,
        wide,
        tall,
        vector,
        vector,
        wide,
        tall,
    )
    return jax.shard_map(body, mesh=fine, in_specs=in_specs, out_specs=out_specs, check_vma=False)
```
